32 devices in a mesh: blk: 4 (over z), batch: 2 (over y), vocab: 4 (over x, core).
Axes of the slice: x: 2, y: 2, z: 4, core: 2. Of those that a mesh axis runs over, the one named last changes fastest.
Arguments:
- hidden: bfloat16 [8, 1024, 768], P(('batch', 'vocab'), 'blk'), may hold values from -6 to 6
- lengths: int32 [8], P(('batch', 'vocab')), may hold values from 64 to 1024, as said below
- student_first_gain: bfloat16 [768], P(('blk', 'batch', 'vocab')), may hold values from 0.5 to 1.5
- student_first_shift: bfloat16 [768], P(('blk', 'batch', 'vocab')), may hold values from -1.5 to 1.5
- student_attend_weight: bfloat16 [768, 2304], P(('blk', 'batch', 'vocab')), may hold values from -0.21875 to 0.21875
- student_attend_bias: bfloat16 [1536], P(('blk', 'batch', 'vocab')), may hold values from -1.5 to 1.5
- student_output_weight: bfloat16 [768, 768], P(('blk', 'batch', 'vocab')), may hold values from -0.625 to 0.625
- student_output_bias: bfloat16 [768], P(('blk', 'batch', 'vocab')), may hold values from -1.5 to 1.5
- student_second_gain: bfloat16 [768], P(('blk', 'batch', 'vocab')), may hold values from 0.5 to 1.5
- student_second_shift: bfloat16 [768], P(('blk', 'batch', 'vocab')), may hold values from -1.5 to 1.5
- student_expand_weight: bfloat16 [768, 3072], P(('blk', 'batch', 'vocab')), may hold values from -0.21875 to 0.21875
- student_expand_bias: bfloat16 [3072], P(('blk', 'batch', 'vocab')), may hold values from -1.5 to 1.5
- student_reduce_weight: bfloat16 [3072, 768], P(('blk', 'batch', 'vocab')), may hold values from -0.109375 to 0.109375
- student_reduce_bias: bfloat16 [768], P(('blk', 'batch', 'vocab')), may hold values from -1.5 to 1.5
- teacher_first_gain: bfloat16 [768], P(('blk', 'batch', 'vocab')), may hold values from 0.5 to 1.5
- teacher_first_shift: bfloat16 [768], P(('blk', 'batch', 'vocab')), may hold values from -1.5 to 1.5
- teacher_attend_weight: bfloat16 [768, 2304], P(('blk', 'batch', 'vocab')), may hold values from -0.21875 to 0.21875
- teacher_attend_bias: bfloat16 [1536], P(('blk', 'batch', 'vocab')), may hold values from -1.5 to 1.5
- teacher_output_weight: bfloat16 [768, 768], P(('blk', 'batch', 'vocab')), may hold values from -0.625 to 0.625
- teacher_output_bias: bfloat16 [768], P(('blk', 'batch', 'vocab')), may hold values from -1.5 to 1.5
- teacher_second_gain: bfloat16 [768], P(('blk', 'batch', 'vocab')), may hold values from 0.5 to 1.5
- teacher_second_shift: bfloat16 [768], P(('blk', 'batch', 'vocab')), may hold values from -1.5 to 1.5
- teacher_expand_weight: bfloat16 [768, 3072], P(('blk', 'batch', 'vocab')), may hold values from -0.21875 to 0.21875
- teacher_expand_bias: bfloat16 [3072], P(('blk', 'batch', 'vocab')), may hold values from -1.5 to 1.5
- teacher_reduce_weight: bfloat16 [3072, 768], P(('blk', 'batch', 'vocab')), may hold values from -0.109375 to 0.109375
- teacher_reduce_bias: bfloat16 [768], P(('blk', 'batch', 'vocab')), may hold values from -1.5 to 1.5
- final_gain: bfloat16 [768], replicated, may hold values from 0.5 to 1.5
- final_shift: bfloat16 [768], replicated, may hold values from -1.5 to 1.5
- embedding: bfloat16 [50304, 768], P('vocab'), may hold values from -0.59765625 to 0.59765625
Outputs:
- grad_student_first_gain: float32 [768], P(('blk', 'batch', 'vocab'))
- grad_student_first_shift: float32 [768], P(('blk', 'batch', 'vocab'))
- grad_student_attend_weight: float32 [768, 2304], P(('blk', 'batch', 'vocab'))
- grad_student_attend_bias: float32 [1536], P(('blk', 'batch', 'vocab'))
- grad_student_output_weight: float32 [768, 768], P(('blk', 'batch', 'vocab'))
- grad_student_output_bias: float32 [768], P(('blk', 'batch', 'vocab'))
- grad_student_second_gain: float32 [768], P(('blk', 'batch', 'vocab'))
- grad_student_second_shift: float32 [768], P(('blk', 'batch', 'vocab'))
- grad_student_expand_weight: float32 [768, 3072], P(('blk', 'batch', 'vocab'))
- grad_student_expand_bias: float32 [3072], P(('blk', 'batch', 'vocab'))
- grad_student_reduce_weight: float32 [3072, 768], P(('blk', 'batch', 'vocab'))
- grad_student_reduce_bias: float32 [768], P(('blk', 'batch', 'vocab'))
- grad_teacher_first_gain: float32 [768], P(('blk', 'batch', 'vocab'))
- grad_teacher_first_shift: float32 [768], P(('blk', 'batch', 'vocab'))
- grad_teacher_attend_weight: float32 [768, 2304], P(('blk', 'batch', 'vocab'))
- grad_teacher_attend_bias: float32 [1536], P(('blk', 'batch', 'vocab'))
- grad_teacher_output_weight: float32 [768, 768], P(('blk', 'batch', 'vocab'))
- grad_teacher_output_bias: float32 [768], P(('blk', 'batch', 'vocab'))
- grad_teacher_second_gain: float32 [768], P(('blk', 'batch', 'vocab'))
- grad_teacher_second_shift: float32 [768], P(('blk', 'batch', 'vocab'))
- grad_teacher_expand_weight: float32 [768, 3072], P(('blk', 'batch', 'vocab'))
- grad_teacher_expand_bias: float32 [3072], P(('blk', 'batch', 'vocab'))
- grad_teacher_reduce_weight: float32 [3072, 768], P(('blk', 'batch', 'vocab'))
- grad_teacher_reduce_bias: float32 [768], P(('blk', 'batch', 'vocab'))
- input_grad: float32 [8, 1024, 768], P(('batch', 'vocab'), 'blk')
- kl: float32 [8, 1024], P(('batch', 'vocab'), 'blk')
The draws below stay inside these ranges and needn't reach their ends.
Inputs may be any that keep to these rules, and one draw needn't show every extreme that they name: `lengths`: in each run of 4 consecutive sequences counted from the first, at least one sequence has length 1024.
All inputs are finite; a program needn't handle non-finite values.
Results may differ from the reference program's by a relative error of at most 0.025.
Values may be sent and summed in bfloat16 or wider, within the bound.
No kernel may reach another device: no remote copies, remote signals or barrier semaphores. Data moves between devices by JAX's collectives and lax.ppermute only.
A program may use at most 256 MiB of HBM per device.

```python
import math
import jax
import jax.numpy as jnp
from jax import lax

D = 768
HEADS = 12
HEAD = 64
FF = 3072
VOCAB = 50304
VOCAB_REAL = 50257
LEN = 1024
GROUP_SEQS = 4
SEQS = 8


def draw_lengths(key, part):
    key = jax.random.fold_in(key, 7)
    keys_split = jax.random.split(key, 4)
    groups = SEQS // GROUP_SEQS
    chosen = jax.random.randint(keys_split[0], (groups, 1), 0, GROUP_SEQS)
    kinds = jax.random.randint(keys_split[1], (groups, GROUP_SEQS), 0, 4)
    short_lengths = jax.random.randint(keys_split[2], (groups, GROUP_SEQS), LEN // 16, LEN // 4 + 1)
    long_lengths = jax.random.randint(keys_split[3], (groups, GROUP_SEQS), 3 * LEN // 4, LEN + 1)
    drawn = jnp.where(kinds == 0, short_lengths, long_lengths)
    slots = jnp.arange(GROUP_SEQS)[None, :]
    drawn = jnp.where(slots == chosen, LEN, drawn)
    return drawn.reshape(SEQS).astype(jnp.int32)


def block_levels(own_key, extent, cuts, smallest, high):
    gain = 1.0
    for position, parts in cuts:
        draws = jax.random.uniform(jax.random.fold_in(jax.random.fold_in(own_key, 6), position), (parts,), jnp.float32, smallest / len(cuts), high / len(cuts))
        gain = gain * jnp.repeat(jnp.exp(draws), extent[position] // parts).reshape((-1,) + (1,) * (len(extent) - 1 - position))
    return gain


def scatter_about(own_key, shape, scale, reach, shards=(), kind=jnp.bfloat16):
    result = jax.random.normal(own_key, shape, jnp.float32) * scale
    if len(shards) > 0:
        result = block_levels(own_key, shape, shards, -0.22, 0.18) * result
    return jnp.clip(result, min=-reach, max=reach).astype(kind)


def setup_inputs(seed: int = 0) -> dict:
    splits = jax.random.split(jax.random.key(seed), 30)
    return {
        "hidden": scatter_about(splits[0], (SEQS, LEN, D), 1.0, 6.0, ((0, 8), (1, 4))),
        "lengths": draw_lengths(jax.random.fold_in(splits[29], 71), 0),
        "student_first_gain": jnp.clip(1.0 + 0.1 * jax.random.normal(splits[2], (D,), jnp.float32), 0.5, 1.5).astype(jnp.bfloat16),
        "student_first_shift": scatter_about(splits[3], (D,), 0.3, 1.5, ((0, 32),)),
        "student_attend_weight": scatter_about(splits[4], (D, 3 * D), D ** -0.5, 0.21875, ((0, 32),)),
        "student_attend_bias": scatter_about(splits[5], (2 * D,), 0.3, 1.5, ((0, 32),)),
        "student_output_weight": scatter_about(splits[6], (D, D), (D // 8) ** -0.5, 0.625, ((0, 32),)),
        "student_output_bias": scatter_about(splits[7], (D,), 0.3, 1.5, ((0, 32),)),
        "student_second_gain": jnp.clip(1.0 + 0.1 * jax.random.normal(splits[8], (D,), jnp.float32), 0.5, 1.5).astype(jnp.bfloat16),
        "student_second_shift": scatter_about(splits[9], (D,), 0.3, 1.5, ((0, 32),)),
        "student_expand_weight": scatter_about(splits[10], (D, FF), D ** -0.5, 0.21875, ((0, 32),)),
        "student_expand_bias": scatter_about(splits[11], (FF,), 0.3, 1.5, ((0, 32),)),
        "student_reduce_weight": scatter_about(splits[12], (FF, D), FF ** -0.5, 0.109375, ((0, 32),)),
        "student_reduce_bias": scatter_about(splits[13], (D,), 0.3, 1.5, ((0, 32),)),
        "teacher_first_gain": jnp.clip(1.0 + 0.1 * jax.random.normal(splits[14], (D,), jnp.float32), 0.5, 1.5).astype(jnp.bfloat16),
        "teacher_first_shift": scatter_about(splits[15], (D,), 0.3, 1.5, ((0, 32),)),
        "teacher_attend_weight": scatter_about(splits[16], (D, 3 * D), D ** -0.5, 0.21875, ((0, 32),)),
        "teacher_attend_bias": scatter_about(splits[17], (2 * D,), 0.3, 1.5, ((0, 32),)),
        "teacher_output_weight": scatter_about(splits[18], (D, D), (D // 8) ** -0.5, 0.625, ((0, 32),)),
        "teacher_output_bias": scatter_about(splits[19], (D,), 0.3, 1.5, ((0, 32),)),
        "teacher_second_gain": jnp.clip(1.0 + 0.1 * jax.random.normal(splits[20], (D,), jnp.float32), 0.5, 1.5).astype(jnp.bfloat16),
        "teacher_second_shift": scatter_about(splits[21], (D,), 0.3, 1.5, ((0, 32),)),
        "teacher_expand_weight": scatter_about(splits[22], (D, FF), D ** -0.5, 0.21875, ((0, 32),)),
        "teacher_expand_bias": scatter_about(splits[23], (FF,), 0.3, 1.5, ((0, 32),)),
        "teacher_reduce_weight": scatter_about(splits[24], (FF, D), FF ** -0.5, 0.109375, ((0, 32),)),
        "teacher_reduce_bias": scatter_about(splits[25], (D,), 0.3, 1.5, ((0, 32),)),
        "final_gain": jnp.clip(1.0 + 0.1 * jax.random.normal(splits[26], (D,), jnp.float32), 0.5, 1.5).astype(jnp.bfloat16),
        "final_shift": scatter_about(splits[27], (D,), 0.3, 1.5),
        "embedding": scatter_about(splits[28], (VOCAB, D), 0.1, 0.59765625, ((0, 4),)),
    }


@jax.custom_vjp
def low(v):
    return lax.optimization_barrier(v.astype(jnp.bfloat16)).astype(jnp.float32)

@jax.custom_vjp
def low_back(v):
    return v

def low_keep(v):
    return (low(v), None)

def low_pass(kept, grad):
    return (grad,)

def back_keep(v):
    return (v, None)

def back_low(kept, grad):
    return (low(grad),)
low.defvjp(low_keep, low_pass)
low_back.defvjp(back_keep, back_low)
highest_precision = lax.Precision.HIGHEST

def product(left_side, right_side):
    return jnp.dot(left_side, right_side, precision=highest_precision)

def layer_norm(inputs, gain_row, shift_row):
    centred = inputs - lax.optimization_barrier(jnp.mean(inputs, axis=-1, keepdims=True))
    spread = lax.optimization_barrier(jnp.mean(centred * centred, axis=-1, keepdims=True))
    return centred * lax.rsqrt(spread + 1e-05) * gain_row + shift_row

def block_forward(seq_rows, params, key_mask):
    first_gain, first_shift, attend_weight, attend_bias, output_weight, output_bias, second_gain, second_shift, expand_weight, expand_bias, reduce_weight, reduce_bias = params
    normed_one = low(layer_norm(seq_rows, first_gain, first_shift))
    joined = product(normed_one, attend_weight)
    query_rows = low_back(low(joined[:, :D] + attend_bias[:D])).reshape(LEN, HEADS, HEAD)
    key_rows = low_back(low(joined[:, D:2 * D])).reshape(LEN, HEADS, HEAD)
    value_rows = low_back(low(joined[:, 2 * D:] + attend_bias[D:])).reshape(LEN, HEADS, HEAD)
    scores = low_back(jnp.einsum('qhd,khd->hqk', query_rows, key_rows, precision=highest_precision) * HEAD ** (-0.5))
    scores = jnp.where(key_mask[None], scores, -1e+30)
    attn_weights = low(jax.nn.softmax(scores, axis=-1))
    mixed_rows = jnp.einsum('hqk,khd->qhd', attn_weights, value_rows, precision=highest_precision).reshape(LEN, D)
    mixed_rows = low_back(low(mixed_rows))
    middle = seq_rows + low_back(product(mixed_rows, output_weight) + output_bias)
    normed_two = low(layer_norm(middle, second_gain, second_shift))
    inner_rows = low_back(product(normed_two, expand_weight) + expand_bias)
    active = low(jax.nn.gelu(inner_rows, approximate=True))
    return middle + low_back(product(active, reduce_weight) + reduce_bias)

def divergence(rows_student, rows_teacher, embed_rows, column_valid):
    logit_student = low_back(product(rows_student, embed_rows.T))
    logit_teacher = low_back(product(rows_teacher, embed_rows.T))
    scaled_student = jnp.where(column_valid, logit_student * 0.5, -1e+30)
    scaled_teacher = jnp.where(column_valid, logit_teacher * 0.5, -1e+30)
    log_student = jax.nn.log_softmax(scaled_student, axis=-1)
    log_teacher = jax.nn.log_softmax(scaled_teacher, axis=-1)
    summand = jnp.where(column_valid, jnp.exp(log_teacher) * (log_teacher - log_student), 0.0)
    return lax.optimization_barrier(jnp.sum(summand, axis=-1))

def reference(hidden, lengths, student_first_gain, student_first_shift, student_attend_weight, student_attend_bias, student_output_weight, student_output_bias, student_second_gain, student_second_shift, student_expand_weight, student_expand_bias, student_reduce_weight, student_reduce_bias, teacher_first_gain, teacher_first_shift, teacher_attend_weight, teacher_attend_bias, teacher_output_weight, teacher_output_bias, teacher_second_gain, teacher_second_shift, teacher_expand_weight, teacher_expand_bias, teacher_reduce_weight, teacher_reduce_bias, final_gain, final_shift, embedding):
    params_student = tuple((array_in.astype(jnp.float32) for array_in in (student_first_gain, student_first_shift, student_attend_weight, student_attend_bias, student_output_weight, student_output_bias, student_second_gain, student_second_shift, student_expand_weight, student_expand_bias, student_reduce_weight, student_reduce_bias)))
    params_teacher = tuple((array_in.astype(jnp.float32) for array_in in (teacher_first_gain, teacher_first_shift, teacher_attend_weight, teacher_attend_bias, teacher_output_weight, teacher_output_bias, teacher_second_gain, teacher_second_shift, teacher_expand_weight, teacher_expand_bias, teacher_reduce_weight, teacher_reduce_bias)))
    embed_rows = embedding.astype(jnp.float32)
    gain_final = final_gain.astype(jnp.float32)
    shift_final = final_shift.astype(jnp.float32)
    positions = jnp.arange(LEN, dtype=jnp.int32)
    column_valid = (jnp.arange(VOCAB, dtype=jnp.int32) < VOCAB_REAL)[None, :]
    row_block = math.gcd(LEN, 256)

    def sequence_loss(seq_rows, seq_length, student, teacher):
        key_mask = (positions[None, :] <= positions[:, None]) & (positions[None, :] < seq_length)
        out_student = block_forward(seq_rows, student, key_mask)
        out_teacher = block_forward(seq_rows, teacher, key_mask)
        rows_student = low(layer_norm(out_student, gain_final, shift_final)).reshape(LEN // row_block, row_block, D)
        rows_teacher = low(layer_norm(out_teacher, gain_final, shift_final)).reshape(LEN // row_block, row_block, D)
        row_piece = jax.checkpoint(lambda row_pair: divergence(row_pair[0], row_pair[1], embed_rows, column_valid))
        per_row = lax.map(row_piece, (rows_student, rows_teacher)).reshape(LEN)
        return 4.0 * per_row * (positions < seq_length).astype(jnp.float32)

    def forward(all_rows, student, teacher):
        seq_step = jax.checkpoint(lambda seq_rows, seq_length: sequence_loss(seq_rows, seq_length, student, teacher))

        def scan_step(carried, seq_pair):
            return (carried, seq_step(seq_pair[0], seq_pair[1]))
        _, losses = lax.scan(scan_step, None, (all_rows, lengths))
        return losses
    losses, pull = jax.vjp(forward, hidden.astype(jnp.float32), params_student, params_teacher)
    grad_rows, grad_student, grad_teacher = pull(jnp.ones_like(losses))
    return (grad_student[0], grad_student[1], grad_student[2], grad_student[3], grad_student[4], grad_student[5], grad_student[6], grad_student[7], grad_student[8], grad_student[9], grad_student[10], grad_student[11], grad_teacher[0], grad_teacher[1], grad_teacher[2], grad_teacher[3], grad_teacher[4], grad_teacher[5], grad_teacher[6], grad_teacher[7], grad_teacher[8], grad_teacher[9], grad_teacher[10], grad_teacher[11], grad_rows, losses)
```

```python
import functools
import math

import jax
import jax.numpy as jnp
from jax import lax
from jax.experimental import pallas as pl
from jax.experimental.pallas import tpu as pltpu
from jax.sharding import PartitionSpec as P

HEADS = 12
HEAD = 64
VOCAB_REAL = 50257
BLK, BATCH, VOCAB = "blk", "batch", "vocab"
EVERY = (BLK, BATCH, VOCAB)


def for_sending(shard):
    return jax.tree.map(lambda a: a.astype(jnp.bfloat16) if a.dtype == jnp.float32 else a, shard)


def layer_norm(inputs, gain_row, shift_row):
    centred = inputs - jnp.mean(inputs, axis=-1, keepdims=True)
    spread = jnp.mean(centred * centred, axis=-1, keepdims=True)
    return centred * lax.rsqrt(spread + 1e-05) * gain_row + shift_row


def gelu_tanh(inputs):
    return jax.nn.gelu(inputs, approximate=True)


def matmul_plain(left_side, right_side):
    return jnp.dot(left_side, right_side, preferred_element_type=jnp.float32)


def matmul_right_t(left_side, right_side):
    return lax.dot_general(
        left_side, right_side, (((1,), (1,)), ((), ())), preferred_element_type=jnp.float32
    )


def matmul_left_t(left_side, right_side):
    return lax.dot_general(
        left_side, right_side, (((0,), (0,)), ((), ())), preferred_element_type=jnp.float32
    )


def column_sums(rows_low):
    return jnp.sum(rows_low.astype(jnp.float32), axis=0)


def split_heads(rows_flat):
    return rows_flat.reshape(rows_flat.shape[0], rows_flat.shape[1], HEADS, HEAD)


def front_half(inputs, params):
    model_width = inputs.shape[-1]
    normed_one = layer_norm(
        inputs, params[0].astype(jnp.float32), params[1].astype(jnp.float32)
    ).astype(jnp.bfloat16)
    joined = matmul_plain(normed_one.reshape(-1, model_width), params[2])
    bias_row = params[3].astype(jnp.float32)
    query_rows = (
        (joined[:, :model_width] + bias_row[:model_width])
        .astype(jnp.bfloat16)
        .reshape(inputs.shape)
    )
    key_rows = joined[:, model_width : 2 * model_width].astype(jnp.bfloat16).reshape(inputs.shape)
    value_rows = (
        (joined[:, 2 * model_width :] + bias_row[model_width:])
        .astype(jnp.bfloat16)
        .reshape(inputs.shape)
    )
    return (normed_one.reshape(-1, model_width), query_rows, key_rows, value_rows)


def attend_block(carried, block_in, first_row, queries, query_pos, seq_lengths):
    head_scale = HEAD ** (-0.5)
    key_count = block_in[0].shape[1]
    key_pos = jnp.arange(key_count, dtype=jnp.int32)
    allowed = (
        (key_pos[None, None, :] <= query_pos[None, :, None])
        & (key_pos[None, None, :] < seq_lengths[:, None, None])
    )[:, None]
    skipped = (first_row > query_pos[-1]) | (first_row >= jnp.max(seq_lengths))

    def attend_update():
        results = []
        for model_index in range(2):
            running, row_max, row_total = carried[model_index]
            key_rows = split_heads(block_in[2 * model_index])
            value_rows = split_heads(block_in[2 * model_index + 1])
            scores = (
                jnp.einsum(
                    "sqhd,skhd->shqk",
                    queries[model_index],
                    key_rows,
                    preferred_element_type=jnp.float32,
                )
                * head_scale
            )
            new_max = jnp.maximum(row_max, jnp.max(jnp.where(allowed, scores, -1e30), axis=-1))
            weights = jnp.where(allowed, jnp.exp(scores - new_max[..., None]), 0.0)
            row_total = jnp.sum(weights, axis=-1)
            running = jnp.einsum(
                "shqk,skhd->shqd",
                weights.astype(jnp.bfloat16),
                value_rows,
                preferred_element_type=jnp.float32,
            )
            results.append((running, new_max, row_total))
        return tuple(results)

    return lax.cond(skipped, lambda: carried, attend_update)


def query_grad_block(
    carried, block_in, first_row, queries, grads_heads, log_totals, deltas, query_pos, seq_lengths
):
    head_scale = HEAD ** (-0.5)
    key_count = block_in[0].shape[1]
    key_pos = jnp.arange(key_count, dtype=jnp.int32)
    allowed = (
        (key_pos[None, None, :] <= query_pos[None, :, None])
        & (key_pos[None, None, :] < seq_lengths[:, None, None])
    )[:, None]
    skipped = (first_row > query_pos[-1]) | (first_row >= jnp.max(seq_lengths))

    def query_update():
        results = []
        for model_index in range(2):
            key_rows = split_heads(block_in[2 * model_index])
            value_rows = split_heads(block_in[2 * model_index + 1])
            scores = (
                jnp.einsum(
                    "sqhd,skhd->shqk",
                    queries[model_index],
                    key_rows,
                    preferred_element_type=jnp.float32,
                )
                * head_scale
            )
            prob_rows = jnp.where(
                allowed, jnp.exp(scores - log_totals[model_index][..., None]), 0.0
            )
            grad_prob = jnp.einsum(
                "sqhd,skhd->shqk",
                grads_heads[model_index],
                value_rows,
                preferred_element_type=jnp.float32,
            )
            grad_scores = (prob_rows * (grad_prob - deltas[model_index][..., None])).astype(
                jnp.bfloat16
            )
            results.append(
                carried[model_index]
                + jnp.einsum(
                    "shqk,skhd->shqd", grad_scores, key_rows, preferred_element_type=jnp.float32
                )
                * head_scale
            )
        return tuple(results)

    return lax.cond(skipped, lambda: carried, query_update)


def key_grad_block(carried, block_in, first_row, keys_local, values_local, key_pos, seq_lengths):
    head_scale = HEAD ** (-0.5)
    query_count = block_in[0].shape[1]
    query_pos = jnp.arange(query_count, dtype=jnp.int32)
    allowed = (
        (key_pos[None, None, :] <= query_pos[None, :, None])
        & (key_pos[None, None, :] < seq_lengths[:, None, None])
    )[:, None]
    skipped = (first_row + query_count - 1 < key_pos[0]) | (key_pos[0] >= jnp.max(seq_lengths))

    def key_update():
        results = []
        for model_index in range(2):
            grad_keys, grad_values = carried[model_index]
            query_rows = split_heads(block_in[4 * model_index])
            grad_rows = split_heads(block_in[4 * model_index + 1])
            log_rows = jnp.transpose(block_in[4 * model_index + 2], (0, 2, 1))
            delta_rows = jnp.transpose(block_in[4 * model_index + 3], (0, 2, 1))
            scores = (
                jnp.einsum(
                    "sqhd,skhd->shqk",
                    query_rows,
                    keys_local[model_index],
                    preferred_element_type=jnp.float32,
                )
                * head_scale
            )
            prob_rows = jnp.where(allowed, jnp.exp(scores - log_rows[..., None]), 0.0)
            grad_values = grad_values + jnp.einsum(
                "shqk,sqhd->shkd",
                prob_rows.astype(jnp.bfloat16),
                grad_rows,
                preferred_element_type=jnp.float32,
            )
            grad_prob = jnp.einsum(
                "sqhd,skhd->shqk",
                grad_rows,
                values_local[model_index],
                preferred_element_type=jnp.float32,
            )
            grad_scores = (prob_rows * (grad_prob - delta_rows[..., None])).astype(jnp.bfloat16)
            grad_keys = (
                grad_keys
                + jnp.einsum(
                    "shqk,sqhd->shkd", grad_scores, query_rows, preferred_element_type=jnp.float32
                )
                * head_scale
            )
            results.append((grad_keys, grad_values))
        return tuple(results)

    return lax.cond(skipped, lambda: carried, key_update)


def shards(
    hidden,
    lengths,
    student_first_gain,
    student_first_shift,
    student_attend_weight,
    student_attend_bias,
    student_output_weight,
    student_output_bias,
    student_second_gain,
    student_second_shift,
    student_expand_weight,
    student_expand_bias,
    student_reduce_weight,
    student_reduce_bias,
    teacher_first_gain,
    teacher_first_shift,
    teacher_attend_weight,
    teacher_attend_bias,
    teacher_output_weight,
    teacher_output_bias,
    teacher_second_gain,
    teacher_second_shift,
    teacher_expand_weight,
    teacher_expand_bias,
    teacher_reduce_weight,
    teacher_reduce_bias,
    final_gain,
    final_shift,
    embedding,
):
    gathered = (
        lax.all_gather(student_first_gain, EVERY, axis=0, tiled=True),
        lax.all_gather(student_first_shift, EVERY, axis=0, tiled=True),
        lax.all_gather(student_attend_weight, EVERY, axis=0, tiled=True),
        lax.all_gather(student_attend_bias, EVERY, axis=0, tiled=True),
        lax.all_gather(student_output_weight, EVERY, axis=0, tiled=True),
        lax.all_gather(student_output_bias, EVERY, axis=0, tiled=True),
        lax.all_gather(student_second_gain, EVERY, axis=0, tiled=True),
        lax.all_gather(student_second_shift, EVERY, axis=0, tiled=True),
        lax.all_gather(student_expand_weight, EVERY, axis=0, tiled=True),
        lax.all_gather(student_expand_bias, EVERY, axis=0, tiled=True),
        lax.all_gather(student_reduce_weight, EVERY, axis=0, tiled=True),
        lax.all_gather(student_reduce_bias, EVERY, axis=0, tiled=True),
        lax.all_gather(teacher_first_gain, EVERY, axis=0, tiled=True),
        lax.all_gather(teacher_first_shift, EVERY, axis=0, tiled=True),
        lax.all_gather(teacher_attend_weight, EVERY, axis=0, tiled=True),
        lax.all_gather(teacher_attend_bias, EVERY, axis=0, tiled=True),
        lax.all_gather(teacher_output_weight, EVERY, axis=0, tiled=True),
        lax.all_gather(teacher_output_bias, EVERY, axis=0, tiled=True),
        lax.all_gather(teacher_second_gain, EVERY, axis=0, tiled=True),
        lax.all_gather(teacher_second_shift, EVERY, axis=0, tiled=True),
        lax.all_gather(teacher_expand_weight, EVERY, axis=0, tiled=True),
        lax.all_gather(teacher_expand_bias, EVERY, axis=0, tiled=True),
        lax.all_gather(teacher_reduce_weight, EVERY, axis=0, tiled=True),
        lax.all_gather(teacher_reduce_bias, EVERY, axis=0, tiled=True),
    )
    models = (tuple(gathered[:12]), tuple(gathered[12:]))
    batch_seqs, rows_local, model_width = hidden.shape
    row_count = batch_seqs * rows_local
    inputs = hidden.astype(jnp.float32)
    inputs_flat = inputs.reshape(row_count, model_width)
    query_pos = lax.axis_index(BLK) * rows_local + jnp.arange(rows_local, dtype=jnp.int32)
    fronts = [front_half(inputs, params) for params in models]
    queries = (split_heads(fronts[0][1]), split_heads(fronts[1][1]))
    zero_heads = jnp.zeros((batch_seqs, HEADS, rows_local, HEAD), jnp.float32)
    zero_rows = jnp.zeros((batch_seqs, HEADS, rows_local), jnp.float32)
    start_state = (
        zero_heads,
        jnp.full((batch_seqs, HEADS, rows_local), -1e30, jnp.float32),
        zero_rows,
    )
    folded = attend_block(
        (start_state, start_state),
        (
            lax.all_gather(fronts[0][2], BLK, axis=1, tiled=True),
            lax.all_gather(fronts[0][3], BLK, axis=1, tiled=True),
            lax.all_gather(fronts[1][2], BLK, axis=1, tiled=True),
            lax.all_gather(fronts[1][3], BLK, axis=1, tiled=True),
        ),
        jnp.int32(0),
        queries,
        query_pos,
        lengths,
    )
    gain_final = final_gain.astype(jnp.float32)
    shift_final = final_shift.astype(jnp.float32)
    caches = []
    final_rows = []
    for model_index in range(2):
        params = models[model_index]
        running, row_max, row_total = folded[model_index]
        mixed_rows = (
            jnp.transpose(running / row_total[..., None], (0, 2, 1, 3))
            .reshape(row_count, model_width)
            .astype(jnp.bfloat16)
        )
        log_total = row_max + jnp.log(row_total)
        middle = inputs_flat + matmul_plain(mixed_rows, params[4]) + params[5].astype(jnp.float32)
        normed_two = layer_norm(
            middle, params[6].astype(jnp.float32), params[7].astype(jnp.float32)
        ).astype(jnp.bfloat16)
        inner_rows = matmul_plain(normed_two, params[8]) + params[9].astype(jnp.float32)
        active = gelu_tanh(inner_rows).astype(jnp.bfloat16)
        block_out = middle + matmul_plain(active, params[10]) + params[11].astype(jnp.float32)
        final_rows.append(layer_norm(block_out, gain_final, shift_final).astype(jnp.bfloat16))
        caches.append((mixed_rows, log_total, middle, normed_two, inner_rows, active, block_out))
    all_rows = lax.all_gather(jnp.stack(final_rows), VOCAB, axis=1, tiled=True)
    vocab_local = embedding.shape[0]
    vocab_index = lax.axis_index(VOCAB)
    column_valid = (
        vocab_index * vocab_local + jnp.arange(vocab_local, dtype=jnp.int32) < VOCAB_REAL
    )[None, :]
    total_rows = all_rows.shape[1]

    def scaled_logits(rows_pair):
        scaled_student = jnp.where(
            column_valid, matmul_right_t(rows_pair[0], embedding) * 0.5, -1e30
        )
        scaled_teacher = jnp.where(
            column_valid, matmul_right_t(rows_pair[1], embedding) * 0.5, -1e30
        )
        return (scaled_student, scaled_teacher)

    stat_rows = math.gcd(total_rows, 512)

    def local_stats(block_index):
        rows_pair = lax.dynamic_slice_in_dim(all_rows, block_index * stat_rows, stat_rows, 1)
        scaled_student, scaled_teacher = scaled_logits(rows_pair)
        max_student = jnp.max(scaled_student, axis=-1)
        max_teacher = jnp.max(scaled_teacher, axis=-1)
        exp_student = jnp.where(column_valid, jnp.exp(scaled_student - max_student[:, None]), 0.0)
        exp_teacher = jnp.where(column_valid, jnp.exp(scaled_teacher - max_teacher[:, None]), 0.0)
        cross_sum = jnp.sum(exp_teacher * (scaled_teacher - scaled_student), axis=-1)
        return (
            max_student,
            jnp.sum(exp_student, axis=-1),
            max_teacher,
            jnp.sum(exp_teacher, axis=-1),
            cross_sum,
        )

    stat_blocks = lax.map(local_stats, jnp.arange(total_rows // stat_rows))
    max_student, sum_student, max_teacher, sum_teacher, cross_sum = [
        stat_block.reshape(total_rows) for stat_block in stat_blocks
    ]
    top_student, top_teacher = lax.pmax((max_student, max_teacher), VOCAB)
    factor_student = jnp.exp(max_student - top_student)
    factor_teacher = jnp.exp(max_teacher - top_teacher)
    sum_student, sum_teacher, cross_sum = lax.psum(
        (sum_student * factor_student, sum_teacher * factor_teacher, cross_sum * factor_teacher),
        VOCAB,
    )
    max_student, max_teacher = (top_student, top_teacher)
    lse_student = max_student + jnp.log(sum_student)
    lse_teacher = max_teacher + jnp.log(sum_teacher)
    divergence_rows = cross_sum / sum_teacher - lse_teacher + lse_student
    valid_rows = (query_pos[None, :] < lengths[:, None]).astype(jnp.float32)
    own_start = vocab_index * row_count
    kl_out = (
        4.0
        * lax.dynamic_slice_in_dim(divergence_rows, own_start, row_count).reshape(
            batch_seqs, rows_local
        )
        * valid_rows
    )
    step_rows = math.gcd(row_count * lax.axis_size(VOCAB), 512)

    def one_block(block_index):
        begin = block_index * step_rows
        rows_pair = lax.dynamic_slice_in_dim(all_rows, begin, step_rows, 1)
        scaled_student, scaled_teacher = scaled_logits(rows_pair)
        log_student = (
            scaled_student - lax.dynamic_slice_in_dim(lse_student, begin, step_rows)[:, None]
        )
        log_teacher = (
            scaled_teacher - lax.dynamic_slice_in_dim(lse_teacher, begin, step_rows)[:, None]
        )
        row_kl = lax.dynamic_slice_in_dim(divergence_rows, begin, step_rows)[:, None]
        prob_student = jnp.where(column_valid, jnp.exp(log_student), 0.0)
        prob_teacher = jnp.where(column_valid, jnp.exp(log_teacher), 0.0)
        grad_student = (2.0 * (prob_student - prob_teacher)).astype(jnp.bfloat16)
        grad_teacher = (2.0 * prob_teacher * (log_teacher - log_student - row_kl)).astype(
            jnp.bfloat16
        )
        return jnp.concatenate(
            [matmul_plain(grad_student, embedding), matmul_plain(grad_teacher, embedding)], axis=1
        )

    grad_final = (
        lax.psum_scatter(
            lax.map(one_block, jnp.arange(row_count * lax.axis_size(VOCAB) // step_rows))
            .reshape(row_count * lax.axis_size(VOCAB), 2 * model_width)
            .astype(jnp.bfloat16),
            VOCAB,
            scatter_dimension=0,
            tiled=True,
        ).astype(jnp.float32)
        * valid_rows.reshape(row_count)[:, None]
    )
    regathered = (
        lax.all_gather(student_first_gain, EVERY, axis=0, tiled=True),
        lax.all_gather(student_first_shift, EVERY, axis=0, tiled=True),
        lax.all_gather(student_attend_weight, EVERY, axis=0, tiled=True),
        lax.all_gather(student_attend_bias, EVERY, axis=0, tiled=True),
        lax.all_gather(student_output_weight, EVERY, axis=0, tiled=True),
        lax.all_gather(student_output_bias, EVERY, axis=0, tiled=True),
        lax.all_gather(student_second_gain, EVERY, axis=0, tiled=True),
        lax.all_gather(student_second_shift, EVERY, axis=0, tiled=True),
        lax.all_gather(student_expand_weight, EVERY, axis=0, tiled=True),
        lax.all_gather(student_expand_bias, EVERY, axis=0, tiled=True),
        lax.all_gather(student_reduce_weight, EVERY, axis=0, tiled=True),
        lax.all_gather(student_reduce_bias, EVERY, axis=0, tiled=True),
        lax.all_gather(teacher_first_gain, EVERY, axis=0, tiled=True),
        lax.all_gather(teacher_first_shift, EVERY, axis=0, tiled=True),
        lax.all_gather(teacher_attend_weight, EVERY, axis=0, tiled=True),
        lax.all_gather(teacher_attend_bias, EVERY, axis=0, tiled=True),
        lax.all_gather(teacher_output_weight, EVERY, axis=0, tiled=True),
        lax.all_gather(teacher_output_bias, EVERY, axis=0, tiled=True),
        lax.all_gather(teacher_second_gain, EVERY, axis=0, tiled=True),
        lax.all_gather(teacher_second_shift, EVERY, axis=0, tiled=True),
        lax.all_gather(teacher_expand_weight, EVERY, axis=0, tiled=True),
        lax.all_gather(teacher_expand_bias, EVERY, axis=0, tiled=True),
        lax.all_gather(teacher_reduce_weight, EVERY, axis=0, tiled=True),
        lax.all_gather(teacher_reduce_bias, EVERY, axis=0, tiled=True),
    )
    back_models = (tuple(regathered[:12]), tuple(regathered[12:]))
    uppers = []
    middle_pairs = []
    for model_index in range(2):
        params = back_models[model_index]
        mixed_rows, log_total, middle, normed_two, inner_rows, active, block_out = caches[
            model_index
        ]
        _, final_pull = jax.vjp(
            lambda rows_in: layer_norm(rows_in, gain_final, shift_final), block_out
        )
        grad_out = final_pull(
            grad_final[:, model_index * model_width : (model_index + 1) * model_width]
        )[0]
        branch_low = grad_out.astype(jnp.bfloat16)
        grad_reduce_bias = column_sums(branch_low)
        grad_active = matmul_right_t(branch_low, params[10])
        _, gelu_pull = jax.vjp(gelu_tanh, inner_rows)
        inner_grad = gelu_pull(grad_active)[0].astype(jnp.bfloat16)
        grad_expand_bias = column_sums(inner_grad)
        grad_normed_two = matmul_right_t(inner_grad, params[8])
        _, second_pull = jax.vjp(
            layer_norm, middle, params[6].astype(jnp.float32), params[7].astype(jnp.float32)
        )
        middle_part, grad_second_gain, grad_second_shift = second_pull(grad_normed_two)
        grad_middle = grad_out + middle_part
        attn_low = grad_middle.astype(jnp.bfloat16)
        grad_output_bias = column_sums(attn_low)
        grad_mixed = matmul_right_t(attn_low, params[4]).astype(jnp.bfloat16)
        delta_rows = jnp.sum(
            (grad_mixed.astype(jnp.float32) * mixed_rows.astype(jnp.float32)).reshape(
                batch_seqs, rows_local, HEADS, HEAD
            ),
            axis=-1,
        )
        uppers.append(
            (
                grad_output_bias,
                grad_second_gain,
                grad_second_shift,
                grad_expand_bias,
                grad_reduce_bias,
                grad_middle,
                grad_mixed.reshape(batch_seqs, rows_local, model_width),
                delta_rows,
            )
        )
        middle_pairs.append(
            ((mixed_rows, attn_low), (normed_two, inner_grad), (active, branch_low))
        )
    grads_heads = (split_heads(uppers[0][6]), split_heads(uppers[1][6]))
    log_totals = (caches[0][1], caches[1][1])
    deltas = (jnp.transpose(uppers[0][7], (0, 2, 1)), jnp.transpose(uppers[1][7], (0, 2, 1)))
    query_grads = query_grad_block(
        (zero_heads, zero_heads),
        (
            lax.all_gather(fronts[0][2], BLK, axis=1, tiled=True),
            lax.all_gather(fronts[0][3], BLK, axis=1, tiled=True),
            lax.all_gather(fronts[1][2], BLK, axis=1, tiled=True),
            lax.all_gather(fronts[1][3], BLK, axis=1, tiled=True),
        ),
        jnp.int32(0),
        queries,
        grads_heads,
        log_totals,
        deltas,
        query_pos,
        lengths,
    )
    keys_local = (split_heads(fronts[0][2]), split_heads(fronts[1][2]))
    values_local = (split_heads(fronts[0][3]), split_heads(fronts[1][3]))
    key_grads = key_grad_block(
        ((zero_heads, zero_heads), (zero_heads, zero_heads)),
        (
            lax.all_gather(fronts[0][1], BLK, axis=1, tiled=True),
            lax.all_gather(uppers[0][6], BLK, axis=1, tiled=True),
            lax.all_gather(
                for_sending(jnp.transpose(log_totals[0], (0, 2, 1))), BLK, axis=1, tiled=True
            ),
            lax.all_gather(uppers[0][7].astype(jnp.bfloat16), BLK, axis=1, tiled=True).astype(
                jnp.float32
            ),
            lax.all_gather(fronts[1][1], BLK, axis=1, tiled=True),
            lax.all_gather(uppers[1][6], BLK, axis=1, tiled=True),
            lax.all_gather(
                for_sending(jnp.transpose(log_totals[1], (0, 2, 1))), BLK, axis=1, tiled=True
            ),
            lax.all_gather(uppers[1][7].astype(jnp.bfloat16), BLK, axis=1, tiled=True).astype(
                jnp.float32
            ),
        ),
        jnp.int32(0),
        keys_local,
        values_local,
        query_pos,
        lengths,
    )
    vectors = []
    pairs = []
    input_grad = jnp.zeros((row_count, model_width), jnp.float32)
    for model_index in range(2):
        params = back_models[model_index]
        upper = uppers[model_index]
        grad_keys, grad_values = key_grads[model_index]
        joined_grad = jnp.concatenate(
            [
                jnp.transpose(query_grads[model_index], (0, 2, 1, 3)).reshape(
                    row_count, model_width
                ),
                jnp.transpose(grad_keys, (0, 2, 1, 3)).reshape(row_count, model_width),
                jnp.transpose(grad_values, (0, 2, 1, 3)).reshape(row_count, model_width),
            ],
            axis=1,
        ).astype(jnp.bfloat16)
        bias_sums = column_sums(joined_grad)
        grad_attend_bias = jnp.concatenate([bias_sums[:model_width], bias_sums[2 * model_width :]])
        grad_normed_one = matmul_right_t(joined_grad, params[2])
        _, first_pull = jax.vjp(
            layer_norm, inputs_flat, params[0].astype(jnp.float32), params[1].astype(jnp.float32)
        )
        input_part, grad_first_gain, grad_first_shift = first_pull(grad_normed_one)
        input_grad = input_grad + upper[5] + input_part
        vectors.append(
            [
                grad_first_gain,
                grad_first_shift,
                grad_attend_bias,
                upper[0],
                upper[1],
                upper[2],
                upper[3],
                upper[4],
            ]
        )
        pairs.append(
            [
                (fronts[model_index][0], joined_grad),
                middle_pairs[model_index][0],
                middle_pairs[model_index][1],
                middle_pairs[model_index][2],
            ]
        )
    grads = []
    for model_index in range(2):
        matrix_list = [matmul_left_t(pair[0], pair[1]) for pair in pairs[model_index]]
        vector_list = vectors[model_index]
        grads.extend(
            [
                vector_list[0],
                vector_list[1],
                matrix_list[0],
                vector_list[2],
                matrix_list[1],
                vector_list[3],
                vector_list[4],
                vector_list[5],
                matrix_list[2],
                vector_list[6],
                matrix_list[3],
                vector_list[7],
            ]
        )
    summed = (
        lax.psum_scatter(grads[0], EVERY, scatter_dimension=0, tiled=True),
        lax.psum_scatter(grads[1], EVERY, scatter_dimension=0, tiled=True),
        lax.psum_scatter(grads[2], EVERY, scatter_dimension=0, tiled=True),
        lax.psum_scatter(grads[3], EVERY, scatter_dimension=0, tiled=True),
        lax.psum_scatter(grads[4], EVERY, scatter_dimension=0, tiled=True),
        lax.psum_scatter(grads[5], EVERY, scatter_dimension=0, tiled=True),
        lax.psum_scatter(grads[6], EVERY, scatter_dimension=0, tiled=True),
        lax.psum_scatter(grads[7], EVERY, scatter_dimension=0, tiled=True),
        lax.psum_scatter(grads[8], EVERY, scatter_dimension=0, tiled=True),
        lax.psum_scatter(grads[9], EVERY, scatter_dimension=0, tiled=True),
        lax.psum_scatter(grads[10], EVERY, scatter_dimension=0, tiled=True),
        lax.psum_scatter(grads[11], EVERY, scatter_dimension=0, tiled=True),
        lax.psum_scatter(grads[12], EVERY, scatter_dimension=0, tiled=True),
        lax.psum_scatter(grads[13], EVERY, scatter_dimension=0, tiled=True),
        lax.psum_scatter(grads[14], EVERY, scatter_dimension=0, tiled=True),
        lax.psum_scatter(grads[15], EVERY, scatter_dimension=0, tiled=True),
        lax.psum_scatter(grads[16], EVERY, scatter_dimension=0, tiled=True),
        lax.psum_scatter(grads[17], EVERY, scatter_dimension=0, tiled=True),
        lax.psum_scatter(grads[18], EVERY, scatter_dimension=0, tiled=True),
        lax.psum_scatter(grads[19], EVERY, scatter_dimension=0, tiled=True),
        lax.psum_scatter(grads[20], EVERY, scatter_dimension=0, tiled=True),
        lax.psum_scatter(grads[21], EVERY, scatter_dimension=0, tiled=True),
        lax.psum_scatter(grads[22], EVERY, scatter_dimension=0, tiled=True),
        lax.psum_scatter(grads[23], EVERY, scatter_dimension=0, tiled=True),
    )
    return tuple(summed) + (input_grad.reshape(batch_seqs, rows_local, model_width), kl_out)


LANES = 128
MARGIN = 16.0
VMEM_BYTES = 60 * 1024 * 1024


def lane_fold(tile_in, combine):
    folded = tile_in[:, :LANES]
    for start in range(LANES, tile_in.shape[1], LANES):
        folded = combine(folded, tile_in[:, start : start + LANES])
    return folded


def whole_block(shape):
    return pl.BlockSpec(shape, lambda *_: (0,) * len(shape))


def vocab_stats_kernel(
    scalars_ref,
    student_low_ref,
    student_high_ref,
    teacher_low_ref,
    teacher_high_ref,
    embed_ref,
    logit_student_ref,
    logit_teacher_ref,
    stats_ref,
    tile_max_s,
    tile_max_t,
    max_s,
    max_t,
    sum_s,
    sum_t,
    cross,
    part_s,
    part_t,
    part_x,
    *,
    tile,
    rows_block,
):
    step_index = pl.program_id(0)
    steps = pl.num_programs(0)
    half_rows = student_low_ref.shape[1]
    rows = 2 * half_rows

    @pl.when(step_index == 0)
    def _():
        max_s[...] = jnp.full_like(max_s, -1e30)
        max_t[...] = jnp.full_like(max_t, -1e30)
        for total in (sum_s, sum_t, cross):
            total[...] = jnp.zeros_like(total)

    def sums(scaled_s, scaled_t, top_s, top_t):
        shifted_s = scaled_s - top_s
        shifted_t = scaled_t - top_t
        exp_s = jnp.exp(shifted_s)
        exp_t = jnp.exp(shifted_t)
        return (
            lane_fold(exp_s, jnp.add),
            lane_fold(exp_t, jnp.add),
            lane_fold(exp_t * (shifted_t - shifted_s), jnp.add),
        )

    def one_tile(masked):
        embed_tile = embed_ref[...]
        excess = None
        for start in range(0, rows, rows_block):
            here = pl.ds(start, rows_block)
            source = pl.ds(start % half_rows, rows_block)
            student_ref = student_low_ref if start < half_rows else student_high_ref
            teacher_ref = teacher_low_ref if start < half_rows else teacher_high_ref
            scaled_s = matmul_right_t(student_ref[0, source, :], embed_tile)
            scaled_t = matmul_right_t(teacher_ref[0, source, :], embed_tile)
            if masked:
                column = lax.broadcasted_iota(jnp.int32, (1, tile), 1) + step_index * tile
                scaled_s = jnp.where(column < scalars_ref[0], scaled_s, -1e30)
                scaled_t = jnp.where(column < scalars_ref[0], scaled_t, -1e30)
            logit_student_ref[here, :] = scaled_s
            logit_teacher_ref[here, :] = scaled_t
            tops_s = lane_fold(scaled_s, jnp.maximum)
            tops_t = lane_fold(scaled_t, jnp.maximum)
            tile_max_s[here, :] = tops_s
            tile_max_t[here, :] = tops_t
            old_s = max_s[here, :]
            old_t = max_t[here, :]
            part_s[here, :], part_t[here, :], part_x[here, :] = sums(
                scaled_s, scaled_t, old_s[:, :1], old_t[:, :1]
            )
            over = jnp.maximum(tops_s - old_s, tops_t - old_t)
            excess = over if excess is None else jnp.maximum(excess, over)

        @pl.when(jnp.max(excess) > MARGIN)
        def _():
            def rescale(chunk, _):
                here = pl.ds(pl.multiple_of(chunk * 64, 64), 64)
                old_s = max_s[here, :]
                old_t = max_t[here, :]
                new_s = jnp.maximum(old_s, jnp.max(tile_max_s[here, :], axis=1, keepdims=True))
                new_t = jnp.maximum(old_t, jnp.max(tile_max_t[here, :], axis=1, keepdims=True))
                factor_t = jnp.exp(old_t - new_t)
                moved = (old_t - old_s) - (new_t - new_s)
                max_s[here, :] = new_s
                max_t[here, :] = new_t
                sum_s[here, :] = sum_s[here, :] * jnp.exp(old_s - new_s)
                cross[here, :] = (cross[here, :] + moved * sum_t[here, :]) * factor_t
                sum_t[here, :] = sum_t[here, :] * factor_t
                part_s[here, :], part_t[here, :], part_x[here, :] = sums(
                    logit_student_ref[here, :],
                    logit_teacher_ref[here, :],
                    new_s[:, :1],
                    new_t[:, :1],
                )
                return 0

            lax.fori_loop(0, rows // 64, rescale, 0)

        sum_s[...] += part_s[...]
        sum_t[...] += part_t[...]
        cross[...] += part_x[...]

    @pl.when(step_index < steps - 1)
    def _():
        one_tile(False)

    @pl.when(step_index == steps - 1)
    def _():
        one_tile(True)
        lane = lax.broadcasted_iota(jnp.int32, (rows, LANES), 1)
        result = jnp.sum(cross[...], axis=1, keepdims=True)
        result = jnp.where(lane == 3, jnp.sum(sum_t[...], axis=1, keepdims=True), result)
        result = jnp.where(lane == 2, jnp.sum(sum_s[...], axis=1, keepdims=True), result)
        result = jnp.where(lane == 0, max_s[...], jnp.where(lane == 1, max_t[...], result))
        stats_ref[...] = result.T[:8, :]


def vocab_stats(final_parts, is_teacher, embedding, valid_columns, tile=1280, rows_block=256):
    _, half_rows, width = final_parts.shape
    rows = 2 * half_rows
    steps = pl.cdiv(embedding.shape[0], tile)
    logits = jax.ShapeDtypeStruct((rows, steps * tile), jnp.float32)
    part_spec = lambda teacher, second: pl.BlockSpec(
        (1, half_rows, width),
        lambda j, scalars: (2 * (scalars[1] ^ teacher) + second, 0, 0),
    )
    return pl.pallas_call(
        functools.partial(vocab_stats_kernel, tile=tile, rows_block=rows_block),
        grid_spec=pltpu.PrefetchScalarGridSpec(
            num_scalar_prefetch=1,
            grid=(steps,),
            in_specs=[part_spec(0, 0), part_spec(0, 1), part_spec(1, 0), part_spec(1, 1)]
            + [pl.BlockSpec((tile, width), lambda j, *_: (j, 0))],
            out_specs=[
                pl.BlockSpec((rows, tile), lambda j, *_: (0, j)),
                pl.BlockSpec((rows, tile), lambda j, *_: (0, j)),
                whole_block((8, rows)),
            ],
            scratch_shapes=[pltpu.VMEM((rows, LANES), jnp.float32)] * 10,
        ),
        out_shape=[logits, logits, jax.ShapeDtypeStruct((8, rows), jnp.float32)],
        compiler_params=pltpu.CompilerParams(vmem_limit_bytes=VMEM_BYTES),
        name="vocab_stats",
    )(
        jnp.stack([valid_columns, is_teacher.astype(jnp.int32)]),
        *[final_parts] * 4,
        embedding,
    )


def vocab_grads_kernel(
    logit_student_ref,
    logit_teacher_ref,
    embed_ref,
    *refs,
    tile,
    columns,
    rows_block,
    count,
):
    stat_refs = refs[:count]
    own_ref, send_ref, divergence_ref, row_ref, student_ref, teacher_ref = refs[count:]
    step_index = pl.program_id(0)
    rows = student_ref.shape[0]
    half_rows = rows // 2

    @pl.when(step_index == 0)
    def _():
        student_ref[...] = jnp.zeros_like(student_ref)
        teacher_ref[...] = jnp.zeros_like(teacher_ref)
        parts = []
        for index in range(count):
            part = stat_refs[index][...]
            if index % 2:
                part = jnp.concatenate([part[:, half_rows:], part[:, :half_rows]], axis=1)
            parts.append([part[k : k + 1, :] for k in range(5)])
        top_s = functools.reduce(jnp.maximum, [p[0] for p in parts])
        top_t = functools.reduce(jnp.maximum, [p[1] for p in parts])
        sum_s = sum(p[2] * jnp.exp(p[0] - top_s) for p in parts)
        sum_t = sum(p[3] * jnp.exp(p[1] - top_t) for p in parts)
        cross = sum((p[4] + (p[1] - p[0]) * p[3]) * jnp.exp(p[1] - top_t) for p in parts)
        lse_s = top_s + jnp.log(sum_s)
        lse_t = top_t + jnp.log(sum_t)
        mean_gap = cross / sum_t
        divergence_ref[...] = jnp.broadcast_to(mean_gap - lse_t + lse_s, divergence_ref.shape)
        line = lax.broadcasted_iota(jnp.int32, (LANES, rows), 0)
        row_ref[...] = jnp.where(line == 0, lse_s, jnp.where(line == 1, lse_t, mean_gap)).T

    def one_tile(masked):
        embed_tile = embed_ref[...]
        if masked:
            row = lax.broadcasted_iota(jnp.int32, (tile, 1), 0) + step_index * tile
            embed_tile = jnp.where(row < columns, embed_tile, jnp.zeros_like(embed_tile))
        for start in range(0, rows, rows_block):
            here = pl.ds(start, rows_block)
            scaled_s = logit_student_ref[here, :]
            scaled_t = logit_teacher_ref[here, :]
            prob_s = jnp.exp(scaled_s - row_ref[here, 0:1])
            prob_t = jnp.exp(scaled_t - row_ref[here, 1:2])
            grad_s = (prob_s - prob_t).astype(jnp.bfloat16)
            grad_t = (prob_t * ((scaled_t - scaled_s) - row_ref[here, 2:3])).astype(jnp.bfloat16)
            student_ref[here, :] += matmul_plain(grad_s, embed_tile)
            teacher_ref[here, :] += matmul_plain(grad_t, embed_tile)

    last = pl.num_programs(0) - 1

    @pl.when(step_index < last)
    def _():
        one_tile(False)

    @pl.when(step_index == last)
    def _():
        one_tile(True)
        for index, sums in enumerate((student_ref, teacher_ref)):
            own_ref[index] = sums[:half_rows, :]
            send_ref[index] = sums[half_rows:, :].astype(jnp.bfloat16)


def vocab_grads(logit_student, logit_teacher, embedding, stat_parts, tile=1280, rows_block=256):
    rows = logit_student.shape[0]
    columns, width = embedding.shape
    halves = (2, rows // 2, width)
    return pl.pallas_call(
        functools.partial(
            vocab_grads_kernel,
            tile=tile,
            columns=columns,
            rows_block=rows_block,
            count=len(stat_parts),
        ),
        grid=(pl.cdiv(columns, tile),),
        in_specs=[
            pl.BlockSpec((rows, tile), lambda j: (0, j)),
            pl.BlockSpec((rows, tile), lambda j: (0, j)),
            pl.BlockSpec((tile, width), lambda j: (j, 0)),
        ]
        + [whole_block((8, rows))] * len(stat_parts),
        out_specs=[whole_block(halves), whole_block(halves), whole_block((8, rows))],
        out_shape=[
            jax.ShapeDtypeStruct(halves, jnp.float32),
            jax.ShapeDtypeStruct(halves, jnp.bfloat16),
            jax.ShapeDtypeStruct((8, rows), jnp.float32),
        ],
        scratch_shapes=[
            pltpu.VMEM((rows, LANES), jnp.float32),
            pltpu.VMEM((rows, width), jnp.float32),
            pltpu.VMEM((rows, width), jnp.float32),
        ],
        compiler_params=pltpu.CompilerParams(vmem_limit_bytes=VMEM_BYTES),
        name="vocab_grads",
    )(logit_student, logit_teacher, embedding, *stat_parts)


def attend_kernel(length_ref, query_ref, key_ref, value_ref, mixed_ref, *, block):
    rows = query_ref.shape[0]
    lane = lax.broadcasted_iota(jnp.int32, (1, LANES), 1)
    for start in range(0, rows, block):
        keys = start + block
        key_pos = lax.broadcasted_iota(jnp.int32, (block, keys), 1)
        query_pos = lax.broadcasted_iota(jnp.int32, (block, keys), 0) + start
        allowed = (key_pos <= query_pos) & (key_pos < length_ref[0])
        outs = []
        for head in range(LANES // HEAD):
            own = (lane // HEAD) == head
            queries = query_ref[start : start + block, :] * HEAD**-0.5
            queries = jnp.where(own, queries, jnp.zeros_like(queries))
            scores = matmul_right_t(queries, key_ref[:keys, :])
            scores = jnp.where(allowed, scores, -1e30)
            weights = jnp.exp(scores - jnp.max(scores, axis=1, keepdims=True))
            total = jnp.sum(weights, axis=1, keepdims=True)
            outs.append(
                matmul_plain(weights.astype(jnp.bfloat16), value_ref[:keys, :]) / total
            )
        mixed_ref[start : start + block, :] = jnp.where(lane < HEAD, outs[0], outs[1]).astype(
            jnp.bfloat16
        )


def attend_rows(joined, seq_length, block):
    rows, width = joined.shape
    third = width // 3
    pairs = third // LANES
    spec = lambda part: pl.BlockSpec((rows, LANES), lambda p, *_: (0, part * pairs + p))
    return pl.pallas_call(
        functools.partial(attend_kernel, block=block),
        grid_spec=pltpu.PrefetchScalarGridSpec(
            num_scalar_prefetch=1,
            grid=(pairs,),
            in_specs=[spec(0), spec(1), spec(2)],
            out_specs=spec(0),
        ),
        out_shape=jax.ShapeDtypeStruct((rows, third), jnp.bfloat16),
        compiler_params=pltpu.CompilerParams(vmem_limit_bytes=VMEM_BYTES),
        name="attend",
    )(seq_length.reshape(1), joined, joined, joined)


def attend_grads_kernel(
    length_ref,
    query_ref,
    key_ref,
    value_ref,
    grad_ref,
    grad_query_ref,
    grad_key_ref,
    grad_value_ref,
    sum_key,
    sum_value,
    *,
    block,
):
    rows = query_ref.shape[0]
    lane = lax.broadcasted_iota(jnp.int32, (1, LANES), 1)
    sum_key[...] = jnp.zeros_like(sum_key)
    sum_value[...] = jnp.zeros_like(sum_value)
    keys_turned = key_ref[...].T
    for start in range(0, rows, block):
        keys = start + block
        key_pos = lax.broadcasted_iota(jnp.int32, (keys, block), 0)
        query_pos = lax.broadcasted_iota(jnp.int32, (keys, block), 1) + start
        allowed = (key_pos <= query_pos) & (key_pos < length_ref[0])
        outs = []
        for head in range(LANES // HEAD):
            own = (lane // HEAD) == head
            queries = query_ref[start : start + block, :] * HEAD**-0.5
            queries = jnp.where(own, queries, jnp.zeros_like(queries))
            grads = grad_ref[start : start + block, :]
            grads = jnp.where(own, grads, jnp.zeros_like(grads))
            scores = matmul_right_t(key_ref[:keys, :], queries)
            scores = jnp.where(allowed, scores, -1e30)
            weights = jnp.exp(scores - jnp.max(scores, axis=0, keepdims=True))
            soft = weights * (1.0 / jnp.sum(weights, axis=0, keepdims=True))
            grad_soft = matmul_right_t(value_ref[:keys, :], grads)
            soft_grad = soft * grad_soft
            delta = jnp.sum(soft_grad, axis=0, keepdims=True)
            grad_scores = (soft_grad - soft * delta).astype(jnp.bfloat16)
            sum_value[:keys, :] += matmul_plain(soft.astype(jnp.bfloat16), grads)
            sum_key[:keys, :] += matmul_plain(grad_scores, queries)
            outs.append(matmul_plain(keys_turned[:, :keys], grad_scores))
        head_row = lax.broadcasted_iota(jnp.int32, (LANES, 1), 0)
        turned = jnp.where(head_row < HEAD, outs[0], outs[1]) * HEAD**-0.5
        grad_query_ref[start : start + block, :] = turned.T.astype(jnp.bfloat16)
    grad_key_ref[...] = sum_key[...].astype(jnp.bfloat16)
    grad_value_ref[...] = sum_value[...].astype(jnp.bfloat16)


def attend_grads(joined, grad_mixed, seq_length, block):
    rows, width = joined.shape
    third = width // 3
    pairs = third // LANES
    spec = lambda part: pl.BlockSpec((rows, LANES), lambda p, *_: (0, part * pairs + p))
    out = jax.ShapeDtypeStruct((rows, third), jnp.bfloat16)
    return pl.pallas_call(
        functools.partial(attend_grads_kernel, block=block),
        grid_spec=pltpu.PrefetchScalarGridSpec(
            num_scalar_prefetch=1,
            grid=(pairs,),
            in_specs=[spec(0), spec(1), spec(2), spec(0)],
            out_specs=[spec(0)] * 3,
            scratch_shapes=[pltpu.VMEM((rows, LANES), jnp.float32)] * 2,
        ),
        out_shape=[out] * 3,
        compiler_params=pltpu.CompilerParams(vmem_limit_bytes=VMEM_BYTES),
        name="attend_grads",
    )(seq_length.reshape(1), joined, joined, joined, grad_mixed)


def place_kernel(own_ref, *refs, count, cuts):
    for index in range(count):
        target = own_ref[0] ^ index
        for (first_row, rows, first_lane, lanes), out in zip(cuts, refs[count:]):
            out[pl.ds(pl.multiple_of(target * rows, 16), rows), :] = refs[index][
                first_row : first_row + rows, first_lane : first_lane + lanes
            ]


def place_blocks(blocks, own, cuts):
    count = len(blocks)
    return pl.pallas_call(
        functools.partial(place_kernel, count=count, cuts=cuts),
        in_specs=[pl.BlockSpec(memory_space=pltpu.SMEM)]
        + [pl.BlockSpec(memory_space=pltpu.VMEM)] * count,
        out_specs=[pl.BlockSpec(memory_space=pltpu.VMEM)] * len(cuts),
        out_shape=[
            jax.ShapeDtypeStruct((count * rows, lanes), jnp.bfloat16)
            for _, rows, _, lanes in cuts
        ],
        compiler_params=pltpu.CompilerParams(vmem_limit_bytes=VMEM_BYTES),
        name="place_blocks",
    )(own.reshape(1), *blocks)


def swap(rows, axis, distance):
    count = lax.axis_size(axis)
    return lax.ppermute(rows, axis, [(index, index ^ distance) for index in range(count)])


def in_pair(second, mine, other, axis=0):
    return jnp.where(
        second,
        jnp.concatenate([other, mine], axis=axis),
        jnp.concatenate([mine, other], axis=axis),
    )


def in_order(index, parts):
    low = (index & 1) == 1
    high = (index & 2) == 2
    pairs = [
        [jnp.where(low, parts[k + 1], parts[k]), jnp.where(low, parts[k], parts[k + 1])]
        for k in (0, 2)
    ]
    return [
        jnp.where(high, pairs[1][0], pairs[0][0]),
        jnp.where(high, pairs[1][1], pairs[0][1]),
        jnp.where(high, pairs[0][0], pairs[1][0]),
        jnp.where(high, pairs[0][1], pairs[1][1]),
    ]


def norm_back(inputs, gain_row, grad):
    centred = inputs - jnp.mean(inputs, axis=-1, keepdims=True)
    inverse = lax.rsqrt(jnp.mean(centred * centred, axis=-1, keepdims=True) + 1e-05)
    normal = centred * inverse
    scaled = grad * gain_row
    along = jnp.mean(scaled * normal, axis=-1, keepdims=True)
    result = inverse * (scaled - jnp.mean(scaled, axis=-1, keepdims=True) - normal * along)
    return result, jnp.sum(grad * normal, axis=0), jnp.sum(grad, axis=0)


def gelu_slope(inputs):
    root = math.sqrt(2.0 / math.pi)
    square = inputs * inputs
    bent = jnp.tanh(root * inputs * (1.0 + 0.044715 * square))
    return 0.5 * (1.0 + bent) + 0.5 * inputs * (1.0 - bent * bent) * root * (
        1.0 + 3 * 0.044715 * square
    )


def rows_of(array_in, start, count):
    return lax.dynamic_slice_in_dim(array_in, start, count, 0)


def columns_of(array_in, start, count):
    return lax.dynamic_slice_in_dim(array_in, start, count, 1)


def pack_weights(params, half, seq_length):
    attend, output, expand, reduce = params[2], params[4], params[8], params[10]
    width = output.shape[1]
    part = width // 2
    wide = expand.shape[1] // 2
    begin = half * part
    front = jnp.concatenate(
        [attend[:, k * width + begin : k * width + begin + part] for k in range(3)], axis=1
    )
    length_parts = jnp.stack([seq_length // 32, seq_length % 32]).astype(jnp.bfloat16)
    lines = [params[k] for k in (0, 1, 5, 6, 7, 11, 3, 9)]
    lines[0] = jnp.concatenate(
        [lines[0], jnp.zeros((LANES - lines[0].shape[0],), jnp.bfloat16), length_parts]
    )
    lines = [jnp.pad(line[None], ((0, 0), (0, 3 * part - line.shape[0]))) for line in lines]
    return (
        jnp.concatenate([front] + lines, axis=0),
        jnp.concatenate(
            [expand[:, half * wide : (half + 1) * wide], output[:, begin : begin + part]], axis=1
        ),
        reduce[:, begin : begin + part],
    )


def exchange_models(slabs):
    index = lax.axis_index(VOCAB)
    stacked = jnp.stack(slabs)
    parts = [lax.dynamic_index_in_dim(stacked, index, 0, keepdims=False)]
    for distance in (1, 2, 3):
        parts.append(
            swap(
                lax.dynamic_index_in_dim(stacked, index ^ distance, 0, keepdims=False),
                VOCAB,
                distance,
            )
        )
    return in_order(index, parts)


def after(value, *others):
    return lax.optimization_barrier((value, others))[0]


def along_blk(block):
    return [block] + [swap(block, BLK, dz) for dz in range(1, lax.axis_size(BLK))]


def along_batch(blocks):
    result = []
    for block in blocks:
        result.append(block)
        result += [swap(block, BATCH, dy) for dy in range(1, lax.axis_size(BATCH))]
    return result


def sum_batch(block_of):
    blk, batch = lax.axis_index(BLK), lax.axis_index(BATCH)
    sums = []
    for dz in list(range(1, lax.axis_size(BLK))) + [0]:
        total = block_of(blk ^ dz, batch).astype(jnp.float32)
        for dy in range(1, lax.axis_size(BATCH)):
            total += swap(block_of(blk ^ dz, batch ^ dy), BATCH, dy).astype(jnp.float32)
        sums.append(total.astype(jnp.bfloat16) if dz else total)
    return sums


def sum_blk(sums):
    total = sums[-1]
    for dz in range(1, lax.axis_size(BLK)):
        total += swap(sums[dz - 1], BLK, dz).astype(jnp.float32)
    return total


def shards_by_model(hidden, lengths, *rest):
    embedding = rest[26]
    gain_final = rest[24].astype(jnp.float32)
    shift_final = rest[25].astype(jnp.float32)
    params = (rest[:12], rest[12:24])
    blk, batch, member = (lax.axis_index(name) for name in EVERY)
    size_blk, size_batch, size_vocab = (lax.axis_size(name) for name in EVERY)
    plane = blk * size_batch + batch
    model, half = member // 2, member % 2
    is_teacher, is_second = model == 1, half == 1
    rows_local, width = hidden.shape[1:]
    rows = rows_local * size_vocab
    own_rows = rows // 2
    part = width // 2
    ff_part = rest[8].shape[1] // 2
    shard_rows = rest[2].shape[0]
    plane_rows = shard_rows * size_vocab
    crossing = (BLK, VOCAB)

    front_slabs, middle_slabs, back_slabs = zip(
        *[pack_weights(params[m], h, lengths[0]) for m in (0, 1) for h in (0, 1)]
    )
    front = exchange_models(front_slabs)
    length_parts = sum(
        jnp.where(blk == source, front[source][shard_rows, LANES : LANES + 2], 0)
        for source in range(size_vocab)
    ).astype(jnp.int32)
    seq_length = 32 * length_parts[0] + length_parts[1]
    front_block = jnp.concatenate(
        [source[:shard_rows] for source in front] + [source[shard_rows:] for source in front],
        axis=0,
    )
    vector_lines = front_block.shape[0] - plane_rows
    front_along = along_blk(front_block)
    middle_block = jnp.concatenate(exchange_models(middle_slabs), axis=0)
    reduce_block = jnp.concatenate(exchange_models(back_slabs), axis=0)
    middle_along = along_blk(middle_block)
    reduce_along = along_blk(reduce_block)

    turn = [
        (a * size_vocab + b, b * size_vocab + a) for a in range(size_blk) for b in range(size_vocab)
    ]
    quarter = lax.ppermute(hidden[0], crossing, turn)
    quarter_far = swap(quarter, VOCAB, 2)
    quarters = in_order(
        member, [quarter, swap(quarter, VOCAB, 1), quarter_far, swap(quarter_far, VOCAB, 1)]
    )
    attend_weight, vectors = place_blocks(
        along_batch(front_along),
        plane,
        ((0, plane_rows, 0, 3 * part), (plane_rows, vector_lines, 0, LANES)),
    )
    middle_blocks = along_batch(middle_along)
    reduce_blocks = along_batch(reduce_along)

    shards_all = size_blk * size_batch * size_vocab
    vectors = vectors.reshape(shards_all, vector_lines // size_vocab, LANES).astype(jnp.float32)
    first_gain, first_shift, output_bias, second_gain, second_shift, reduce_bias = [
        vectors[:, k, :shard_rows].reshape(width) for k in range(6)
    ]
    attend_bias = vectors[:, 6, : 2 * shard_rows].reshape(2 * width)
    expand_bias = vectors[:, 7, : 4 * shard_rows].reshape(2 * ff_part)
    query_bias = rows_of(attend_bias, half * part, part)
    value_bias = rows_of(attend_bias, width + half * part, part)
    joined_bias = jnp.concatenate([query_bias, jnp.zeros((part,), jnp.float32), value_bias])
    expand_bias = rows_of(expand_bias, half * ff_part, ff_part)

    inputs_low = jnp.concatenate(quarters, axis=0)
    inputs = inputs_low.astype(jnp.float32)
    inputs_own = rows_of(inputs_low, half * own_rows, own_rows).astype(jnp.float32)
    normed_one = layer_norm(inputs, first_gain, first_shift).astype(jnp.bfloat16)
    normed_one = after(normed_one, middle_along, reduce_along)
    joined = (matmul_plain(normed_one, attend_weight) + joined_bias).astype(jnp.bfloat16)
    joined = after(joined, middle_blocks[:4])
    block = math.gcd(rows, 256)
    mixed_rows = attend_rows(joined, seq_length, block)
    mixed_rows = after(mixed_rows, middle_blocks)
    expand_weight, output_columns = place_blocks(
        middle_blocks, plane, ((0, plane_rows, 0, ff_part), (0, plane_rows, ff_part, part))
    )
    output_weight = in_pair(
        is_second,
        rows_of(output_columns, half * part, part),
        swap(rows_of(output_columns, (1 - half) * part, part), VOCAB, 1),
        axis=1,
    )
    attended = matmul_plain(mixed_rows, output_weight)
    middle = (
        inputs_own
        + rows_of(attended, half * own_rows, own_rows)
        + swap(rows_of(attended, (1 - half) * own_rows, own_rows), VOCAB, 1)
        + output_bias
    )
    normed_own = layer_norm(middle, second_gain, second_shift).astype(jnp.bfloat16)
    normed_two = jnp.concatenate([normed_own, swap(normed_own, VOCAB, 1)], axis=0)
    inner_rows = matmul_plain(normed_two, expand_weight) + expand_bias
    active = gelu_tanh(inner_rows).astype(jnp.bfloat16)
    active, slope = lax.optimization_barrier((active, gelu_slope(inner_rows)))
    reduce_rows = reduce_block.shape[0]
    (reduce_columns,) = place_blocks(reduce_blocks, plane, ((0, reduce_rows, 0, part),))
    reduce_weight = in_pair(
        is_second,
        rows_of(reduce_columns, half * ff_part, ff_part),
        swap(rows_of(reduce_columns, (1 - half) * ff_part, ff_part), VOCAB, 1),
        axis=1,
    )
    reduced = matmul_plain(active, reduce_weight)
    block_out = middle + reduced[:own_rows] + swap(reduced[own_rows:], VOCAB, 1) + reduce_bias
    final_rows = (0.5 * layer_norm(block_out, gain_final, shift_final)).astype(jnp.bfloat16)

    final_far = swap(final_rows, VOCAB, 2)
    final_parts = jnp.stack(
        [final_rows, swap(final_rows, VOCAB, 1), final_far, swap(final_far, VOCAB, 1)]
    )
    vocab_local = embedding.shape[0]
    valid_columns = jnp.clip(VOCAB_REAL - member * vocab_local, 0, vocab_local)
    logit_student, logit_teacher, stats = vocab_stats(
        final_parts, is_teacher, embedding, valid_columns
    )
    stat_parts = [stats] + [swap(stats, VOCAB, distance) for distance in (1, 2, 3)]
    own_sums, core_sums, divergence_rows = vocab_grads(
        logit_student, logit_teacher, embedding, stat_parts
    )
    positions = jnp.arange(rows, dtype=jnp.int32)
    kl_rows = in_pair(is_second, divergence_rows[0, :own_rows], divergence_rows[0, own_rows:])
    kl_rows = 4.0 * kl_rows * (positions < seq_length).astype(jnp.float32)
    kl_out = lax.ppermute(rows_of(kl_rows, member * rows_local, rows_local), crossing, turn)

    both = own_sums + swap(core_sums, VOCAB, 1).astype(jnp.float32)
    grad_final = jnp.where(is_teacher, both[1], both[0]) + swap(
        jnp.where(is_teacher, both[0], both[1]).astype(jnp.bfloat16), VOCAB, 2
    ).astype(jnp.float32)
    own_valid = (half * own_rows + positions[:own_rows] < seq_length).astype(jnp.float32)
    grad_final = grad_final * (2.0 * own_valid)[:, None]

    grad_out, _, _ = norm_back(block_out, gain_final, grad_final)
    branch_own = grad_out.astype(jnp.bfloat16)
    branch_low = jnp.concatenate([branch_own, swap(branch_own, VOCAB, 1)], axis=0)
    grad_reduce = matmul_left_t(active, branch_low).astype(jnp.bfloat16)
    grad_reduce = in_pair(
        is_second,
        columns_of(grad_reduce, half * part, part),
        swap(columns_of(grad_reduce, (1 - half) * part, part), VOCAB, 1),
    )
    reduce_pairs = sum_batch(
        lambda z, y: rows_of(grad_reduce, (z * size_batch + y) * reduce_rows, reduce_rows)
    )
    grad_active = matmul_right_t(branch_low, reduce_weight)
    inner_grad = (grad_active * slope).astype(jnp.bfloat16)
    grad_normed = matmul_right_t(inner_grad, expand_weight)
    grad_normed_own = grad_normed[:own_rows] + swap(grad_normed[own_rows:], VOCAB, 1)
    middle_part, grad_second_gain, grad_second_shift = norm_back(
        middle, second_gain, grad_normed_own
    )
    grad_middle = grad_out + middle_part
    attn_own = grad_middle.astype(jnp.bfloat16)
    attn_low = in_pair(is_second, attn_own, swap(attn_own, VOCAB, 1))
    grad_mixed = matmul_right_t(attn_low, output_weight).astype(jnp.bfloat16)
    grad_expand = matmul_left_t(normed_two, inner_grad).astype(jnp.bfloat16)
    grad_output = matmul_left_t(mixed_rows, attn_low).astype(jnp.bfloat16)
    grad_output = in_pair(
        is_second,
        columns_of(grad_output, half * part, part),
        swap(columns_of(grad_output, (1 - half) * part, part), VOCAB, 1),
    )
    grad_output = jnp.concatenate([grad_expand, grad_output], axis=1)
    middle_pairs = sum_batch(
        lambda z, y: rows_of(grad_output, (z * size_batch + y) * plane_rows, plane_rows)
    )
    grad_mixed = after(grad_mixed, reduce_pairs[:-1], grad_output)
    joined_grad = jnp.concatenate(attend_grads(joined, grad_mixed, seq_length, block), axis=1)
    reduce_sum = sum_blk(reduce_pairs)
    joined_grad = after(joined_grad, middle_pairs[:-1], reduce_sum)
    middle_sum = sum_blk(middle_pairs)
    grad_normed = matmul_right_t(joined_grad, attend_weight)
    grad_attend = matmul_left_t(normed_one, joined_grad).astype(jnp.bfloat16)
    grad_normed_own = rows_of(grad_normed, half * own_rows, own_rows) + swap(
        rows_of(grad_normed, (1 - half) * own_rows, own_rows), VOCAB, 1
    )
    input_part, grad_first_gain, grad_first_shift = norm_back(
        inputs_own, first_gain, grad_normed_own
    )
    grad_inputs = (grad_middle + input_part).reshape(2, rows_local, width)
    input_sum = jnp.where(is_teacher, grad_inputs[1], grad_inputs[0]) + swap(
        jnp.where(is_teacher, grad_inputs[0], grad_inputs[1]).astype(jnp.bfloat16), VOCAB, 2
    ).astype(jnp.float32)
    home = [
        (a * size_vocab + 2 * m + h, (2 * h + m) * size_vocab + a)
        for a in range(size_blk)
        for m in (0, 1)
        for h in (0, 1)
    ]
    input_grad = lax.ppermute(input_sum.astype(jnp.bfloat16), crossing, home).astype(jnp.float32)

    bias_sums = column_sums(joined_grad)

    def spread_half(values, count):
        return jnp.where(
            jnp.arange(2)[:, None] == half, values.reshape(1, count), 0.0
        ).reshape(2 * count)

    vector_parts = [
        grad_first_gain,
        grad_first_shift,
        column_sums(attn_own),
        grad_second_gain,
        grad_second_shift,
        column_sums(branch_own),
        jnp.concatenate(
            [spread_half(bias_sums[:part], part), spread_half(bias_sums[2 * part :], part)]
        ),
        spread_half(column_sums(inner_grad), ff_part),
    ]
    vector_grads = jnp.concatenate([v.reshape(shards_all, -1) for v in vector_parts], axis=1)
    vector_grads = jnp.pad(
        vector_grads.reshape(size_blk * size_batch, size_vocab, -1),
        ((0, 0), (0, 4), (0, 3 * part - vector_grads.shape[1])),
    ).astype(jnp.bfloat16)
    grad_front = jnp.concatenate(
        [grad_attend.reshape(size_blk * size_batch, plane_rows, 3 * part), vector_grads], axis=1
    )
    front_sum = sum_blk(
        sum_batch(
            lambda z, y: lax.dynamic_index_in_dim(grad_front, z * size_batch + y, 0, keepdims=False)
        )
    )

    share = reduce_rows // size_vocab
    back = exchange_models(
        [reduce_sum[t * share : (t + 1) * share].astype(jnp.bfloat16) for t in range(size_vocab)]
    )
    middles = exchange_models(
        [
            middle_sum[t * shard_rows : (t + 1) * shard_rows].astype(jnp.bfloat16)
            for t in range(size_vocab)
        ]
    )
    front = exchange_models(
        [
            jnp.concatenate(
                [
                    front_sum[t * shard_rows : (t + 1) * shard_rows],
                    jnp.pad(front_sum[plane_rows + t][None], ((0, 7), (0, 0))),
                ],
                axis=0,
            ).astype(jnp.bfloat16)
            for t in range(size_vocab)
        ]
    )
    results = []
    for m in (0, 1):
        sides = front[2 * m : 2 * m + 2]
        vector = sum(side[shard_rows].astype(jnp.float32) for side in sides)
        pieces = [vector[k * shard_rows : (k + 1) * shard_rows] for k in range(6)]
        attend = jnp.concatenate(
            [side[:shard_rows, k * part : (k + 1) * part] for k in range(3) for side in sides],
            axis=1,
        ).astype(jnp.float32)
        sides = middles[2 * m : 2 * m + 2]
        output = jnp.concatenate([side[:, ff_part:] for side in sides], axis=1)
        output = output.astype(jnp.float32)
        expand = jnp.concatenate([side[:, :ff_part] for side in sides], axis=1)
        expand = expand.astype(jnp.float32)
        reduce = jnp.concatenate(back[2 * m : 2 * m + 2], axis=1).astype(jnp.float32)
        results += [
            pieces[0],
            pieces[1],
            attend,
            vector[6 * shard_rows : 8 * shard_rows],
            output,
            pieces[2],
            pieces[3],
            pieces[4],
            expand,
            vector[8 * shard_rows : 12 * shard_rows],
            reduce,
            pieces[5],
        ]
    return tuple(results) + (input_grad[None], kl_out[None])


def solution(mesh):
    by_model = mesh.shape[VOCAB] == 4 and mesh.shape[BLK] == 4 and mesh.shape[BATCH] == 2
    return jax.shard_map(
        shards_by_model if by_model else shards,
        mesh=mesh,
        in_specs=(
            P((BATCH, VOCAB), BLK, None),
            P((BATCH, VOCAB)),
            P(EVERY),
            P(EVERY),
            P(EVERY, None),
            P(EVERY),
            P(EVERY, None),
            P(EVERY),
            P(EVERY),
            P(EVERY),
            P(EVERY, None),
            P(EVERY),
            P(EVERY, None),
            P(EVERY),
            P(EVERY),
            P(EVERY),
            P(EVERY, None),
            P(EVERY),
            P(EVERY, None),
            P(EVERY),
            P(EVERY),
            P(EVERY),
            P(EVERY, None),
            P(EVERY),
            P(EVERY, None),
            P(EVERY),
            P(),
            P(),
            P(VOCAB, None),
        ),
        out_specs=(
            P(EVERY),
            P(EVERY),
            P(EVERY, None),
            P(EVERY),
            P(EVERY, None),
            P(EVERY),
            P(EVERY),
            P(EVERY),
            P(EVERY, None),
            P(EVERY),
            P(EVERY, None),
            P(EVERY),
            P(EVERY),
            P(EVERY),
            P(EVERY, None),
            P(EVERY),
            P(EVERY, None),
            P(EVERY),
            P(EVERY),
            P(EVERY),
            P(EVERY, None),
            P(EVERY),
            P(EVERY, None),
            P(EVERY),
            P((BATCH, VOCAB), BLK, None),
            P((BATCH, VOCAB), BLK),
        ),
        check_vma=False,
    )
```

```python
import functools
import math

import jax
import jax.numpy as jnp
from jax import lax
from jax.experimental import pallas as pl
from jax.experimental.pallas import tpu as pltpu
from jax.sharding import PartitionSpec as P

HEADS = 12
HEAD = 64
VOCAB_REAL = 50257
BLK, BATCH, VOCAB = "blk", "batch", "vocab"
EVERY = (BLK, BATCH, VOCAB)


def for_sending(shard):
    return jax.tree.map(lambda a: a.astype(jnp.bfloat16) if a.dtype == jnp.float32 else a, shard)


def layer_norm(inputs, gain_row, shift_row):
    centred = inputs - jnp.mean(inputs, axis=-1, keepdims=True)
    spread = jnp.mean(centred * centred, axis=-1, keepdims=True)
    return centred * lax.rsqrt(spread + 1e-05) * gain_row + shift_row


def gelu_tanh(inputs):
    return jax.nn.gelu(inputs, approximate=True)


def matmul_plain(left_side, right_side):
    return jnp.dot(left_side, right_side, preferred_element_type=jnp.float32)


def matmul_right_t(left_side, right_side):
    return lax.dot_general(
        left_side, right_side, (((1,), (1,)), ((), ())), preferred_element_type=jnp.float32
    )


def matmul_left_t(left_side, right_side):
    return lax.dot_general(
        left_side, right_side, (((0,), (0,)), ((), ())), preferred_element_type=jnp.float32
    )


def column_sums(rows_low):
    return jnp.sum(rows_low.astype(jnp.float32), axis=0)


def split_heads(rows_flat):
    return rows_flat.reshape(rows_flat.shape[0], rows_flat.shape[1], HEADS, HEAD)


def front_half(inputs, params):
    model_width = inputs.shape[-1]
    normed_one = layer_norm(
        inputs, params[0].astype(jnp.float32), params[1].astype(jnp.float32)
    ).astype(jnp.bfloat16)
    joined = matmul_plain(normed_one.reshape(-1, model_width), params[2])
    bias_row = params[3].astype(jnp.float32)
    query_rows = (
        (joined[:, :model_width] + bias_row[:model_width])
        .astype(jnp.bfloat16)
        .reshape(inputs.shape)
    )
    key_rows = joined[:, model_width : 2 * model_width].astype(jnp.bfloat16).reshape(inputs.shape)
    value_rows = (
        (joined[:, 2 * model_width :] + bias_row[model_width:])
        .astype(jnp.bfloat16)
        .reshape(inputs.shape)
    )
    return (normed_one.reshape(-1, model_width), query_rows, key_rows, value_rows)


def attend_block(carried, block_in, first_row, queries, query_pos, seq_lengths):
    head_scale = HEAD ** (-0.5)
    key_count = block_in[0].shape[1]
    key_pos = jnp.arange(key_count, dtype=jnp.int32)
    allowed = (
        (key_pos[None, None, :] <= query_pos[None, :, None])
        & (key_pos[None, None, :] < seq_lengths[:, None, None])
    )[:, None]
    skipped = (first_row > query_pos[-1]) | (first_row >= jnp.max(seq_lengths))

    def attend_update():
        results = []
        for model_index in range(2):
            running, row_max, row_total = carried[model_index]
            key_rows = split_heads(block_in[2 * model_index])
            value_rows = split_heads(block_in[2 * model_index + 1])
            scores = (
                jnp.einsum(
                    "sqhd,skhd->shqk",
                    queries[model_index],
                    key_rows,
                    preferred_element_type=jnp.float32,
                )
                * head_scale
            )
            new_max = jnp.maximum(row_max, jnp.max(jnp.where(allowed, scores, -1e30), axis=-1))
            weights = jnp.where(allowed, jnp.exp(scores - new_max[..., None]), 0.0)
            row_total = jnp.sum(weights, axis=-1)
            running = jnp.einsum(
                "shqk,skhd->shqd",
                weights.astype(jnp.bfloat16),
                value_rows,
                preferred_element_type=jnp.float32,
            )
            results.append((running, new_max, row_total))
        return tuple(results)

    return lax.cond(skipped, lambda: carried, attend_update)


def query_grad_block(
    carried, block_in, first_row, queries, grads_heads, log_totals, deltas, query_pos, seq_lengths
):
    head_scale = HEAD ** (-0.5)
    key_count = block_in[0].shape[1]
    key_pos = jnp.arange(key_count, dtype=jnp.int32)
    allowed = (
        (key_pos[None, None, :] <= query_pos[None, :, None])
        & (key_pos[None, None, :] < seq_lengths[:, None, None])
    )[:, None]
    skipped = (first_row > query_pos[-1]) | (first_row >= jnp.max(seq_lengths))

    def query_update():
        results = []
        for model_index in range(2):
            key_rows = split_heads(block_in[2 * model_index])
            value_rows = split_heads(block_in[2 * model_index + 1])
            scores = (
                jnp.einsum(
                    "sqhd,skhd->shqk",
                    queries[model_index],
                    key_rows,
                    preferred_element_type=jnp.float32,
                )
                * head_scale
            )
            prob_rows = jnp.where(
                allowed, jnp.exp(scores - log_totals[model_index][..., None]), 0.0
            )
            grad_prob = jnp.einsum(
                "sqhd,skhd->shqk",
                grads_heads[model_index],
                value_rows,
                preferred_element_type=jnp.float32,
            )
            grad_scores = (prob_rows * (grad_prob - deltas[model_index][..., None])).astype(
                jnp.bfloat16
            )
            results.append(
                carried[model_index]
                + jnp.einsum(
                    "shqk,skhd->shqd", grad_scores, key_rows, preferred_element_type=jnp.float32
                )
                * head_scale
            )
        return tuple(results)

    return lax.cond(skipped, lambda: carried, query_update)


def key_grad_block(carried, block_in, first_row, keys_local, values_local, key_pos, seq_lengths):
    head_scale = HEAD ** (-0.5)
    query_count = block_in[0].shape[1]
    query_pos = jnp.arange(query_count, dtype=jnp.int32)
    allowed = (
        (key_pos[None, None, :] <= query_pos[None, :, None])
        & (key_pos[None, None, :] < seq_lengths[:, None, None])
    )[:, None]
    skipped = (first_row + query_count - 1 < key_pos[0]) | (key_pos[0] >= jnp.max(seq_lengths))

    def key_update():
        results = []
        for model_index in range(2):
            grad_keys, grad_values = carried[model_index]
            query_rows = split_heads(block_in[4 * model_index])
            grad_rows = split_heads(block_in[4 * model_index + 1])
            log_rows = jnp.transpose(block_in[4 * model_index + 2], (0, 2, 1))
            delta_rows = jnp.transpose(block_in[4 * model_index + 3], (0, 2, 1))
            scores = (
                jnp.einsum(
                    "sqhd,skhd->shqk",
                    query_rows,
                    keys_local[model_index],
                    preferred_element_type=jnp.float32,
                )
                * head_scale
            )
            prob_rows = jnp.where(allowed, jnp.exp(scores - log_rows[..., None]), 0.0)
            grad_values = grad_values + jnp.einsum(
                "shqk,sqhd->shkd",
                prob_rows.astype(jnp.bfloat16),
                grad_rows,
                preferred_element_type=jnp.float32,
            )
            grad_prob = jnp.einsum(
                "sqhd,skhd->shqk",
                grad_rows,
                values_local[model_index],
                preferred_element_type=jnp.float32,
            )
            grad_scores = (prob_rows * (grad_prob - delta_rows[..., None])).astype(jnp.bfloat16)
            grad_keys = (
                grad_keys
                + jnp.einsum(
                    "shqk,sqhd->shkd", grad_scores, query_rows, preferred_element_type=jnp.float32
                )
                * head_scale
            )
            results.append((grad_keys, grad_values))
        return tuple(results)

    return lax.cond(skipped, lambda: carried, key_update)


def shards(
    hidden,
    lengths,
    student_first_gain,
    student_first_shift,
    student_attend_weight,
    student_attend_bias,
    student_output_weight,
    student_output_bias,
    student_second_gain,
    student_second_shift,
    student_expand_weight,
    student_expand_bias,
    student_reduce_weight,
    student_reduce_bias,
    teacher_first_gain,
    teacher_first_shift,
    teacher_attend_weight,
    teacher_attend_bias,
    teacher_output_weight,
    teacher_output_bias,
    teacher_second_gain,
    teacher_second_shift,
    teacher_expand_weight,
    teacher_expand_bias,
    teacher_reduce_weight,
    teacher_reduce_bias,
    final_gain,
    final_shift,
    embedding,
):
    gathered = (
        lax.all_gather(student_first_gain, EVERY, axis=0, tiled=True),
        lax.all_gather(student_first_shift, EVERY, axis=0, tiled=True),
        lax.all_gather(student_attend_weight, EVERY, axis=0, tiled=True),
        lax.all_gather(student_attend_bias, EVERY, axis=0, tiled=True),
        lax.all_gather(student_output_weight, EVERY, axis=0, tiled=True),
        lax.all_gather(student_output_bias, EVERY, axis=0, tiled=True),
        lax.all_gather(student_second_gain, EVERY, axis=0, tiled=True),
        lax.all_gather(student_second_shift, EVERY, axis=0, tiled=True),
        lax.all_gather(student_expand_weight, EVERY, axis=0, tiled=True),
        lax.all_gather(student_expand_bias, EVERY, axis=0, tiled=True),
        lax.all_gather(student_reduce_weight, EVERY, axis=0, tiled=True),
        lax.all_gather(student_reduce_bias, EVERY, axis=0, tiled=True),
        lax.all_gather(teacher_first_gain, EVERY, axis=0, tiled=True),
        lax.all_gather(teacher_first_shift, EVERY, axis=0, tiled=True),
        lax.all_gather(teacher_attend_weight, EVERY, axis=0, tiled=True),
        lax.all_gather(teacher_attend_bias, EVERY, axis=0, tiled=True),
        lax.all_gather(teacher_output_weight, EVERY, axis=0, tiled=True),
        lax.all_gather(teacher_output_bias, EVERY, axis=0, tiled=True),
        lax.all_gather(teacher_second_gain, EVERY, axis=0, tiled=True),
        lax.all_gather(teacher_second_shift, EVERY, axis=0, tiled=True),
        lax.all_gather(teacher_expand_weight, EVERY, axis=0, tiled=True),
        lax.all_gather(teacher_expand_bias, EVERY, axis=0, tiled=True),
        lax.all_gather(teacher_reduce_weight, EVERY, axis=0, tiled=True),
        lax.all_gather(teacher_reduce_bias, EVERY, axis=0, tiled=True),
    )
    models = (tuple(gathered[:12]), tuple(gathered[12:]))
    batch_seqs, rows_local, model_width = hidden.shape
    row_count = batch_seqs * rows_local
    inputs = hidden.astype(jnp.float32)
    inputs_flat = inputs.reshape(row_count, model_width)
    query_pos = lax.axis_index(BLK) * rows_local + jnp.arange(rows_local, dtype=jnp.int32)
    fronts = [front_half(inputs, params) for params in models]
    queries = (split_heads(fronts[0][1]), split_heads(fronts[1][1]))
    zero_heads = jnp.zeros((batch_seqs, HEADS, rows_local, HEAD), jnp.float32)
    zero_rows = jnp.zeros((batch_seqs, HEADS, rows_local), jnp.float32)
    start_state = (
        zero_heads,
        jnp.full((batch_seqs, HEADS, rows_local), -1e30, jnp.float32),
        zero_rows,
    )
    folded = attend_block(
        (start_state, start_state),
        (
            lax.all_gather(fronts[0][2], BLK, axis=1, tiled=True),
            lax.all_gather(fronts[0][3], BLK, axis=1, tiled=True),
            lax.all_gather(fronts[1][2], BLK, axis=1, tiled=True),
            lax.all_gather(fronts[1][3], BLK, axis=1, tiled=True),
        ),
        jnp.int32(0),
        queries,
        query_pos,
        lengths,
    )
    gain_final = final_gain.astype(jnp.float32)
    shift_final = final_shift.astype(jnp.float32)
    caches = []
    final_rows = []
    for model_index in range(2):
        params = models[model_index]
        running, row_max, row_total = folded[model_index]
        mixed_rows = (
            jnp.transpose(running / row_total[..., None], (0, 2, 1, 3))
            .reshape(row_count, model_width)
            .astype(jnp.bfloat16)
        )
        log_total = row_max + jnp.log(row_total)
        middle = inputs_flat + matmul_plain(mixed_rows, params[4]) + params[5].astype(jnp.float32)
        normed_two = layer_norm(
            middle, params[6].astype(jnp.float32), params[7].astype(jnp.float32)
        ).astype(jnp.bfloat16)
        inner_rows = matmul_plain(normed_two, params[8]) + params[9].astype(jnp.float32)
        active = gelu_tanh(inner_rows).astype(jnp.bfloat16)
        block_out = middle + matmul_plain(active, params[10]) + params[11].astype(jnp.float32)
        final_rows.append(layer_norm(block_out, gain_final, shift_final).astype(jnp.bfloat16))
        caches.append((mixed_rows, log_total, middle, normed_two, inner_rows, active, block_out))
    all_rows = lax.all_gather(jnp.stack(final_rows), VOCAB, axis=1, tiled=True)
    vocab_local = embedding.shape[0]
    vocab_index = lax.axis_index(VOCAB)
    column_valid = (
        vocab_index * vocab_local + jnp.arange(vocab_local, dtype=jnp.int32) < VOCAB_REAL
    )[None, :]
    total_rows = all_rows.shape[1]

    def scaled_logits(rows_pair):
        scaled_student = jnp.where(
            column_valid, matmul_right_t(rows_pair[0], embedding) * 0.5, -1e30
        )
        scaled_teacher = jnp.where(
            column_valid, matmul_right_t(rows_pair[1], embedding) * 0.5, -1e30
        )
        return (scaled_student, scaled_teacher)

    stat_rows = math.gcd(total_rows, 512)

    def local_stats(block_index):
        rows_pair = lax.dynamic_slice_in_dim(all_rows, block_index * stat_rows, stat_rows, 1)
        scaled_student, scaled_teacher = scaled_logits(rows_pair)
        max_student = jnp.max(scaled_student, axis=-1)
        max_teacher = jnp.max(scaled_teacher, axis=-1)
        exp_student = jnp.where(column_valid, jnp.exp(scaled_student - max_student[:, None]), 0.0)
        exp_teacher = jnp.where(column_valid, jnp.exp(scaled_teacher - max_teacher[:, None]), 0.0)
        cross_sum = jnp.sum(exp_teacher * (scaled_teacher - scaled_student), axis=-1)
        return (
            max_student,
            jnp.sum(exp_student, axis=-1),
            max_teacher,
            jnp.sum(exp_teacher, axis=-1),
            cross_sum,
        )

    stat_blocks = lax.map(local_stats, jnp.arange(total_rows // stat_rows))
    max_student, sum_student, max_teacher, sum_teacher, cross_sum = [
        stat_block.reshape(total_rows) for stat_block in stat_blocks
    ]
    top_student, top_teacher = lax.pmax((max_student, max_teacher), VOCAB)
    factor_student = jnp.exp(max_student - top_student)
    factor_teacher = jnp.exp(max_teacher - top_teacher)
    sum_student, sum_teacher, cross_sum = lax.psum(
        (sum_student * factor_student, sum_teacher * factor_teacher, cross_sum * factor_teacher),
        VOCAB,
    )
    max_student, max_teacher = (top_student, top_teacher)
    lse_student = max_student + jnp.log(sum_student)
    lse_teacher = max_teacher + jnp.log(sum_teacher)
    divergence_rows = cross_sum / sum_teacher - lse_teacher + lse_student
    valid_rows = (query_pos[None, :] < lengths[:, None]).astype(jnp.float32)
    own_start = vocab_index * row_count
    kl_out = (
        4.0
        * lax.dynamic_slice_in_dim(divergence_rows, own_start, row_count).reshape(
            batch_seqs, rows_local
        )
        * valid_rows
    )
    step_rows = math.gcd(row_count * lax.axis_size(VOCAB), 512)

    def one_block(block_index):
        begin = block_index * step_rows
        rows_pair = lax.dynamic_slice_in_dim(all_rows, begin, step_rows, 1)
        scaled_student, scaled_teacher = scaled_logits(rows_pair)
        log_student = (
            scaled_student - lax.dynamic_slice_in_dim(lse_student, begin, step_rows)[:, None]
        )
        log_teacher = (
            scaled_teacher - lax.dynamic_slice_in_dim(lse_teacher, begin, step_rows)[:, None]
        )
        row_kl = lax.dynamic_slice_in_dim(divergence_rows, begin, step_rows)[:, None]
        prob_student = jnp.where(column_valid, jnp.exp(log_student), 0.0)
        prob_teacher = jnp.where(column_valid, jnp.exp(log_teacher), 0.0)
        grad_student = (2.0 * (prob_student - prob_teacher)).astype(jnp.bfloat16)
        grad_teacher = (2.0 * prob_teacher * (log_teacher - log_student - row_kl)).astype(
            jnp.bfloat16
        )
        return jnp.concatenate(
            [matmul_plain(grad_student, embedding), matmul_plain(grad_teacher, embedding)], axis=1
        )

    grad_final = (
        lax.psum_scatter(
            lax.map(one_block, jnp.arange(row_count * lax.axis_size(VOCAB) // step_rows))
            .reshape(row_count * lax.axis_size(VOCAB), 2 * model_width)
            .astype(jnp.bfloat16),
            VOCAB,
            scatter_dimension=0,
            tiled=True,
        ).astype(jnp.float32)
        * valid_rows.reshape(row_count)[:, None]
    )
    regathered = (
        lax.all_gather(student_first_gain, EVERY, axis=0, tiled=True),
        lax.all_gather(student_first_shift, EVERY, axis=0, tiled=True),
        lax.all_gather(student_attend_weight, EVERY, axis=0, tiled=True),
        lax.all_gather(student_attend_bias, EVERY, axis=0, tiled=True),
        lax.all_gather(student_output_weight, EVERY, axis=0, tiled=True),
        lax.all_gather(student_output_bias, EVERY, axis=0, tiled=True),
        lax.all_gather(student_second_gain, EVERY, axis=0, tiled=True),
        lax.all_gather(student_second_shift, EVERY, axis=0, tiled=True),
        lax.all_gather(student_expand_weight, EVERY, axis=0, tiled=True),
        lax.all_gather(student_expand_bias, EVERY, axis=0, tiled=True),
        lax.all_gather(student_reduce_weight, EVERY, axis=0, tiled=True),
        lax.all_gather(student_reduce_bias, EVERY, axis=0, tiled=True),
        lax.all_gather(teacher_first_gain, EVERY, axis=0, tiled=True),
        lax.all_gather(teacher_first_shift, EVERY, axis=0, tiled=True),
        lax.all_gather(teacher_attend_weight, EVERY, axis=0, tiled=True),
        lax.all_gather(teacher_attend_bias, EVERY, axis=0, tiled=True),
        lax.all_gather(teacher_output_weight, EVERY, axis=0, tiled=True),
        lax.all_gather(teacher_output_bias, EVERY, axis=0, tiled=True),
        lax.all_gather(teacher_second_gain, EVERY, axis=0, tiled=True),
        lax.all_gather(teacher_second_shift, EVERY, axis=0, tiled=True),
        lax.all_gather(teacher_expand_weight, EVERY, axis=0, tiled=True),
        lax.all_gather(teacher_expand_bias, EVERY, axis=0, tiled=True),
        lax.all_gather(teacher_reduce_weight, EVERY, axis=0, tiled=True),
        lax.all_gather(teacher_reduce_bias, EVERY, axis=0, tiled=True),
    )
    back_models = (tuple(regathered[:12]), tuple(regathered[12:]))
    uppers = []
    middle_pairs = []
    for model_index in range(2):
        params = back_models[model_index]
        mixed_rows, log_total, middle, normed_two, inner_rows, active, block_out = caches[
            model_index
        ]
        _, final_pull = jax.vjp(
            lambda rows_in: layer_norm(rows_in, gain_final, shift_final), block_out
        )
        grad_out = final_pull(
            grad_final[:, model_index * model_width : (model_index + 1) * model_width]
        )[0]
        branch_low = grad_out.astype(jnp.bfloat16)
        grad_reduce_bias = column_sums(branch_low)
        grad_active = matmul_right_t(branch_low, params[10])
        _, gelu_pull = jax.vjp(gelu_tanh, inner_rows)
        inner_grad = gelu_pull(grad_active)[0].astype(jnp.bfloat16)
        grad_expand_bias = column_sums(inner_grad)
        grad_normed_two = matmul_right_t(inner_grad, params[8])
        _, second_pull = jax.vjp(
            layer_norm, middle, params[6].astype(jnp.float32), params[7].astype(jnp.float32)
        )
        middle_part, grad_second_gain, grad_second_shift = second_pull(grad_normed_two)
        grad_middle = grad_out + middle_part
        attn_low = grad_middle.astype(jnp.bfloat16)
        grad_output_bias = column_sums(attn_low)
        grad_mixed = matmul_right_t(attn_low, params[4]).astype(jnp.bfloat16)
        delta_rows = jnp.sum(
            (grad_mixed.astype(jnp.float32) * mixed_rows.astype(jnp.float32)).reshape(
                batch_seqs, rows_local, HEADS, HEAD
            ),
            axis=-1,
        )
        uppers.append(
            (
                grad_output_bias,
                grad_second_gain,
                grad_second_shift,
                grad_expand_bias,
                grad_reduce_bias,
                grad_middle,
                grad_mixed.reshape(batch_seqs, rows_local, model_width),
                delta_rows,
            )
        )
        middle_pairs.append(
            ((mixed_rows, attn_low), (normed_two, inner_grad), (active, branch_low))
        )
    grads_heads = (split_heads(uppers[0][6]), split_heads(uppers[1][6]))
    log_totals = (caches[0][1], caches[1][1])
    deltas = (jnp.transpose(uppers[0][7], (0, 2, 1)), jnp.transpose(uppers[1][7], (0, 2, 1)))
    query_grads = query_grad_block(
        (zero_heads, zero_heads),
        (
            lax.all_gather(fronts[0][2], BLK, axis=1, tiled=True),
            lax.all_gather(fronts[0][3], BLK, axis=1, tiled=True),
            lax.all_gather(fronts[1][2], BLK, axis=1, tiled=True),
            lax.all_gather(fronts[1][3], BLK, axis=1, tiled=True),
        ),
        jnp.int32(0),
        queries,
        grads_heads,
        log_totals,
        deltas,
        query_pos,
        lengths,
    )
    keys_local = (split_heads(fronts[0][2]), split_heads(fronts[1][2]))
    values_local = (split_heads(fronts[0][3]), split_heads(fronts[1][3]))
    key_grads = key_grad_block(
        ((zero_heads, zero_heads), (zero_heads, zero_heads)),
        (
            lax.all_gather(fronts[0][1], BLK, axis=1, tiled=True),
            lax.all_gather(uppers[0][6], BLK, axis=1, tiled=True),
            lax.all_gather(
                for_sending(jnp.transpose(log_totals[0], (0, 2, 1))), BLK, axis=1, tiled=True
            ),
            lax.all_gather(uppers[0][7].astype(jnp.bfloat16), BLK, axis=1, tiled=True).astype(
                jnp.float32
            ),
            lax.all_gather(fronts[1][1], BLK, axis=1, tiled=True),
            lax.all_gather(uppers[1][6], BLK, axis=1, tiled=True),
            lax.all_gather(
                for_sending(jnp.transpose(log_totals[1], (0, 2, 1))), BLK, axis=1, tiled=True
            ),
            lax.all_gather(uppers[1][7].astype(jnp.bfloat16), BLK, axis=1, tiled=True).astype(
                jnp.float32
            ),
        ),
        jnp.int32(0),
        keys_local,
        values_local,
        query_pos,
        lengths,
    )
    vectors = []
    pairs = []
    input_grad = jnp.zeros((row_count, model_width), jnp.float32)
    for model_index in range(2):
        params = back_models[model_index]
        upper = uppers[model_index]
        grad_keys, grad_values = key_grads[model_index]
        joined_grad = jnp.concatenate(
            [
                jnp.transpose(query_grads[model_index], (0, 2, 1, 3)).reshape(
                    row_count, model_width
                ),
                jnp.transpose(grad_keys, (0, 2, 1, 3)).reshape(row_count, model_width),
                jnp.transpose(grad_values, (0, 2, 1, 3)).reshape(row_count, model_width),
            ],
            axis=1,
        ).astype(jnp.bfloat16)
        bias_sums = column_sums(joined_grad)
        grad_attend_bias = jnp.concatenate([bias_sums[:model_width], bias_sums[2 * model_width :]])
        grad_normed_one = matmul_right_t(joined_grad, params[2])
        _, first_pull = jax.vjp(
            layer_norm, inputs_flat, params[0].astype(jnp.float32), params[1].astype(jnp.float32)
        )
        input_part, grad_first_gain, grad_first_shift = first_pull(grad_normed_one)
        input_grad = input_grad + upper[5] + input_part
        vectors.append(
            [
                grad_first_gain,
                grad_first_shift,
                grad_attend_bias,
                upper[0],
                upper[1],
                upper[2],
                upper[3],
                upper[4],
            ]
        )
        pairs.append(
            [
                (fronts[model_index][0], joined_grad),
                middle_pairs[model_index][0],
                middle_pairs[model_index][1],
                middle_pairs[model_index][2],
            ]
        )
    grads = []
    for model_index in range(2):
        matrix_list = [matmul_left_t(pair[0], pair[1]) for pair in pairs[model_index]]
        vector_list = vectors[model_index]
        grads.extend(
            [
                vector_list[0],
                vector_list[1],
                matrix_list[0],
                vector_list[2],
                matrix_list[1],
                vector_list[3],
                vector_list[4],
                vector_list[5],
                matrix_list[2],
                vector_list[6],
                matrix_list[3],
                vector_list[7],
            ]
        )
    summed = (
        lax.psum_scatter(grads[0], EVERY, scatter_dimension=0, tiled=True),
        lax.psum_scatter(grads[1], EVERY, scatter_dimension=0, tiled=True),
        lax.psum_scatter(grads[2], EVERY, scatter_dimension=0, tiled=True),
        lax.psum_scatter(grads[3], EVERY, scatter_dimension=0, tiled=True),
        lax.psum_scatter(grads[4], EVERY, scatter_dimension=0, tiled=True),
        lax.psum_scatter(grads[5], EVERY, scatter_dimension=0, tiled=True),
        lax.psum_scatter(grads[6], EVERY, scatter_dimension=0, tiled=True),
        lax.psum_scatter(grads[7], EVERY, scatter_dimension=0, tiled=True),
        lax.psum_scatter(grads[8], EVERY, scatter_dimension=0, tiled=True),
        lax.psum_scatter(grads[9], EVERY, scatter_dimension=0, tiled=True),
        lax.psum_scatter(grads[10], EVERY, scatter_dimension=0, tiled=True),
        lax.psum_scatter(grads[11], EVERY, scatter_dimension=0, tiled=True),
        lax.psum_scatter(grads[12], EVERY, scatter_dimension=0, tiled=True),
        lax.psum_scatter(grads[13], EVERY, scatter_dimension=0, tiled=True),
        lax.psum_scatter(grads[14], EVERY, scatter_dimension=0, tiled=True),
        lax.psum_scatter(grads[15], EVERY, scatter_dimension=0, tiled=True),
        lax.psum_scatter(grads[16], EVERY, scatter_dimension=0, tiled=True),
        lax.psum_scatter(grads[17], EVERY, scatter_dimension=0, tiled=True),
        lax.psum_scatter(grads[18], EVERY, scatter_dimension=0, tiled=True),
        lax.psum_scatter(grads[19], EVERY, scatter_dimension=0, tiled=True),
        lax.psum_scatter(grads[20], EVERY, scatter_dimension=0, tiled=True),
        lax.psum_scatter(grads[21], EVERY, scatter_dimension=0, tiled=True),
        lax.psum_scatter(grads[22], EVERY, scatter_dimension=0, tiled=True),
        lax.psum_scatter(grads[23], EVERY, scatter_dimension=0, tiled=True),
    )
    return tuple(summed) + (input_grad.reshape(batch_seqs, rows_local, model_width), kl_out)


LANES = 128
MARGIN = 16.0
VMEM_BYTES = 60 * 1024 * 1024


def lane_fold(tile_in, combine):
    folded = tile_in[:, :LANES]
    for start in range(LANES, tile_in.shape[1], LANES):
        folded = combine(folded, tile_in[:, start : start + LANES])
    return folded


def whole_block(shape):
    return pl.BlockSpec(shape, lambda *_: (0,) * len(shape))


def vocab_stats_kernel(
    scalars_ref,
    student_low_ref,
    student_high_ref,
    teacher_low_ref,
    teacher_high_ref,
    embed_ref,
    logit_student_ref,
    logit_teacher_ref,
    stats_ref,
    tile_max_s,
    tile_max_t,
    max_s,
    max_t,
    sum_s,
    sum_t,
    cross,
    part_s,
    part_t,
    part_x,
    *,
    tile,
    rows_block,
):
    step_index = pl.program_id(0)
    steps = pl.num_programs(0)
    half_rows = student_low_ref.shape[1]
    rows = 2 * half_rows

    @pl.when(step_index == 0)
    def _():
        max_s[...] = jnp.full_like(max_s, -1e30)
        max_t[...] = jnp.full_like(max_t, -1e30)
        for total in (sum_s, sum_t, cross):
            total[...] = jnp.zeros_like(total)

    def sums(scaled_s, scaled_t, top_s, top_t):
        shifted_s = scaled_s - top_s
        shifted_t = scaled_t - top_t
        exp_s = jnp.exp(shifted_s)
        exp_t = jnp.exp(shifted_t)
        return (
            lane_fold(exp_s, jnp.add),
            lane_fold(exp_t, jnp.add),
            lane_fold(exp_t * (shifted_t - shifted_s), jnp.add),
        )

    def one_tile(masked):
        embed_tile = embed_ref[...]
        excess = None
        for start in range(0, rows, rows_block):
            here = pl.ds(start, rows_block)
            source = pl.ds(start % half_rows, rows_block)
            student_ref = student_low_ref if start < half_rows else student_high_ref
            teacher_ref = teacher_low_ref if start < half_rows else teacher_high_ref
            scaled_s = matmul_right_t(student_ref[0, source, :], embed_tile)
            scaled_t = matmul_right_t(teacher_ref[0, source, :], embed_tile)
            if masked:
                column = lax.broadcasted_iota(jnp.int32, (1, tile), 1) + step_index * tile
                scaled_s = jnp.where(column < scalars_ref[0], scaled_s, -1e30)
                scaled_t = jnp.where(column < scalars_ref[0], scaled_t, -1e30)
            logit_student_ref[here, :] = scaled_s
            logit_teacher_ref[here, :] = scaled_t
            tops_s = lane_fold(scaled_s, jnp.maximum)
            tops_t = lane_fold(scaled_t, jnp.maximum)
            tile_max_s[here, :] = tops_s
            tile_max_t[here, :] = tops_t
            old_s = max_s[here, :]
            old_t = max_t[here, :]
            part_s[here, :], part_t[here, :], part_x[here, :] = sums(
                scaled_s, scaled_t, old_s[:, :1], old_t[:, :1]
            )
            over = jnp.maximum(tops_s - old_s, tops_t - old_t)
            excess = over if excess is None else jnp.maximum(excess, over)

        @pl.when(jnp.max(excess) > MARGIN)
        def _():
            def rescale(chunk, _):
                here = pl.ds(pl.multiple_of(chunk * 64, 64), 64)
                old_s = max_s[here, :]
                old_t = max_t[here, :]
                new_s = jnp.maximum(old_s, jnp.max(tile_max_s[here, :], axis=1, keepdims=True))
                new_t = jnp.maximum(old_t, jnp.max(tile_max_t[here, :], axis=1, keepdims=True))
                factor_t = jnp.exp(old_t - new_t)
                moved = (old_t - old_s) - (new_t - new_s)
                max_s[here, :] = new_s
                max_t[here, :] = new_t
                sum_s[here, :] = sum_s[here, :] * jnp.exp(old_s - new_s)
                cross[here, :] = (cross[here, :] + moved * sum_t[here, :]) * factor_t
                sum_t[here, :] = sum_t[here, :] * factor_t
                part_s[here, :], part_t[here, :], part_x[here, :] = sums(
                    logit_student_ref[here, :],
                    logit_teacher_ref[here, :],
                    new_s[:, :1],
                    new_t[:, :1],
                )
                return 0

            lax.fori_loop(0, rows // 64, rescale, 0)

        sum_s[...] += part_s[...]
        sum_t[...] += part_t[...]
        cross[...] += part_x[...]

    @pl.when(step_index < steps - 1)
    def _():
        one_tile(False)

    @pl.when(step_index == steps - 1)
    def _():
        one_tile(True)
        lane = lax.broadcasted_iota(jnp.int32, (rows, LANES), 1)
        result = jnp.sum(cross[...], axis=1, keepdims=True)
        result = jnp.where(lane == 3, jnp.sum(sum_t[...], axis=1, keepdims=True), result)
        result = jnp.where(lane == 2, jnp.sum(sum_s[...], axis=1, keepdims=True), result)
        result = jnp.where(lane == 0, max_s[...], jnp.where(lane == 1, max_t[...], result))
        stats_ref[...] = result.T[:8, :]


def vocab_stats(final_parts, is_teacher, embedding, valid_columns, tile=1280, rows_block=256):
    _, half_rows, width = final_parts.shape
    rows = 2 * half_rows
    steps = pl.cdiv(embedding.shape[0], tile)
    logits = jax.ShapeDtypeStruct((rows, steps * tile), jnp.float32)
    part_spec = lambda teacher, second: pl.BlockSpec(
        (1, half_rows, width),
        lambda j, scalars: (2 * (scalars[1] ^ teacher) + second, 0, 0),
    )
    return pl.pallas_call(
        functools.partial(vocab_stats_kernel, tile=tile, rows_block=rows_block),
        grid_spec=pltpu.PrefetchScalarGridSpec(
            num_scalar_prefetch=1,
            grid=(steps,),
            in_specs=[part_spec(0, 0), part_spec(0, 1), part_spec(1, 0), part_spec(1, 1)]
            + [pl.BlockSpec((tile, width), lambda j, *_: (j, 0))],
            out_specs=[
                pl.BlockSpec((rows, tile), lambda j, *_: (0, j)),
                pl.BlockSpec((rows, tile), lambda j, *_: (0, j)),
                whole_block((8, rows)),
            ],
            scratch_shapes=[pltpu.VMEM((rows, LANES), jnp.float32)] * 10,
        ),
        out_shape=[logits, logits, jax.ShapeDtypeStruct((8, rows), jnp.float32)],
        compiler_params=pltpu.CompilerParams(vmem_limit_bytes=VMEM_BYTES),
        name="vocab_stats",
    )(
        jnp.stack([valid_columns, is_teacher.astype(jnp.int32)]),
        *[final_parts] * 4,
        embedding,
    )


def vocab_grads_kernel(
    logit_student_ref,
    logit_teacher_ref,
    embed_ref,
    *refs,
    tile,
    columns,
    rows_block,
    count,
):
    stat_refs = refs[:count]
    own_ref, send_ref, divergence_ref, row_ref, student_ref, teacher_ref = refs[count:]
    step_index = pl.program_id(0)
    rows = student_ref.shape[0]
    half_rows = rows // 2

    @pl.when(step_index == 0)
    def _():
        student_ref[...] = jnp.zeros_like(student_ref)
        teacher_ref[...] = jnp.zeros_like(teacher_ref)
        parts = []
        for index in range(count):
            part = stat_refs[index][...]
            if index % 2:
                part = jnp.concatenate([part[:, half_rows:], part[:, :half_rows]], axis=1)
            parts.append([part[k : k + 1, :] for k in range(5)])
        top_s = functools.reduce(jnp.maximum, [p[0] for p in parts])
        top_t = functools.reduce(jnp.maximum, [p[1] for p in parts])
        sum_s = sum(p[2] * jnp.exp(p[0] - top_s) for p in parts)
        sum_t = sum(p[3] * jnp.exp(p[1] - top_t) for p in parts)
        cross = sum((p[4] + (p[1] - p[0]) * p[3]) * jnp.exp(p[1] - top_t) for p in parts)
        lse_s = top_s + jnp.log(sum_s)
        lse_t = top_t + jnp.log(sum_t)
        mean_gap = cross / sum_t
        divergence_ref[...] = jnp.broadcast_to(mean_gap - lse_t + lse_s, divergence_ref.shape)
        line = lax.broadcasted_iota(jnp.int32, (LANES, rows), 0)
        row_ref[...] = jnp.where(line == 0, lse_s, jnp.where(line == 1, lse_t, mean_gap)).T

    def one_tile(masked):
        embed_tile = embed_ref[...]
        if masked:
            row = lax.broadcasted_iota(jnp.int32, (tile, 1), 0) + step_index * tile
            embed_tile = jnp.where(row < columns, embed_tile, jnp.zeros_like(embed_tile))
        for start in range(0, rows, rows_block):
            here = pl.ds(start, rows_block)
            scaled_s = logit_student_ref[here, :]
            scaled_t = logit_teacher_ref[here, :]
            prob_s = jnp.exp(scaled_s - row_ref[here, 0:1])
            prob_t = jnp.exp(scaled_t - row_ref[here, 1:2])
            grad_s = (prob_s - prob_t).astype(jnp.bfloat16)
            grad_t = (prob_t * ((scaled_t - scaled_s) - row_ref[here, 2:3])).astype(jnp.bfloat16)
            student_ref[here, :] += matmul_plain(grad_s, embed_tile)
            teacher_ref[here, :] += matmul_plain(grad_t, embed_tile)

    last = pl.num_programs(0) - 1

    @pl.when(step_index < last)
    def _():
        one_tile(False)

    @pl.when(step_index == last)
    def _():
        one_tile(True)
        for index, sums in enumerate((student_ref, teacher_ref)):
            own_ref[index] = sums[:half_rows, :]
            send_ref[index] = sums[half_rows:, :].astype(jnp.bfloat16)


def vocab_grads(logit_student, logit_teacher, embedding, stat_parts, tile=1280, rows_block=256):
    rows = logit_student.shape[0]
    columns, width = embedding.shape
    halves = (2, rows // 2, width)
    return pl.pallas_call(
        functools.partial(
            vocab_grads_kernel,
            tile=tile,
            columns=columns,
            rows_block=rows_block,
            count=len(stat_parts),
        ),
        grid=(pl.cdiv(columns, tile),),
        in_specs=[
            pl.BlockSpec((rows, tile), lambda j: (0, j)),
            pl.BlockSpec((rows, tile), lambda j: (0, j)),
            pl.BlockSpec((tile, width), lambda j: (j, 0)),
        ]
        + [whole_block((8, rows))] * len(stat_parts),
        out_specs=[whole_block(halves), whole_block(halves), whole_block((8, rows))],
        out_shape=[
            jax.ShapeDtypeStruct(halves, jnp.float32),
            jax.ShapeDtypeStruct(halves, jnp.bfloat16),
            jax.ShapeDtypeStruct((8, rows), jnp.float32),
        ],
        scratch_shapes=[
            pltpu.VMEM((rows, LANES), jnp.float32),
            pltpu.VMEM((rows, width), jnp.float32),
            pltpu.VMEM((rows, width), jnp.float32),
        ],
        compiler_params=pltpu.CompilerParams(vmem_limit_bytes=VMEM_BYTES),
        name="vocab_grads",
    )(logit_student, logit_teacher, embedding, *stat_parts)


def attend_kernel(length_ref, query_ref, key_ref, value_ref, mixed_ref, *, block):
    rows = query_ref.shape[0]
    lane = lax.broadcasted_iota(jnp.int32, (1, LANES), 1)
    for start in range(0, rows, block):
        keys = start + block
        key_pos = lax.broadcasted_iota(jnp.int32, (block, keys), 1)
        query_pos = lax.broadcasted_iota(jnp.int32, (block, keys), 0) + start
        allowed = (key_pos <= query_pos) & (key_pos < length_ref[0])
        outs = []
        for head in range(LANES // HEAD):
            own = (lane // HEAD) == head
            queries = query_ref[start : start + block, :] * HEAD**-0.5
            queries = jnp.where(own, queries, jnp.zeros_like(queries))
            scores = matmul_right_t(queries, key_ref[:keys, :])
            scores = jnp.where(allowed, scores, -1e30)
            weights = jnp.exp(scores - jnp.max(scores, axis=1, keepdims=True))
            total = jnp.sum(weights, axis=1, keepdims=True)
            outs.append(
                matmul_plain(weights.astype(jnp.bfloat16), value_ref[:keys, :]) / total
            )
        mixed_ref[start : start + block, :] = jnp.where(lane < HEAD, outs[0], outs[1]).astype(
            jnp.bfloat16
        )


def attend_rows(joined, seq_length, block):
    rows, width = joined.shape
    third = width // 3
    pairs = third // LANES
    spec = lambda part: pl.BlockSpec((rows, LANES), lambda p, *_: (0, part * pairs + p))
    return pl.pallas_call(
        functools.partial(attend_kernel, block=block),
        grid_spec=pltpu.PrefetchScalarGridSpec(
            num_scalar_prefetch=1,
            grid=(pairs,),
            in_specs=[spec(0), spec(1), spec(2)],
            out_specs=spec(0),
        ),
        out_shape=jax.ShapeDtypeStruct((rows, third), jnp.bfloat16),
        compiler_params=pltpu.CompilerParams(vmem_limit_bytes=VMEM_BYTES),
        name="attend",
    )(seq_length.reshape(1), joined, joined, joined)


def attend_grads_kernel(
    length_ref,
    query_ref,
    key_ref,
    value_ref,
    grad_ref,
    grad_query_ref,
    grad_key_ref,
    grad_value_ref,
    sum_key,
    sum_value,
    *,
    block,
):
    rows = query_ref.shape[0]
    lane = lax.broadcasted_iota(jnp.int32, (1, LANES), 1)
    sum_key[...] = jnp.zeros_like(sum_key)
    sum_value[...] = jnp.zeros_like(sum_value)
    keys_turned = key_ref[...].T
    for start in range(0, rows, block):
        keys = start + block
        key_pos = lax.broadcasted_iota(jnp.int32, (keys, block), 0)
        query_pos = lax.broadcasted_iota(jnp.int32, (keys, block), 1) + start
        allowed = (key_pos <= query_pos) & (key_pos < length_ref[0])
        outs = []
        for head in range(LANES // HEAD):
            own = (lane // HEAD) == head
            queries = query_ref[start : start + block, :] * HEAD**-0.5
            queries = jnp.where(own, queries, jnp.zeros_like(queries))
            grads = grad_ref[start : start + block, :]
            grads = jnp.where(own, grads, jnp.zeros_like(grads))
            scores = matmul_right_t(key_ref[:keys, :], queries)
            scores = jnp.where(allowed, scores, -1e30)
            weights = jnp.exp(scores - jnp.max(scores, axis=0, keepdims=True))
            soft = weights * (1.0 / jnp.sum(weights, axis=0, keepdims=True))
            grad_soft = matmul_right_t(value_ref[:keys, :], grads)
            soft_grad = soft * grad_soft
            delta = jnp.sum(soft_grad, axis=0, keepdims=True)
            grad_scores = (soft_grad - soft * delta).astype(jnp.bfloat16)
            sum_value[:keys, :] += matmul_plain(soft.astype(jnp.bfloat16), grads)
            sum_key[:keys, :] += matmul_plain(grad_scores, queries)
            outs.append(matmul_plain(keys_turned[:, :keys], grad_scores))
        head_row = lax.broadcasted_iota(jnp.int32, (LANES, 1), 0)
        turned = jnp.where(head_row < HEAD, outs[0], outs[1]) * HEAD**-0.5
        grad_query_ref[start : start + block, :] = turned.T.astype(jnp.bfloat16)
    grad_key_ref[...] = sum_key[...].astype(jnp.bfloat16)
    grad_value_ref[...] = sum_value[...].astype(jnp.bfloat16)


def attend_grads(joined, grad_mixed, seq_length, block):
    rows, width = joined.shape
    third = width // 3
    pairs = third // LANES
    spec = lambda part: pl.BlockSpec((rows, LANES), lambda p, *_: (0, part * pairs + p))
    out = jax.ShapeDtypeStruct((rows, third), jnp.bfloat16)
    return pl.pallas_call(
        functools.partial(attend_grads_kernel, block=block),
        grid_spec=pltpu.PrefetchScalarGridSpec(
            num_scalar_prefetch=1,
            grid=(pairs,),
            in_specs=[spec(0), spec(1), spec(2), spec(0)],
            out_specs=[spec(0)] * 3,
            scratch_shapes=[pltpu.VMEM((rows, LANES), jnp.float32)] * 2,
        ),
        out_shape=[out] * 3,
        compiler_params=pltpu.CompilerParams(vmem_limit_bytes=VMEM_BYTES),
        name="attend_grads",
    )(seq_length.reshape(1), joined, joined, joined, grad_mixed)


def place_kernel(own_ref, *refs, order, cuts):
    count = len(order)
    for block_ref, indices in zip(refs, order):
        height = block_ref.shape[0] // len(indices)
        for place, index in enumerate(indices):
            target = own_ref[0] ^ index
            for (first_row, rows, first_lane, lanes), out in zip(cuts, refs[count:]):
                first = place * height + first_row
                out[pl.ds(pl.multiple_of(target * rows, 16), rows), :] = block_ref[
                    first : first + rows, first_lane : first_lane + lanes
                ]


def place_blocks(gathered, own, cuts):
    gathered, order = gathered
    return pl.pallas_call(
        functools.partial(place_kernel, order=order, cuts=cuts),
        in_specs=[pl.BlockSpec(memory_space=pltpu.SMEM)]
        + [pl.BlockSpec(memory_space=pltpu.VMEM)] * len(order),
        out_specs=[pl.BlockSpec(memory_space=pltpu.VMEM)] * len(cuts),
        out_shape=[
            jax.ShapeDtypeStruct((8 * rows, lanes), jnp.bfloat16) for _, rows, _, lanes in cuts
        ],
        compiler_params=pltpu.CompilerParams(vmem_limit_bytes=VMEM_BYTES),
        name="place_blocks",
    )(own.reshape(1), *gathered)


def swap(rows, axis, distance):
    count = lax.axis_size(axis)
    return lax.ppermute(rows, axis, [(index, index ^ distance) for index in range(count)])


def in_pair(second, mine, other, axis=0):
    return jnp.where(
        second,
        jnp.concatenate([other, mine], axis=axis),
        jnp.concatenate([mine, other], axis=axis),
    )


def in_order(index, parts):
    low = (index & 1) == 1
    high = (index & 2) == 2
    pairs = [
        [jnp.where(low, parts[k + 1], parts[k]), jnp.where(low, parts[k], parts[k + 1])]
        for k in (0, 2)
    ]
    return [
        jnp.where(high, pairs[1][0], pairs[0][0]),
        jnp.where(high, pairs[1][1], pairs[0][1]),
        jnp.where(high, pairs[0][0], pairs[1][0]),
        jnp.where(high, pairs[0][1], pairs[1][1]),
    ]


def norm_back(inputs, gain_row, grad):
    centred = inputs - jnp.mean(inputs, axis=-1, keepdims=True)
    inverse = lax.rsqrt(jnp.mean(centred * centred, axis=-1, keepdims=True) + 1e-05)
    normal = centred * inverse
    scaled = grad * gain_row
    along = jnp.mean(scaled * normal, axis=-1, keepdims=True)
    result = inverse * (scaled - jnp.mean(scaled, axis=-1, keepdims=True) - normal * along)
    return result, jnp.sum(grad * normal, axis=0), jnp.sum(grad, axis=0)


def gelu_slope(inputs):
    root = math.sqrt(2.0 / math.pi)
    square = inputs * inputs
    bent = jnp.tanh(root * inputs * (1.0 + 0.044715 * square))
    return 0.5 * (1.0 + bent) + 0.5 * inputs * (1.0 - bent * bent) * root * (
        1.0 + 3 * 0.044715 * square
    )


def rows_of(array_in, start, count):
    return lax.dynamic_slice_in_dim(array_in, start, count, 0)


def columns_of(array_in, start, count):
    return lax.dynamic_slice_in_dim(array_in, start, count, 1)


def vector_lines_of(params, seq_length, width):
    short, middle, wide = [
        jnp.stack([jnp.stack([p[k] for k in numbers]) for p in params])
        for numbers in ((0, 1, 5, 6, 7, 11), (3,), (9,))
    ]
    lines = jnp.concatenate(
        [
            jnp.pad(group, ((0, 0), (0, 0), (0, LANES - group.shape[2])))
            for group in (short, middle, wide)
        ],
        axis=1,
    )
    length_parts = jnp.stack([seq_length // 32, seq_length % 32]).astype(jnp.bfloat16)
    length_parts = jnp.broadcast_to(length_parts, lines.shape[:2] + (2,))
    lines = jnp.concatenate([lines, length_parts], axis=2)
    return jnp.pad(lines, ((0, 0), (0, 0), (0, width - lines.shape[2])))


def pack_weights(params, half, lines):
    attend, output, expand, reduce = params[2], params[4], params[8], params[10]
    width = output.shape[1]
    part = width // 2
    wide = expand.shape[1] // 2
    begin = half * part
    front = jnp.concatenate(
        [attend[:, k * width + begin : k * width + begin + part] for k in range(3)], axis=1
    )
    return (
        jnp.concatenate([front, lines], axis=0),
        jnp.concatenate(
            [
                expand[:, start : start + part]
                for start in range(half * wide, (half + 1) * wide, part)
            ]
            + [output[:, begin : begin + part], reduce[:, begin : begin + part]],
            axis=0,
        ),
    )


def exchange_models(slabs):
    index = lax.axis_index(VOCAB)
    stacked = jnp.stack(slabs)
    parts = [lax.dynamic_index_in_dim(stacked, index, 0, keepdims=False)]
    for distance in (1, 2, 3):
        parts.append(
            swap(
                lax.dynamic_index_in_dim(stacked, index ^ distance, 0, keepdims=False),
                VOCAB,
                distance,
            )
        )
    return in_order(index, parts)


def after(value, *others):
    return lax.optimization_barrier((value, others))[0]


def held_after(held, *others):
    return after(held[0], *others), held[1]


def halves_of(axis_name, bit):
    distance = 1 << bit
    return distance, distance * (lax.axis_size(BATCH) if axis_name == BLK else 1)


def double(held, axis_name, bit):
    arrays, order = held
    distance, offset = halves_of(axis_name, bit)
    sent = jnp.concatenate(arrays, axis=0) if len(arrays) > 1 else arrays[0]
    sources = sum(order, ())
    return (
        arrays + (swap(sent, axis_name, distance),),
        order + (tuple(source ^ offset for source in sources),),
    )


def halve(addends, axis_name, bit):
    axis = 2 if axis_name == BATCH else 1 - bit
    own = (lax.axis_index(axis_name) >> bit) & 1
    mine = lax.dynamic_slice_in_dim(addends, own, 1, axis)
    theirs = lax.dynamic_slice_in_dim(addends, 1 - own, 1, axis)
    return mine.astype(jnp.float32) + swap(
        theirs.astype(jnp.bfloat16), axis_name, 1 << bit
    ).astype(jnp.float32)


def shards_by_model(hidden, lengths, *rest):
    embedding = rest[26]
    gain_final = rest[24].astype(jnp.float32)
    shift_final = rest[25].astype(jnp.float32)
    params = (rest[:12], rest[12:24])
    blk, batch, member = (lax.axis_index(name) for name in EVERY)
    size_blk, size_batch, size_vocab = (lax.axis_size(name) for name in EVERY)
    plane = blk * size_batch + batch
    model, half = member // 2, member % 2
    is_teacher, is_second = model == 1, half == 1
    rows_local, width = hidden.shape[1:]
    rows = rows_local * size_vocab
    own_rows = rows // 2
    part = width // 2
    ff_part = rest[8].shape[1] // 2
    shard_rows = rest[2].shape[0]
    plane_rows = shard_rows * size_vocab
    crossing = (BLK, VOCAB)

    turn = [
        (a * size_vocab + b, b * size_vocab + a) for a in range(size_blk) for b in range(size_vocab)
    ]
    quarter = lax.ppermute(hidden[0], crossing, turn)

    lines = vector_lines_of(params, lengths[0], 3 * part)
    front_slabs, back_slabs = zip(
        *[pack_weights(params[m], h, lines[m]) for m in (0, 1) for h in (0, 1)]
    )
    front = exchange_models(front_slabs)
    back = exchange_models(after(back_slabs, front))
    length_parts = sum(
        jnp.where(blk == source, front[source][shard_rows, LANES : LANES + 2], 0)
        for source in range(size_vocab)
    ).astype(jnp.int32)
    seq_length = 32 * length_parts[0] + length_parts[1]
    front_block = jnp.concatenate(
        [source[:shard_rows] for source in front] + [source[shard_rows:] for source in front],
        axis=0,
    )
    units = (ff_part + part) // part
    middle_block = jnp.concatenate(
        [
            jnp.concatenate(
                [source[k * shard_rows : (k + 1) * shard_rows] for source in back], axis=0
            )
            for k in range(units)
        ],
        axis=1,
    )
    reduce_block = jnp.concatenate([source[units * shard_rows :] for source in back], axis=0)
    vector_lines = front_block.shape[0] - plane_rows
    reduce_rows = reduce_block.shape[0]

    front_held = double(((after(front_block, quarter),), ((0,),)), BLK, 1)
    middle_held = double(((after(middle_block, front_held[0]),), ((0,),)), BLK, 1)
    reduce_held = double(((after(reduce_block, middle_held[0]),), ((0,),)), BLK, 1)
    quarter_far = swap(after(quarter, front), VOCAB, 2)
    quarters = in_order(
        member, [quarter, swap(quarter, VOCAB, 1), quarter_far, swap(quarter_far, VOCAB, 1)]
    )
    front_held = double(front_held, BLK, 0)
    front_held = double(held_after(front_held, middle_held[0]), BATCH, 0)
    middle_held = double(middle_held, BATCH, 0)
    reduce_held = double(reduce_held, BLK, 0)
    attend_weight, vectors = place_blocks(
        front_held,
        plane,
        ((0, plane_rows, 0, 3 * part), (plane_rows, vector_lines, 0, LANES)),
    )

    shards_all = size_blk * size_batch * size_vocab
    vectors = vectors.reshape(shards_all, vector_lines // size_vocab, LANES).astype(jnp.float32)
    first_gain, first_shift, output_bias, second_gain, second_shift, reduce_bias = [
        vectors[:, k, :shard_rows].reshape(width) for k in range(6)
    ]
    attend_bias = vectors[:, 6, : 2 * shard_rows].reshape(2 * width)
    expand_bias = vectors[:, 7, : 4 * shard_rows].reshape(2 * ff_part)
    query_bias = rows_of(attend_bias, half * part, part)
    value_bias = rows_of(attend_bias, width + half * part, part)
    joined_bias = jnp.concatenate([query_bias, jnp.zeros((part,), jnp.float32), value_bias])
    expand_bias = rows_of(expand_bias, half * ff_part, ff_part)

    inputs_low = jnp.concatenate(quarters, axis=0)
    inputs = inputs_low.astype(jnp.float32)
    inputs_own = rows_of(inputs_low, half * own_rows, own_rows).astype(jnp.float32)
    normed_one = layer_norm(inputs, first_gain, first_shift).astype(jnp.bfloat16)
    normed_one = after(normed_one, middle_held[0], reduce_held[0])
    joined = (matmul_plain(normed_one, attend_weight) + joined_bias).astype(jnp.bfloat16)
    block = math.gcd(rows, 256)
    mixed_rows = attend_rows(joined, seq_length, block)
    middle_held = held_after(double(middle_held, BLK, 0), mixed_rows)
    reduce_held = double(reduce_held, BATCH, 0)
    mixed_rows = after(mixed_rows, middle_held[0], reduce_held[0])
    expand_weight, output_columns = place_blocks(
        middle_held, plane, ((0, plane_rows, 0, ff_part), (0, plane_rows, ff_part, part))
    )
    output_weight = in_pair(
        is_second,
        rows_of(output_columns, half * part, part),
        swap(rows_of(output_columns, (1 - half) * part, part), VOCAB, 1),
        axis=1,
    )
    attended = matmul_plain(mixed_rows, output_weight)
    middle = (
        inputs_own
        + rows_of(attended, half * own_rows, own_rows)
        + swap(rows_of(attended, (1 - half) * own_rows, own_rows), VOCAB, 1)
        + output_bias
    )
    normed_own = layer_norm(middle, second_gain, second_shift).astype(jnp.bfloat16)
    normed_two = jnp.concatenate([normed_own, swap(normed_own, VOCAB, 1)], axis=0)
    inner_rows = matmul_plain(normed_two, expand_weight) + expand_bias
    active = gelu_tanh(inner_rows).astype(jnp.bfloat16)
    active, slope = lax.optimization_barrier((active, gelu_slope(inner_rows)))
    (reduce_columns,) = place_blocks(reduce_held, plane, ((0, reduce_rows, 0, part),))
    reduce_weight = in_pair(
        is_second,
        rows_of(reduce_columns, half * ff_part, ff_part),
        swap(rows_of(reduce_columns, (1 - half) * ff_part, ff_part), VOCAB, 1),
        axis=1,
    )
    reduced = matmul_plain(active, reduce_weight)
    block_out = middle + reduced[:own_rows] + swap(reduced[own_rows:], VOCAB, 1) + reduce_bias
    final_rows = (0.5 * layer_norm(block_out, gain_final, shift_final)).astype(jnp.bfloat16)

    final_far = swap(final_rows, VOCAB, 2)
    final_parts = jnp.stack(
        [final_rows, swap(final_rows, VOCAB, 1), final_far, swap(final_far, VOCAB, 1)]
    )
    vocab_local = embedding.shape[0]
    valid_columns = jnp.clip(VOCAB_REAL - member * vocab_local, 0, vocab_local)
    logit_student, logit_teacher, stats = vocab_stats(
        final_parts, is_teacher, embedding, valid_columns
    )
    stat_parts = [stats] + [swap(stats, VOCAB, distance) for distance in (1, 2, 3)]
    own_sums, core_sums, divergence_rows = vocab_grads(
        logit_student, logit_teacher, embedding, stat_parts
    )
    positions = jnp.arange(rows, dtype=jnp.int32)
    kl_rows = in_pair(is_second, divergence_rows[0, :own_rows], divergence_rows[0, own_rows:])
    kl_rows = 4.0 * kl_rows * (positions < seq_length).astype(jnp.float32)

    both = own_sums + swap(core_sums, VOCAB, 1).astype(jnp.float32)
    grad_final = jnp.where(is_teacher, both[1], both[0]) + swap(
        jnp.where(is_teacher, both[0], both[1]).astype(jnp.bfloat16), VOCAB, 2
    ).astype(jnp.float32)
    own_valid = (half * own_rows + positions[:own_rows] < seq_length).astype(jnp.float32)
    grad_final = grad_final * (2.0 * own_valid)[:, None]

    grad_out, _, _ = norm_back(block_out, gain_final, grad_final)
    branch_own = grad_out.astype(jnp.bfloat16)
    branch_low = jnp.concatenate([branch_own, swap(branch_own, VOCAB, 1)], axis=0)
    grad_reduce = matmul_left_t(active, branch_low).astype(jnp.bfloat16)
    grad_reduce = in_pair(
        is_second,
        columns_of(grad_reduce, half * part, part),
        swap(columns_of(grad_reduce, (1 - half) * part, part), VOCAB, 1),
    )
    grid = (2, 2, 2)
    reduce_sum = halve(grad_reduce.reshape(grid + (reduce_rows, part)), BATCH, 0)
    grad_active = matmul_right_t(branch_low, reduce_weight)
    inner_grad = (grad_active * slope).astype(jnp.bfloat16)
    grad_normed = matmul_right_t(inner_grad, expand_weight)
    grad_normed_own = grad_normed[:own_rows] + swap(grad_normed[own_rows:], VOCAB, 1)
    middle_part, grad_second_gain, grad_second_shift = norm_back(
        middle, second_gain, grad_normed_own
    )
    grad_middle = grad_out + middle_part
    attn_own = grad_middle.astype(jnp.bfloat16)
    attn_low = in_pair(is_second, attn_own, swap(attn_own, VOCAB, 1))
    grad_mixed = matmul_right_t(attn_low, output_weight).astype(jnp.bfloat16)
    grad_expand = matmul_left_t(normed_two, inner_grad).astype(jnp.bfloat16)
    grad_output = matmul_left_t(mixed_rows, attn_low).astype(jnp.bfloat16)
    grad_output = in_pair(
        is_second,
        columns_of(grad_output, half * part, part),
        swap(columns_of(grad_output, (1 - half) * part, part), VOCAB, 1),
    )
    grad_middles = jnp.concatenate([grad_expand, grad_output], axis=1)
    grad_middles = grad_middles.reshape(grid + (plane_rows, ff_part + part))
    middle_sum = halve(grad_middles, BLK, 0)
    joined_grad = jnp.concatenate(attend_grads(joined, grad_mixed, seq_length, block), axis=1)
    reduce_sum = halve(after(reduce_sum, joined_grad), BLK, 0)
    joined_grad = after(joined_grad, middle_sum)
    grad_normed = matmul_right_t(joined_grad, attend_weight)
    grad_attend = matmul_left_t(normed_one, joined_grad).astype(jnp.bfloat16)
    grad_normed_own = rows_of(grad_normed, half * own_rows, own_rows) + swap(
        rows_of(grad_normed, (1 - half) * own_rows, own_rows), VOCAB, 1
    )
    input_part, grad_first_gain, grad_first_shift = norm_back(
        inputs_own, first_gain, grad_normed_own
    )
    grad_inputs = (grad_middle + input_part).reshape(2, rows_local, width)
    input_sum = jnp.where(is_teacher, grad_inputs[1], grad_inputs[0]) + swap(
        jnp.where(is_teacher, grad_inputs[0], grad_inputs[1]).astype(jnp.bfloat16), VOCAB, 2
    ).astype(jnp.float32)
    home = [
        (a * size_vocab + 2 * m + h, (2 * h + m) * size_vocab + a)
        for a in range(size_blk)
        for m in (0, 1)
        for h in (0, 1)
    ]
    input_grad = lax.ppermute(input_sum.astype(jnp.bfloat16), crossing, home).astype(jnp.float32)
    kl_rows = after(rows_of(kl_rows, member * rows_local, rows_local), input_sum)
    kl_out = lax.ppermute(kl_rows, crossing, turn)

    bias_sums = column_sums(joined_grad)

    def spread_half(values, count):
        return jnp.where(
            jnp.arange(2)[:, None] == half, values.reshape(1, count), 0.0
        ).reshape(2 * count)

    vector_parts = [
        grad_first_gain,
        grad_first_shift,
        column_sums(attn_own),
        grad_second_gain,
        grad_second_shift,
        column_sums(branch_own),
        jnp.concatenate(
            [spread_half(bias_sums[:part], part), spread_half(bias_sums[2 * part :], part)]
        ),
        spread_half(column_sums(inner_grad), ff_part),
    ]
    vector_grads = jnp.concatenate([v.reshape(shards_all, -1) for v in vector_parts], axis=1)
    vector_grads = jnp.pad(
        vector_grads.reshape(size_blk * size_batch, size_vocab, -1),
        ((0, 0), (0, 4), (0, 3 * part - vector_grads.shape[1])),
    ).astype(jnp.bfloat16)
    grad_front = jnp.concatenate(
        [grad_attend.reshape(size_blk * size_batch, plane_rows, 3 * part), vector_grads], axis=1
    )
    middle_sum = halve(after(middle_sum, grad_front), BATCH, 0)
    reduce_sum = halve(after(reduce_sum, grad_front), BLK, 1)[0, 0, 0]
    front_sum = halve(grad_front.reshape(grid + grad_front.shape[1:]), BLK, 0)
    middle_sum = halve(middle_sum, BLK, 1)[0, 0, 0]
    front_sum = halve(halve(front_sum, BATCH, 0), BLK, 1)[0, 0, 0]

    share = reduce_rows // size_vocab
    back = exchange_models(
        [
            jnp.concatenate(
                [
                    middle_sum[t * shard_rows : (t + 1) * shard_rows, k * part : (k + 1) * part]
                    for k in range(units)
                ]
                + [reduce_sum[t * share : (t + 1) * share]],
                axis=0,
            ).astype(jnp.bfloat16)
            for t in range(size_vocab)
        ]
    )
    front = exchange_models(
        [
            jnp.concatenate(
                [
                    front_sum[t * shard_rows : (t + 1) * shard_rows],
                    jnp.pad(front_sum[plane_rows + t][None], ((0, 7), (0, 0))),
                ],
                axis=0,
            ).astype(jnp.bfloat16)
            for t in range(size_vocab)
        ]
    )
    results = []
    for m in (0, 1):
        sides = front[2 * m : 2 * m + 2]
        vector = sum(side[shard_rows].astype(jnp.float32) for side in sides)
        pieces = [vector[k * shard_rows : (k + 1) * shard_rows] for k in range(6)]
        attend = jnp.concatenate(
            [side[:shard_rows, k * part : (k + 1) * part] for k in range(3) for side in sides],
            axis=1,
        ).astype(jnp.float32)
        sides = back[2 * m : 2 * m + 2]
        output = jnp.concatenate(
            [side[(units - 1) * shard_rows : units * shard_rows] for side in sides], axis=1
        ).astype(jnp.float32)
        expand = jnp.concatenate(
            [
                side[k * shard_rows : (k + 1) * shard_rows]
                for side in sides
                for k in range(units - 1)
            ],
            axis=1,
        ).astype(jnp.float32)
        reduce = jnp.concatenate([side[units * shard_rows :] for side in sides], axis=1)
        reduce = reduce.astype(jnp.float32)
        results += [
            pieces[0],
            pieces[1],
            attend,
            vector[6 * shard_rows : 8 * shard_rows],
            output,
            pieces[2],
            pieces[3],
            pieces[4],
            expand,
            vector[8 * shard_rows : 12 * shard_rows],
            reduce,
            pieces[5],
        ]
    return tuple(results) + (input_grad[None], kl_out[None])


def solution(mesh):
    by_model = mesh.shape[VOCAB] == 4 and mesh.shape[BLK] == 4 and mesh.shape[BATCH] == 2
    return jax.shard_map(
        shards_by_model if by_model else shards,
        mesh=mesh,
        in_specs=(
            P((BATCH, VOCAB), BLK, None),
            P((BATCH, VOCAB)),
            P(EVERY),
            P(EVERY),
            P(EVERY, None),
            P(EVERY),
            P(EVERY, None),
            P(EVERY),
            P(EVERY),
            P(EVERY),
            P(EVERY, None),
            P(EVERY),
            P(EVERY, None),
            P(EVERY),
            P(EVERY),
            P(EVERY),
            P(EVERY, None),
            P(EVERY),
            P(EVERY, None),
            P(EVERY),
            P(EVERY),
            P(EVERY),
            P(EVERY, None),
            P(EVERY),
            P(EVERY, None),
            P(EVERY),
            P(),
            P(),
            P(VOCAB, None),
        ),
        out_specs=(
            P(EVERY),
            P(EVERY),
            P(EVERY, None),
            P(EVERY),
            P(EVERY, None),
            P(EVERY),
            P(EVERY),
            P(EVERY),
            P(EVERY, None),
            P(EVERY),
            P(EVERY, None),
            P(EVERY),
            P(EVERY),
            P(EVERY),
            P(EVERY, None),
            P(EVERY),
            P(EVERY, None),
            P(EVERY),
            P(EVERY),
            P(EVERY),
            P(EVERY, None),
            P(EVERY),
            P(EVERY, None),
            P(EVERY),
            P((BATCH, VOCAB), BLK, None),
            P((BATCH, VOCAB), BLK),
        ),
        check_vma=False,
    )
```

```python
import functools
import math

import jax
import jax.numpy as jnp
from jax import lax
from jax.experimental import pallas as pl
from jax.experimental.pallas import tpu as pltpu
from jax.sharding import PartitionSpec as P

HEADS = 12
HEAD = 64
VOCAB_REAL = 50257
BLK, BATCH, VOCAB = "blk", "batch", "vocab"
EVERY = (BLK, BATCH, VOCAB)


def for_sending(shard):
    return jax.tree.map(lambda a: a.astype(jnp.bfloat16) if a.dtype == jnp.float32 else a, shard)


def layer_norm(inputs, gain_row, shift_row):
    centred = inputs - jnp.mean(inputs, axis=-1, keepdims=True)
    spread = jnp.mean(centred * centred, axis=-1, keepdims=True)
    return centred * lax.rsqrt(spread + 1e-05) * gain_row + shift_row


def gelu_tanh(inputs):
    return jax.nn.gelu(inputs, approximate=True)


def matmul_plain(left_side, right_side):
    return jnp.dot(left_side, right_side, preferred_element_type=jnp.float32)


def matmul_right_t(left_side, right_side):
    return lax.dot_general(
        left_side, right_side, (((1,), (1,)), ((), ())), preferred_element_type=jnp.float32
    )


def matmul_left_t(left_side, right_side):
    return lax.dot_general(
        left_side, right_side, (((0,), (0,)), ((), ())), preferred_element_type=jnp.float32
    )


def column_sums(rows_low):
    return jnp.sum(rows_low.astype(jnp.float32), axis=0)


def split_heads(rows_flat):
    return rows_flat.reshape(rows_flat.shape[0], rows_flat.shape[1], HEADS, HEAD)


def front_half(inputs, params):
    model_width = inputs.shape[-1]
    normed_one = layer_norm(
        inputs, params[0].astype(jnp.float32), params[1].astype(jnp.float32)
    ).astype(jnp.bfloat16)
    joined = matmul_plain(normed_one.reshape(-1, model_width), params[2])
    bias_row = params[3].astype(jnp.float32)
    query_rows = (
        (joined[:, :model_width] + bias_row[:model_width])
        .astype(jnp.bfloat16)
        .reshape(inputs.shape)
    )
    key_rows = joined[:, model_width : 2 * model_width].astype(jnp.bfloat16).reshape(inputs.shape)
    value_rows = (
        (joined[:, 2 * model_width :] + bias_row[model_width:])
        .astype(jnp.bfloat16)
        .reshape(inputs.shape)
    )
    return (normed_one.reshape(-1, model_width), query_rows, key_rows, value_rows)


def attend_block(carried, block_in, first_row, queries, query_pos, seq_lengths):
    head_scale = HEAD ** (-0.5)
    key_count = block_in[0].shape[1]
    key_pos = jnp.arange(key_count, dtype=jnp.int32)
    allowed = (
        (key_pos[None, None, :] <= query_pos[None, :, None])
        & (key_pos[None, None, :] < seq_lengths[:, None, None])
    )[:, None]
    skipped = (first_row > query_pos[-1]) | (first_row >= jnp.max(seq_lengths))

    def attend_update():
        results = []
        for model_index in range(2):
            running, row_max, row_total = carried[model_index]
            key_rows = split_heads(block_in[2 * model_index])
            value_rows = split_heads(block_in[2 * model_index + 1])
            scores = (
                jnp.einsum(
                    "sqhd,skhd->shqk",
                    queries[model_index],
                    key_rows,
                    preferred_element_type=jnp.float32,
                )
                * head_scale
            )
            new_max = jnp.maximum(row_max, jnp.max(jnp.where(allowed, scores, -1e30), axis=-1))
            weights = jnp.where(allowed, jnp.exp(scores - new_max[..., None]), 0.0)
            row_total = jnp.sum(weights, axis=-1)
            running = jnp.einsum(
                "shqk,skhd->shqd",
                weights.astype(jnp.bfloat16),
                value_rows,
                preferred_element_type=jnp.float32,
            )
            results.append((running, new_max, row_total))
        return tuple(results)

    return lax.cond(skipped, lambda: carried, attend_update)


def query_grad_block(
    carried, block_in, first_row, queries, grads_heads, log_totals, deltas, query_pos, seq_lengths
):
    head_scale = HEAD ** (-0.5)
    key_count = block_in[0].shape[1]
    key_pos = jnp.arange(key_count, dtype=jnp.int32)
    allowed = (
        (key_pos[None, None, :] <= query_pos[None, :, None])
        & (key_pos[None, None, :] < seq_lengths[:, None, None])
    )[:, None]
    skipped = (first_row > query_pos[-1]) | (first_row >= jnp.max(seq_lengths))

    def query_update():
        results = []
        for model_index in range(2):
            key_rows = split_heads(block_in[2 * model_index])
            value_rows = split_heads(block_in[2 * model_index + 1])
            scores = (
                jnp.einsum(
                    "sqhd,skhd->shqk",
                    queries[model_index],
                    key_rows,
                    preferred_element_type=jnp.float32,
                )
                * head_scale
            )
            prob_rows = jnp.where(
                allowed, jnp.exp(scores - log_totals[model_index][..., None]), 0.0
            )
            grad_prob = jnp.einsum(
                "sqhd,skhd->shqk",
                grads_heads[model_index],
                value_rows,
                preferred_element_type=jnp.float32,
            )
            grad_scores = (prob_rows * (grad_prob - deltas[model_index][..., None])).astype(
                jnp.bfloat16
            )
            results.append(
                carried[model_index]
                + jnp.einsum(
                    "shqk,skhd->shqd", grad_scores, key_rows, preferred_element_type=jnp.float32
                )
                * head_scale
            )
        return tuple(results)

    return lax.cond(skipped, lambda: carried, query_update)


def key_grad_block(carried, block_in, first_row, keys_local, values_local, key_pos, seq_lengths):
    head_scale = HEAD ** (-0.5)
    query_count = block_in[0].shape[1]
    query_pos = jnp.arange(query_count, dtype=jnp.int32)
    allowed = (
        (key_pos[None, None, :] <= query_pos[None, :, None])
        & (key_pos[None, None, :] < seq_lengths[:, None, None])
    )[:, None]
    skipped = (first_row + query_count - 1 < key_pos[0]) | (key_pos[0] >= jnp.max(seq_lengths))

    def key_update():
        results = []
        for model_index in range(2):
            grad_keys, grad_values = carried[model_index]
            query_rows = split_heads(block_in[4 * model_index])
            grad_rows = split_heads(block_in[4 * model_index + 1])
            log_rows = jnp.transpose(block_in[4 * model_index + 2], (0, 2, 1))
            delta_rows = jnp.transpose(block_in[4 * model_index + 3], (0, 2, 1))
            scores = (
                jnp.einsum(
                    "sqhd,skhd->shqk",
                    query_rows,
                    keys_local[model_index],
                    preferred_element_type=jnp.float32,
                )
                * head_scale
            )
            prob_rows = jnp.where(allowed, jnp.exp(scores - log_rows[..., None]), 0.0)
            grad_values = grad_values + jnp.einsum(
                "shqk,sqhd->shkd",
                prob_rows.astype(jnp.bfloat16),
                grad_rows,
                preferred_element_type=jnp.float32,
            )
            grad_prob = jnp.einsum(
                "sqhd,skhd->shqk",
                grad_rows,
                values_local[model_index],
                preferred_element_type=jnp.float32,
            )
            grad_scores = (prob_rows * (grad_prob - delta_rows[..., None])).astype(jnp.bfloat16)
            grad_keys = (
                grad_keys
                + jnp.einsum(
                    "shqk,sqhd->shkd", grad_scores, query_rows, preferred_element_type=jnp.float32
                )
                * head_scale
            )
            results.append((grad_keys, grad_values))
        return tuple(results)

    return lax.cond(skipped, lambda: carried, key_update)


def shards(
    hidden,
    lengths,
    student_first_gain,
    student_first_shift,
    student_attend_weight,
    student_attend_bias,
    student_output_weight,
    student_output_bias,
    student_second_gain,
    student_second_shift,
    student_expand_weight,
    student_expand_bias,
    student_reduce_weight,
    student_reduce_bias,
    teacher_first_gain,
    teacher_first_shift,
    teacher_attend_weight,
    teacher_attend_bias,
    teacher_output_weight,
    teacher_output_bias,
    teacher_second_gain,
    teacher_second_shift,
    teacher_expand_weight,
    teacher_expand_bias,
    teacher_reduce_weight,
    teacher_reduce_bias,
    final_gain,
    final_shift,
    embedding,
):
    gathered = (
        lax.all_gather(student_first_gain, EVERY, axis=0, tiled=True),
        lax.all_gather(student_first_shift, EVERY, axis=0, tiled=True),
        lax.all_gather(student_attend_weight, EVERY, axis=0, tiled=True),
        lax.all_gather(student_attend_bias, EVERY, axis=0, tiled=True),
        lax.all_gather(student_output_weight, EVERY, axis=0, tiled=True),
        lax.all_gather(student_output_bias, EVERY, axis=0, tiled=True),
        lax.all_gather(student_second_gain, EVERY, axis=0, tiled=True),
        lax.all_gather(student_second_shift, EVERY, axis=0, tiled=True),
        lax.all_gather(student_expand_weight, EVERY, axis=0, tiled=True),
        lax.all_gather(student_expand_bias, EVERY, axis=0, tiled=True),
        lax.all_gather(student_reduce_weight, EVERY, axis=0, tiled=True),
        lax.all_gather(student_reduce_bias, EVERY, axis=0, tiled=True),
        lax.all_gather(teacher_first_gain, EVERY, axis=0, tiled=True),
        lax.all_gather(teacher_first_shift, EVERY, axis=0, tiled=True),
        lax.all_gather(teacher_attend_weight, EVERY, axis=0, tiled=True),
        lax.all_gather(teacher_attend_bias, EVERY, axis=0, tiled=True),
        lax.all_gather(teacher_output_weight, EVERY, axis=0, tiled=True),
        lax.all_gather(teacher_output_bias, EVERY, axis=0, tiled=True),
        lax.all_gather(teacher_second_gain, EVERY, axis=0, tiled=True),
        lax.all_gather(teacher_second_shift, EVERY, axis=0, tiled=True),
        lax.all_gather(teacher_expand_weight, EVERY, axis=0, tiled=True),
        lax.all_gather(teacher_expand_bias, EVERY, axis=0, tiled=True),
        lax.all_gather(teacher_reduce_weight, EVERY, axis=0, tiled=True),
        lax.all_gather(teacher_reduce_bias, EVERY, axis=0, tiled=True),
    )
    models = (tuple(gathered[:12]), tuple(gathered[12:]))
    batch_seqs, rows_local, model_width = hidden.shape
    row_count = batch_seqs * rows_local
    inputs = hidden.astype(jnp.float32)
    inputs_flat = inputs.reshape(row_count, model_width)
    query_pos = lax.axis_index(BLK) * rows_local + jnp.arange(rows_local, dtype=jnp.int32)
    fronts = [front_half(inputs, params) for params in models]
    queries = (split_heads(fronts[0][1]), split_heads(fronts[1][1]))
    zero_heads = jnp.zeros((batch_seqs, HEADS, rows_local, HEAD), jnp.float32)
    zero_rows = jnp.zeros((batch_seqs, HEADS, rows_local), jnp.float32)
    start_state = (
        zero_heads,
        jnp.full((batch_seqs, HEADS, rows_local), -1e30, jnp.float32),
        zero_rows,
    )
    folded = attend_block(
        (start_state, start_state),
        (
            lax.all_gather(fronts[0][2], BLK, axis=1, tiled=True),
            lax.all_gather(fronts[0][3], BLK, axis=1, tiled=True),
            lax.all_gather(fronts[1][2], BLK, axis=1, tiled=True),
            lax.all_gather(fronts[1][3], BLK, axis=1, tiled=True),
        ),
        jnp.int32(0),
        queries,
        query_pos,
        lengths,
    )
    gain_final = final_gain.astype(jnp.float32)
    shift_final = final_shift.astype(jnp.float32)
    caches = []
    final_rows = []
    for model_index in range(2):
        params = models[model_index]
        running, row_max, row_total = folded[model_index]
        mixed_rows = (
            jnp.transpose(running / row_total[..., None], (0, 2, 1, 3))
            .reshape(row_count, model_width)
            .astype(jnp.bfloat16)
        )
        log_total = row_max + jnp.log(row_total)
        middle = inputs_flat + matmul_plain(mixed_rows, params[4]) + params[5].astype(jnp.float32)
        normed_two = layer_norm(
            middle, params[6].astype(jnp.float32), params[7].astype(jnp.float32)
        ).astype(jnp.bfloat16)
        inner_rows = matmul_plain(normed_two, params[8]) + params[9].astype(jnp.float32)
        active = gelu_tanh(inner_rows).astype(jnp.bfloat16)
        block_out = middle + matmul_plain(active, params[10]) + params[11].astype(jnp.float32)
        final_rows.append(layer_norm(block_out, gain_final, shift_final).astype(jnp.bfloat16))
        caches.append((mixed_rows, log_total, middle, normed_two, inner_rows, active, block_out))
    all_rows = lax.all_gather(jnp.stack(final_rows), VOCAB, axis=1, tiled=True)
    vocab_local = embedding.shape[0]
    vocab_index = lax.axis_index(VOCAB)
    column_valid = (
        vocab_index * vocab_local + jnp.arange(vocab_local, dtype=jnp.int32) < VOCAB_REAL
    )[None, :]
    total_rows = all_rows.shape[1]

    def scaled_logits(rows_pair):
        scaled_student = jnp.where(
            column_valid, matmul_right_t(rows_pair[0], embedding) * 0.5, -1e30
        )
        scaled_teacher = jnp.where(
            column_valid, matmul_right_t(rows_pair[1], embedding) * 0.5, -1e30
        )
        return (scaled_student, scaled_teacher)

    stat_rows = math.gcd(total_rows, 512)

    def local_stats(block_index):
        rows_pair = lax.dynamic_slice_in_dim(all_rows, block_index * stat_rows, stat_rows, 1)
        scaled_student, scaled_teacher = scaled_logits(rows_pair)
        max_student = jnp.max(scaled_student, axis=-1)
        max_teacher = jnp.max(scaled_teacher, axis=-1)
        exp_student = jnp.where(column_valid, jnp.exp(scaled_student - max_student[:, None]), 0.0)
        exp_teacher = jnp.where(column_valid, jnp.exp(scaled_teacher - max_teacher[:, None]), 0.0)
        cross_sum = jnp.sum(exp_teacher * (scaled_teacher - scaled_student), axis=-1)
        return (
            max_student,
            jnp.sum(exp_student, axis=-1),
            max_teacher,
            jnp.sum(exp_teacher, axis=-1),
            cross_sum,
        )

    stat_blocks = lax.map(local_stats, jnp.arange(total_rows // stat_rows))
    max_student, sum_student, max_teacher, sum_teacher, cross_sum = [
        stat_block.reshape(total_rows) for stat_block in stat_blocks
    ]
    top_student, top_teacher = lax.pmax((max_student, max_teacher), VOCAB)
    factor_student = jnp.exp(max_student - top_student)
    factor_teacher = jnp.exp(max_teacher - top_teacher)
    sum_student, sum_teacher, cross_sum = lax.psum(
        (sum_student * factor_student, sum_teacher * factor_teacher, cross_sum * factor_teacher),
        VOCAB,
    )
    max_student, max_teacher = (top_student, top_teacher)
    lse_student = max_student + jnp.log(sum_student)
    lse_teacher = max_teacher + jnp.log(sum_teacher)
    divergence_rows = cross_sum / sum_teacher - lse_teacher + lse_student
    valid_rows = (query_pos[None, :] < lengths[:, None]).astype(jnp.float32)
    own_start = vocab_index * row_count
    kl_out = (
        4.0
        * lax.dynamic_slice_in_dim(divergence_rows, own_start, row_count).reshape(
            batch_seqs, rows_local
        )
        * valid_rows
    )
    step_rows = math.gcd(row_count * lax.axis_size(VOCAB), 512)

    def one_block(block_index):
        begin = block_index * step_rows
        rows_pair = lax.dynamic_slice_in_dim(all_rows, begin, step_rows, 1)
        scaled_student, scaled_teacher = scaled_logits(rows_pair)
        log_student = (
            scaled_student - lax.dynamic_slice_in_dim(lse_student, begin, step_rows)[:, None]
        )
        log_teacher = (
            scaled_teacher - lax.dynamic_slice_in_dim(lse_teacher, begin, step_rows)[:, None]
        )
        row_kl = lax.dynamic_slice_in_dim(divergence_rows, begin, step_rows)[:, None]
        prob_student = jnp.where(column_valid, jnp.exp(log_student), 0.0)
        prob_teacher = jnp.where(column_valid, jnp.exp(log_teacher), 0.0)
        grad_student = (2.0 * (prob_student - prob_teacher)).astype(jnp.bfloat16)
        grad_teacher = (2.0 * prob_teacher * (log_teacher - log_student - row_kl)).astype(
            jnp.bfloat16
        )
        return jnp.concatenate(
            [matmul_plain(grad_student, embedding), matmul_plain(grad_teacher, embedding)], axis=1
        )

    grad_final = (
        lax.psum_scatter(
            lax.map(one_block, jnp.arange(row_count * lax.axis_size(VOCAB) // step_rows))
            .reshape(row_count * lax.axis_size(VOCAB), 2 * model_width)
            .astype(jnp.bfloat16),
            VOCAB,
            scatter_dimension=0,
            tiled=True,
        ).astype(jnp.float32)
        * valid_rows.reshape(row_count)[:, None]
    )
    regathered = (
        lax.all_gather(student_first_gain, EVERY, axis=0, tiled=True),
        lax.all_gather(student_first_shift, EVERY, axis=0, tiled=True),
        lax.all_gather(student_attend_weight, EVERY, axis=0, tiled=True),
        lax.all_gather(student_attend_bias, EVERY, axis=0, tiled=True),
        lax.all_gather(student_output_weight, EVERY, axis=0, tiled=True),
        lax.all_gather(student_output_bias, EVERY, axis=0, tiled=True),
        lax.all_gather(student_second_gain, EVERY, axis=0, tiled=True),
        lax.all_gather(student_second_shift, EVERY, axis=0, tiled=True),
        lax.all_gather(student_expand_weight, EVERY, axis=0, tiled=True),
        lax.all_gather(student_expand_bias, EVERY, axis=0, tiled=True),
        lax.all_gather(student_reduce_weight, EVERY, axis=0, tiled=True),
        lax.all_gather(student_reduce_bias, EVERY, axis=0, tiled=True),
        lax.all_gather(teacher_first_gain, EVERY, axis=0, tiled=True),
        lax.all_gather(teacher_first_shift, EVERY, axis=0, tiled=True),
        lax.all_gather(teacher_attend_weight, EVERY, axis=0, tiled=True),
        lax.all_gather(teacher_attend_bias, EVERY, axis=0, tiled=True),
        lax.all_gather(teacher_output_weight, EVERY, axis=0, tiled=True),
        lax.all_gather(teacher_output_bias, EVERY, axis=0, tiled=True),
        lax.all_gather(teacher_second_gain, EVERY, axis=0, tiled=True),
        lax.all_gather(teacher_second_shift, EVERY, axis=0, tiled=True),
        lax.all_gather(teacher_expand_weight, EVERY, axis=0, tiled=True),
        lax.all_gather(teacher_expand_bias, EVERY, axis=0, tiled=True),
        lax.all_gather(teacher_reduce_weight, EVERY, axis=0, tiled=True),
        lax.all_gather(teacher_reduce_bias, EVERY, axis=0, tiled=True),
    )
    back_models = (tuple(regathered[:12]), tuple(regathered[12:]))
    uppers = []
    middle_pairs = []
    for model_index in range(2):
        params = back_models[model_index]
        mixed_rows, log_total, middle, normed_two, inner_rows, active, block_out = caches[
            model_index
        ]
        _, final_pull = jax.vjp(
            lambda rows_in: layer_norm(rows_in, gain_final, shift_final), block_out
        )
        grad_out = final_pull(
            grad_final[:, model_index * model_width : (model_index + 1) * model_width]
        )[0]
        branch_low = grad_out.astype(jnp.bfloat16)
        grad_reduce_bias = column_sums(branch_low)
        grad_active = matmul_right_t(branch_low, params[10])
        _, gelu_pull = jax.vjp(gelu_tanh, inner_rows)
        inner_grad = gelu_pull(grad_active)[0].astype(jnp.bfloat16)
        grad_expand_bias = column_sums(inner_grad)
        grad_normed_two = matmul_right_t(inner_grad, params[8])
        _, second_pull = jax.vjp(
            layer_norm, middle, params[6].astype(jnp.float32), params[7].astype(jnp.float32)
        )
        middle_part, grad_second_gain, grad_second_shift = second_pull(grad_normed_two)
        grad_middle = grad_out + middle_part
        attn_low = grad_middle.astype(jnp.bfloat16)
        grad_output_bias = column_sums(attn_low)
        grad_mixed = matmul_right_t(attn_low, params[4]).astype(jnp.bfloat16)
        delta_rows = jnp.sum(
            (grad_mixed.astype(jnp.float32) * mixed_rows.astype(jnp.float32)).reshape(
                batch_seqs, rows_local, HEADS, HEAD
            ),
            axis=-1,
        )
        uppers.append(
            (
                grad_output_bias,
                grad_second_gain,
                grad_second_shift,
                grad_expand_bias,
                grad_reduce_bias,
                grad_middle,
                grad_mixed.reshape(batch_seqs, rows_local, model_width),
                delta_rows,
            )
        )
        middle_pairs.append(
            ((mixed_rows, attn_low), (normed_two, inner_grad), (active, branch_low))
        )
    grads_heads = (split_heads(uppers[0][6]), split_heads(uppers[1][6]))
    log_totals = (caches[0][1], caches[1][1])
    deltas = (jnp.transpose(uppers[0][7], (0, 2, 1)), jnp.transpose(uppers[1][7], (0, 2, 1)))
    query_grads = query_grad_block(
        (zero_heads, zero_heads),
        (
            lax.all_gather(fronts[0][2], BLK, axis=1, tiled=True),
            lax.all_gather(fronts[0][3], BLK, axis=1, tiled=True),
            lax.all_gather(fronts[1][2], BLK, axis=1, tiled=True),
            lax.all_gather(fronts[1][3], BLK, axis=1, tiled=True),
        ),
        jnp.int32(0),
        queries,
        grads_heads,
        log_totals,
        deltas,
        query_pos,
        lengths,
    )
    keys_local = (split_heads(fronts[0][2]), split_heads(fronts[1][2]))
    values_local = (split_heads(fronts[0][3]), split_heads(fronts[1][3]))
    key_grads = key_grad_block(
        ((zero_heads, zero_heads), (zero_heads, zero_heads)),
        (
            lax.all_gather(fronts[0][1], BLK, axis=1, tiled=True),
            lax.all_gather(uppers[0][6], BLK, axis=1, tiled=True),
            lax.all_gather(
                for_sending(jnp.transpose(log_totals[0], (0, 2, 1))), BLK, axis=1, tiled=True
            ),
            lax.all_gather(uppers[0][7].astype(jnp.bfloat16), BLK, axis=1, tiled=True).astype(
                jnp.float32
            ),
            lax.all_gather(fronts[1][1], BLK, axis=1, tiled=True),
            lax.all_gather(uppers[1][6], BLK, axis=1, tiled=True),
            lax.all_gather(
                for_sending(jnp.transpose(log_totals[1], (0, 2, 1))), BLK, axis=1, tiled=True
            ),
            lax.all_gather(uppers[1][7].astype(jnp.bfloat16), BLK, axis=1, tiled=True).astype(
                jnp.float32
            ),
        ),
        jnp.int32(0),
        keys_local,
        values_local,
        query_pos,
        lengths,
    )
    vectors = []
    pairs = []
    input_grad = jnp.zeros((row_count, model_width), jnp.float32)
    for model_index in range(2):
        params = back_models[model_index]
        upper = uppers[model_index]
        grad_keys, grad_values = key_grads[model_index]
        joined_grad = jnp.concatenate(
            [
                jnp.transpose(query_grads[model_index], (0, 2, 1, 3)).reshape(
                    row_count, model_width
                ),
                jnp.transpose(grad_keys, (0, 2, 1, 3)).reshape(row_count, model_width),
                jnp.transpose(grad_values, (0, 2, 1, 3)).reshape(row_count, model_width),
            ],
            axis=1,
        ).astype(jnp.bfloat16)
        bias_sums = column_sums(joined_grad)
        grad_attend_bias = jnp.concatenate([bias_sums[:model_width], bias_sums[2 * model_width :]])
        grad_normed_one = matmul_right_t(joined_grad, params[2])
        _, first_pull = jax.vjp(
            layer_norm, inputs_flat, params[0].astype(jnp.float32), params[1].astype(jnp.float32)
        )
        input_part, grad_first_gain, grad_first_shift = first_pull(grad_normed_one)
        input_grad = input_grad + upper[5] + input_part
        vectors.append(
            [
                grad_first_gain,
                grad_first_shift,
                grad_attend_bias,
                upper[0],
                upper[1],
                upper[2],
                upper[3],
                upper[4],
            ]
        )
        pairs.append(
            [
                (fronts[model_index][0], joined_grad),
                middle_pairs[model_index][0],
                middle_pairs[model_index][1],
                middle_pairs[model_index][2],
            ]
        )
    grads = []
    for model_index in range(2):
        matrix_list = [matmul_left_t(pair[0], pair[1]) for pair in pairs[model_index]]
        vector_list = vectors[model_index]
        grads.extend(
            [
                vector_list[0],
                vector_list[1],
                matrix_list[0],
                vector_list[2],
                matrix_list[1],
                vector_list[3],
                vector_list[4],
                vector_list[5],
                matrix_list[2],
                vector_list[6],
                matrix_list[3],
                vector_list[7],
            ]
        )
    summed = (
        lax.psum_scatter(grads[0], EVERY, scatter_dimension=0, tiled=True),
        lax.psum_scatter(grads[1], EVERY, scatter_dimension=0, tiled=True),
        lax.psum_scatter(grads[2], EVERY, scatter_dimension=0, tiled=True),
        lax.psum_scatter(grads[3], EVERY, scatter_dimension=0, tiled=True),
        lax.psum_scatter(grads[4], EVERY, scatter_dimension=0, tiled=True),
        lax.psum_scatter(grads[5], EVERY, scatter_dimension=0, tiled=True),
        lax.psum_scatter(grads[6], EVERY, scatter_dimension=0, tiled=True),
        lax.psum_scatter(grads[7], EVERY, scatter_dimension=0, tiled=True),
        lax.psum_scatter(grads[8], EVERY, scatter_dimension=0, tiled=True),
        lax.psum_scatter(grads[9], EVERY, scatter_dimension=0, tiled=True),
        lax.psum_scatter(grads[10], EVERY, scatter_dimension=0, tiled=True),
        lax.psum_scatter(grads[11], EVERY, scatter_dimension=0, tiled=True),
        lax.psum_scatter(grads[12], EVERY, scatter_dimension=0, tiled=True),
        lax.psum_scatter(grads[13], EVERY, scatter_dimension=0, tiled=True),
        lax.psum_scatter(grads[14], EVERY, scatter_dimension=0, tiled=True),
        lax.psum_scatter(grads[15], EVERY, scatter_dimension=0, tiled=True),
        lax.psum_scatter(grads[16], EVERY, scatter_dimension=0, tiled=True),
        lax.psum_scatter(grads[17], EVERY, scatter_dimension=0, tiled=True),
        lax.psum_scatter(grads[18], EVERY, scatter_dimension=0, tiled=True),
        lax.psum_scatter(grads[19], EVERY, scatter_dimension=0, tiled=True),
        lax.psum_scatter(grads[20], EVERY, scatter_dimension=0, tiled=True),
        lax.psum_scatter(grads[21], EVERY, scatter_dimension=0, tiled=True),
        lax.psum_scatter(grads[22], EVERY, scatter_dimension=0, tiled=True),
        lax.psum_scatter(grads[23], EVERY, scatter_dimension=0, tiled=True),
    )
    return tuple(summed) + (input_grad.reshape(batch_seqs, rows_local, model_width), kl_out)


LANES = 128
MARGIN = 16.0
VMEM_BYTES = 60 * 1024 * 1024


def lane_fold(tile_in, combine):
    folded = tile_in[:, :LANES]
    for start in range(LANES, tile_in.shape[1], LANES):
        folded = combine(folded, tile_in[:, start : start + LANES])
    return folded


def whole_block(shape):
    return pl.BlockSpec(shape, lambda *_: (0,) * len(shape))


def vocab_stats_kernel(
    scalars_ref,
    student_low_ref,
    student_high_ref,
    teacher_low_ref,
    teacher_high_ref,
    embed_ref,
    logit_student_ref,
    logit_teacher_ref,
    stats_ref,
    tile_max_s,
    tile_max_t,
    max_s,
    max_t,
    sum_s,
    sum_t,
    cross,
    part_s,
    part_t,
    part_x,
    *,
    tile,
    rows_block,
):
    step_index = pl.program_id(0)
    steps = pl.num_programs(0)
    half_rows = student_low_ref.shape[1]
    rows = 2 * half_rows

    @pl.when(step_index == 0)
    def _():
        max_s[...] = jnp.full_like(max_s, -1e30)
        max_t[...] = jnp.full_like(max_t, -1e30)
        for total in (sum_s, sum_t, cross):
            total[...] = jnp.zeros_like(total)

    def sums(scaled_s, scaled_t, top_s, top_t):
        shifted_s = scaled_s - top_s
        shifted_t = scaled_t - top_t
        exp_s = jnp.exp(shifted_s)
        exp_t = jnp.exp(shifted_t)
        return (
            lane_fold(exp_s, jnp.add),
            lane_fold(exp_t, jnp.add),
            lane_fold(exp_t * (shifted_t - shifted_s), jnp.add),
        )

    def one_tile(masked):
        embed_tile = embed_ref[...]
        excess = None
        for start in range(0, rows, rows_block):
            here = pl.ds(start, rows_block)
            source = pl.ds(start % half_rows, rows_block)
            student_ref = student_low_ref if start < half_rows else student_high_ref
            teacher_ref = teacher_low_ref if start < half_rows else teacher_high_ref
            scaled_s = matmul_right_t(student_ref[0, source, :], embed_tile)
            scaled_t = matmul_right_t(teacher_ref[0, source, :], embed_tile)
            if masked:
                column = lax.broadcasted_iota(jnp.int32, (1, tile), 1) + step_index * tile
                scaled_s = jnp.where(column < scalars_ref[0], scaled_s, -1e30)
                scaled_t = jnp.where(column < scalars_ref[0], scaled_t, -1e30)
            logit_student_ref[here, :] = scaled_s
            logit_teacher_ref[here, :] = scaled_t
            tops_s = lane_fold(scaled_s, jnp.maximum)
            tops_t = lane_fold(scaled_t, jnp.maximum)
            tile_max_s[here, :] = tops_s
            tile_max_t[here, :] = tops_t
            old_s = max_s[here, :]
            old_t = max_t[here, :]
            part_s[here, :], part_t[here, :], part_x[here, :] = sums(
                scaled_s, scaled_t, old_s[:, :1], old_t[:, :1]
            )
            over = jnp.maximum(tops_s - old_s, tops_t - old_t)
            excess = over if excess is None else jnp.maximum(excess, over)

        @pl.when(jnp.max(excess) > MARGIN)
        def _():
            def rescale(chunk, _):
                here = pl.ds(pl.multiple_of(chunk * 64, 64), 64)
                old_s = max_s[here, :]
                old_t = max_t[here, :]
                new_s = jnp.maximum(old_s, jnp.max(tile_max_s[here, :], axis=1, keepdims=True))
                new_t = jnp.maximum(old_t, jnp.max(tile_max_t[here, :], axis=1, keepdims=True))
                factor_t = jnp.exp(old_t - new_t)
                moved = (old_t - old_s) - (new_t - new_s)
                max_s[here, :] = new_s
                max_t[here, :] = new_t
                sum_s[here, :] = sum_s[here, :] * jnp.exp(old_s - new_s)
                cross[here, :] = (cross[here, :] + moved * sum_t[here, :]) * factor_t
                sum_t[here, :] = sum_t[here, :] * factor_t
                part_s[here, :], part_t[here, :], part_x[here, :] = sums(
                    logit_student_ref[here, :],
                    logit_teacher_ref[here, :],
                    new_s[:, :1],
                    new_t[:, :1],
                )
                return 0

            lax.fori_loop(0, rows // 64, rescale, 0)

        sum_s[...] += part_s[...]
        sum_t[...] += part_t[...]
        cross[...] += part_x[...]

    @pl.when(step_index < steps - 1)
    def _():
        one_tile(False)

    @pl.when(step_index == steps - 1)
    def _():
        one_tile(True)
        lane = lax.broadcasted_iota(jnp.int32, (rows, LANES), 1)
        result = jnp.sum(cross[...], axis=1, keepdims=True)
        result = jnp.where(lane == 3, jnp.sum(sum_t[...], axis=1, keepdims=True), result)
        result = jnp.where(lane == 2, jnp.sum(sum_s[...], axis=1, keepdims=True), result)
        result = jnp.where(lane == 0, max_s[...], jnp.where(lane == 1, max_t[...], result))
        stats_ref[...] = result.T[:8, :]


def vocab_stats(final_parts, is_teacher, embedding, valid_columns, tile=1280, rows_block=256):
    _, half_rows, width = final_parts.shape
    rows = 2 * half_rows
    steps = pl.cdiv(embedding.shape[0], tile)
    logits = jax.ShapeDtypeStruct((rows, steps * tile), jnp.float32)
    part_spec = lambda teacher, second: pl.BlockSpec(
        (1, half_rows, width),
        lambda j, scalars: (2 * (scalars[1] ^ teacher) + second, 0, 0),
    )
    return pl.pallas_call(
        functools.partial(vocab_stats_kernel, tile=tile, rows_block=rows_block),
        grid_spec=pltpu.PrefetchScalarGridSpec(
            num_scalar_prefetch=1,
            grid=(steps,),
            in_specs=[part_spec(0, 0), part_spec(0, 1), part_spec(1, 0), part_spec(1, 1)]
            + [pl.BlockSpec((tile, width), lambda j, *_: (j, 0))],
            out_specs=[
                pl.BlockSpec((rows, tile), lambda j, *_: (0, j)),
                pl.BlockSpec((rows, tile), lambda j, *_: (0, j)),
                whole_block((8, rows)),
            ],
            scratch_shapes=[pltpu.VMEM((rows, LANES), jnp.float32)] * 10,
        ),
        out_shape=[logits, logits, jax.ShapeDtypeStruct((8, rows), jnp.float32)],
        compiler_params=pltpu.CompilerParams(vmem_limit_bytes=VMEM_BYTES),
        name="vocab_stats",
    )(
        jnp.stack([valid_columns, is_teacher.astype(jnp.int32)]),
        *[final_parts] * 4,
        embedding,
    )


def vocab_grads_kernel(
    logit_student_ref,
    logit_teacher_ref,
    embed_ref,
    *refs,
    tile,
    columns,
    rows_block,
    count,
):
    stat_refs = refs[:count]
    own_ref, send_ref, divergence_ref, row_ref, student_ref, teacher_ref = refs[count:]
    step_index = pl.program_id(0)
    rows = student_ref.shape[0]
    half_rows = rows // 2

    @pl.when(step_index == 0)
    def _():
        student_ref[...] = jnp.zeros_like(student_ref)
        teacher_ref[...] = jnp.zeros_like(teacher_ref)
        parts = []
        for index in range(count):
            part = stat_refs[index][...]
            if index % 2:
                part = jnp.concatenate([part[:, half_rows:], part[:, :half_rows]], axis=1)
            parts.append([part[k : k + 1, :] for k in range(5)])
        top_s = functools.reduce(jnp.maximum, [p[0] for p in parts])
        top_t = functools.reduce(jnp.maximum, [p[1] for p in parts])
        sum_s = sum(p[2] * jnp.exp(p[0] - top_s) for p in parts)
        sum_t = sum(p[3] * jnp.exp(p[1] - top_t) for p in parts)
        cross = sum((p[4] + (p[1] - p[0]) * p[3]) * jnp.exp(p[1] - top_t) for p in parts)
        lse_s = top_s + jnp.log(sum_s)
        lse_t = top_t + jnp.log(sum_t)
        mean_gap = cross / sum_t
        divergence_ref[...] = jnp.broadcast_to(mean_gap - lse_t + lse_s, divergence_ref.shape)
        line = lax.broadcasted_iota(jnp.int32, (LANES, rows), 0)
        row_ref[...] = jnp.where(line == 0, lse_s, jnp.where(line == 1, lse_t, mean_gap)).T

    def one_tile(masked):
        embed_tile = embed_ref[...]
        if masked:
            row = lax.broadcasted_iota(jnp.int32, (tile, 1), 0) + step_index * tile
            embed_tile = jnp.where(row < columns, embed_tile, jnp.zeros_like(embed_tile))
        for start in range(0, rows, rows_block):
            here = pl.ds(start, rows_block)
            scaled_s = logit_student_ref[here, :]
            scaled_t = logit_teacher_ref[here, :]
            prob_s = jnp.exp(scaled_s - row_ref[here, 0:1])
            prob_t = jnp.exp(scaled_t - row_ref[here, 1:2])
            grad_s = (prob_s - prob_t).astype(jnp.bfloat16)
            grad_t = (prob_t * ((scaled_t - scaled_s) - row_ref[here, 2:3])).astype(jnp.bfloat16)
            student_ref[here, :] += matmul_plain(grad_s, embed_tile)
            teacher_ref[here, :] += matmul_plain(grad_t, embed_tile)

    last = pl.num_programs(0) - 1

    @pl.when(step_index < last)
    def _():
        one_tile(False)

    @pl.when(step_index == last)
    def _():
        one_tile(True)
        for index, sums in enumerate((student_ref, teacher_ref)):
            own_ref[index] = sums[:half_rows, :]
            send_ref[index] = sums[half_rows:, :].astype(jnp.bfloat16)


def vocab_grads(logit_student, logit_teacher, embedding, stat_parts, tile=1280, rows_block=256):
    rows = logit_student.shape[0]
    columns, width = embedding.shape
    halves = (2, rows // 2, width)
    return pl.pallas_call(
        functools.partial(
            vocab_grads_kernel,
            tile=tile,
            columns=columns,
            rows_block=rows_block,
            count=len(stat_parts),
        ),
        grid=(pl.cdiv(columns, tile),),
        in_specs=[
            pl.BlockSpec((rows, tile), lambda j: (0, j)),
            pl.BlockSpec((rows, tile), lambda j: (0, j)),
            pl.BlockSpec((tile, width), lambda j: (j, 0)),
        ]
        + [whole_block((8, rows))] * len(stat_parts),
        out_specs=[whole_block(halves), whole_block(halves), whole_block((8, rows))],
        out_shape=[
            jax.ShapeDtypeStruct(halves, jnp.float32),
            jax.ShapeDtypeStruct(halves, jnp.bfloat16),
            jax.ShapeDtypeStruct((8, rows), jnp.float32),
        ],
        scratch_shapes=[
            pltpu.VMEM((rows, LANES), jnp.float32),
            pltpu.VMEM((rows, width), jnp.float32),
            pltpu.VMEM((rows, width), jnp.float32),
        ],
        compiler_params=pltpu.CompilerParams(vmem_limit_bytes=VMEM_BYTES),
        name="vocab_grads",
    )(logit_student, logit_teacher, embedding, *stat_parts)


def attend_kernel(length_ref, query_ref, key_ref, value_ref, mixed_ref, *, block):
    rows = query_ref.shape[0]
    lane = lax.broadcasted_iota(jnp.int32, (1, LANES), 1)
    for start in range(0, rows, block):
        keys = start + block
        key_pos = lax.broadcasted_iota(jnp.int32, (block, keys), 1)
        query_pos = lax.broadcasted_iota(jnp.int32, (block, keys), 0) + start
        allowed = (key_pos <= query_pos) & (key_pos < length_ref[0])
        outs = []
        for head in range(LANES // HEAD):
            own = (lane // HEAD) == head
            queries = query_ref[start : start + block, :] * HEAD**-0.5
            queries = jnp.where(own, queries, jnp.zeros_like(queries))
            scores = matmul_right_t(queries, key_ref[:keys, :])
            scores = jnp.where(allowed, scores, -1e30)
            weights = jnp.exp(scores - jnp.max(scores, axis=1, keepdims=True))
            total = jnp.sum(weights, axis=1, keepdims=True)
            outs.append(
                matmul_plain(weights.astype(jnp.bfloat16), value_ref[:keys, :]) / total
            )
        mixed_ref[start : start + block, :] = jnp.where(lane < HEAD, outs[0], outs[1]).astype(
            jnp.bfloat16
        )


def attend_rows(joined, seq_length, block):
    rows, width = joined.shape
    third = width // 3
    pairs = third // LANES
    spec = lambda part: pl.BlockSpec((rows, LANES), lambda p, *_: (0, part * pairs + p))
    return pl.pallas_call(
        functools.partial(attend_kernel, block=block),
        grid_spec=pltpu.PrefetchScalarGridSpec(
            num_scalar_prefetch=1,
            grid=(pairs,),
            in_specs=[spec(0), spec(1), spec(2)],
            out_specs=spec(0),
        ),
        out_shape=jax.ShapeDtypeStruct((rows, third), jnp.bfloat16),
        compiler_params=pltpu.CompilerParams(vmem_limit_bytes=VMEM_BYTES),
        name="attend",
    )(seq_length.reshape(1), joined, joined, joined)


def attend_grads_kernel(
    length_ref,
    query_ref,
    key_ref,
    value_ref,
    grad_ref,
    grad_query_ref,
    grad_key_ref,
    grad_value_ref,
    sum_key,
    sum_value,
    *,
    block,
):
    rows = query_ref.shape[0]
    lane = lax.broadcasted_iota(jnp.int32, (1, LANES), 1)
    sum_key[...] = jnp.zeros_like(sum_key)
    sum_value[...] = jnp.zeros_like(sum_value)
    keys_turned = key_ref[...].T
    for start in range(0, rows, block):
        keys = start + block
        key_pos = lax.broadcasted_iota(jnp.int32, (keys, block), 0)
        query_pos = lax.broadcasted_iota(jnp.int32, (keys, block), 1) + start
        allowed = (key_pos <= query_pos) & (key_pos < length_ref[0])
        outs = []
        for head in range(LANES // HEAD):
            own = (lane // HEAD) == head
            queries = query_ref[start : start + block, :] * HEAD**-0.5
            queries = jnp.where(own, queries, jnp.zeros_like(queries))
            grads = grad_ref[start : start + block, :]
            grads = jnp.where(own, grads, jnp.zeros_like(grads))
            scores = matmul_right_t(key_ref[:keys, :], queries)
            scores = jnp.where(allowed, scores, -1e30)
            weights = jnp.exp(scores - jnp.max(scores, axis=0, keepdims=True))
            soft = weights * (1.0 / jnp.sum(weights, axis=0, keepdims=True))
            grad_soft = matmul_right_t(value_ref[:keys, :], grads)
            soft_grad = soft * grad_soft
            delta = jnp.sum(soft_grad, axis=0, keepdims=True)
            grad_scores = (soft_grad - soft * delta).astype(jnp.bfloat16)
            sum_value[:keys, :] += matmul_plain(soft.astype(jnp.bfloat16), grads)
            sum_key[:keys, :] += matmul_plain(grad_scores, queries)
            outs.append(matmul_plain(keys_turned[:, :keys], grad_scores))
        head_row = lax.broadcasted_iota(jnp.int32, (LANES, 1), 0)
        turned = jnp.where(head_row < HEAD, outs[0], outs[1]) * HEAD**-0.5
        grad_query_ref[start : start + block, :] = turned.T.astype(jnp.bfloat16)
    grad_key_ref[...] = sum_key[...].astype(jnp.bfloat16)
    grad_value_ref[...] = sum_value[...].astype(jnp.bfloat16)


def attend_grads(joined, grad_mixed, seq_length, block):
    rows, width = joined.shape
    third = width // 3
    pairs = third // LANES
    spec = lambda part: pl.BlockSpec((rows, LANES), lambda p, *_: (0, part * pairs + p))
    out = jax.ShapeDtypeStruct((rows, third), jnp.bfloat16)
    return pl.pallas_call(
        functools.partial(attend_grads_kernel, block=block),
        grid_spec=pltpu.PrefetchScalarGridSpec(
            num_scalar_prefetch=1,
            grid=(pairs,),
            in_specs=[spec(0), spec(1), spec(2), spec(0)],
            out_specs=[spec(0)] * 3,
            scratch_shapes=[pltpu.VMEM((rows, LANES), jnp.float32)] * 2,
        ),
        out_shape=[out] * 3,
        compiler_params=pltpu.CompilerParams(vmem_limit_bytes=VMEM_BYTES),
        name="attend_grads",
    )(seq_length.reshape(1), joined, joined, joined, grad_mixed)


def place_kernel(own_ref, *refs, order, cuts):
    count = len(order)
    for block_ref, indices in zip(refs, order):
        height = block_ref.shape[0] // len(indices)
        for place, index in enumerate(indices):
            target = own_ref[0] ^ index
            for (first_row, rows, first_lane, lanes), out in zip(cuts, refs[count:]):
                first = place * height + first_row
                out[pl.ds(pl.multiple_of(target * rows, 16), rows), :] = block_ref[
                    first : first + rows, first_lane : first_lane + lanes
                ]


def place_blocks(gathered, own, cuts):
    gathered, order = gathered
    return pl.pallas_call(
        functools.partial(place_kernel, order=order, cuts=cuts),
        in_specs=[pl.BlockSpec(memory_space=pltpu.SMEM)]
        + [pl.BlockSpec(memory_space=pltpu.VMEM)] * len(order),
        out_specs=[pl.BlockSpec(memory_space=pltpu.VMEM)] * len(cuts),
        out_shape=[
            jax.ShapeDtypeStruct((8 * rows, lanes), jnp.bfloat16) for _, rows, _, lanes in cuts
        ],
        compiler_params=pltpu.CompilerParams(vmem_limit_bytes=VMEM_BYTES),
        name="place_blocks",
    )(own.reshape(1), *gathered)


def swap(rows, axis, distance):
    count = lax.axis_size(axis)
    return lax.ppermute(rows, axis, [(index, index ^ distance) for index in range(count)])


def swap_low(rows):
    return swap(rows.astype(jnp.bfloat16), VOCAB, 1).astype(jnp.float32)


def in_pair(second, mine, other, axis=0):
    return jnp.where(
        second,
        jnp.concatenate([other, mine], axis=axis),
        jnp.concatenate([mine, other], axis=axis),
    )


def in_order(index, parts):
    low = (index & 1) == 1
    high = (index & 2) == 2
    pairs = [
        [jnp.where(low, parts[k + 1], parts[k]), jnp.where(low, parts[k], parts[k + 1])]
        for k in (0, 2)
    ]
    return [
        jnp.where(high, pairs[1][0], pairs[0][0]),
        jnp.where(high, pairs[1][1], pairs[0][1]),
        jnp.where(high, pairs[0][0], pairs[1][0]),
        jnp.where(high, pairs[0][1], pairs[1][1]),
    ]


def norm_back(inputs, gain_row, grad):
    centred = inputs - jnp.mean(inputs, axis=-1, keepdims=True)
    inverse = lax.rsqrt(jnp.mean(centred * centred, axis=-1, keepdims=True) + 1e-05)
    normal = centred * inverse
    scaled = grad * gain_row
    along = jnp.mean(scaled * normal, axis=-1, keepdims=True)
    result = inverse * (scaled - jnp.mean(scaled, axis=-1, keepdims=True) - normal * along)
    return result, jnp.sum(grad * normal, axis=0), jnp.sum(grad, axis=0)


def gelu_slope(inputs):
    root = math.sqrt(2.0 / math.pi)
    square = inputs * inputs
    bent = jnp.tanh(root * inputs * (1.0 + 0.044715 * square))
    return 0.5 * (1.0 + bent) + 0.5 * inputs * (1.0 - bent * bent) * root * (
        1.0 + 3 * 0.044715 * square
    )


def rows_of(array_in, start, count):
    return lax.dynamic_slice_in_dim(array_in, start, count, 0)


def columns_of(array_in, start, count):
    return lax.dynamic_slice_in_dim(array_in, start, count, 1)


def vector_lines_of(params, seq_length, width):
    short, middle, wide = [
        jnp.stack([jnp.stack([p[k] for k in numbers]) for p in params])
        for numbers in ((0, 1, 5, 6, 7, 11), (3,), (9,))
    ]
    lines = jnp.concatenate(
        [
            jnp.pad(group, ((0, 0), (0, 0), (0, LANES - group.shape[2])))
            for group in (short, middle, wide)
        ],
        axis=1,
    )
    length_parts = jnp.stack([seq_length // 32, seq_length % 32]).astype(jnp.bfloat16)
    length_parts = jnp.broadcast_to(length_parts, lines.shape[:2] + (2,))
    lines = jnp.concatenate([lines, length_parts], axis=2)
    return jnp.pad(lines, ((0, 0), (0, 0), (0, width - lines.shape[2])))


def pack_weights(params, half, lines):
    attend, output, expand, reduce = params[2], params[4], params[8], params[10]
    width = output.shape[1]
    part = width // 2
    wide = expand.shape[1] // 2
    begin = half * part
    front = jnp.concatenate(
        [attend[:, k * width + begin : k * width + begin + part] for k in range(3)], axis=1
    )
    return (
        jnp.concatenate([front, lines], axis=0),
        jnp.concatenate(
            [
                expand[:, start : start + part]
                for start in range(half * wide, (half + 1) * wide, part)
            ]
            + [output[:, begin : begin + part], reduce[:, begin : begin + part]],
            axis=0,
        ),
    )


def exchange_models(slabs):
    index = lax.axis_index(VOCAB)
    stacked = jnp.stack(slabs)
    parts = [lax.dynamic_index_in_dim(stacked, index, 0, keepdims=False)]
    for distance in (1, 2, 3):
        parts.append(
            swap(
                lax.dynamic_index_in_dim(stacked, index ^ distance, 0, keepdims=False),
                VOCAB,
                distance,
            )
        )
    return in_order(index, parts)


def after(value, *others):
    return lax.optimization_barrier((value, others))[0]


def held_after(held, *others):
    return after(held[0], *others), held[1]


def halves_of(axis_name, bit):
    distance = 1 << bit
    return distance, distance * (lax.axis_size(BATCH) if axis_name == BLK else 1)


def double(held, axis_name, bit):
    arrays, order = held
    distance, offset = halves_of(axis_name, bit)
    sent = jnp.concatenate(arrays, axis=0) if len(arrays) > 1 else arrays[0]
    sources = sum(order, ())
    return (
        arrays + (swap(sent, axis_name, distance),),
        order + (tuple(source ^ offset for source in sources),),
    )


def halve_and_see(addends, axis_name, bit, *waits):
    axis = 2 if axis_name == BATCH else 1 - bit
    own = (lax.axis_index(axis_name) >> bit) & 1
    mine = lax.dynamic_slice_in_dim(addends, own, 1, axis)
    theirs = lax.dynamic_slice_in_dim(addends, 1 - own, 1, axis)
    received = swap(theirs.astype(jnp.bfloat16), axis_name, 1 << bit)
    seen = after(received, *waits) if waits else received
    return mine.astype(jnp.float32) + seen.astype(jnp.float32), received


def halve(addends, axis_name, bit, *waits):
    return halve_and_see(addends, axis_name, bit, *waits)[0]


def shards_by_model(hidden, lengths, *rest):
    embedding = rest[26]
    gain_final = rest[24].astype(jnp.float32)
    shift_final = rest[25].astype(jnp.float32)
    params = (rest[:12], rest[12:24])
    blk, batch, member = (lax.axis_index(name) for name in EVERY)
    size_blk, size_batch, size_vocab = (lax.axis_size(name) for name in EVERY)
    plane = blk * size_batch + batch
    model, half = member // 2, member % 2
    is_teacher, is_second = model == 1, half == 1
    rows_local, width = hidden.shape[1:]
    rows = rows_local * size_vocab
    own_rows = rows // 2
    part = width // 2
    ff_part = rest[8].shape[1] // 2
    shard_rows = rest[2].shape[0]
    plane_rows = shard_rows * size_vocab
    crossing = (BLK, VOCAB)

    lines = vector_lines_of(params, lengths[0], 3 * part)
    front_slabs, back_slabs = zip(
        *[pack_weights(params[m], h, lines[m]) for m in (0, 1) for h in (0, 1)]
    )
    front = exchange_models(front_slabs)
    back = exchange_models(after(back_slabs, front))
    length_parts = sum(
        jnp.where(blk == source, front[source][shard_rows, LANES : LANES + 2], 0)
        for source in range(size_vocab)
    ).astype(jnp.int32)
    seq_length = 32 * length_parts[0] + length_parts[1]
    front_block = jnp.concatenate(
        [source[:shard_rows] for source in front] + [source[shard_rows:] for source in front],
        axis=0,
    )
    units = (ff_part + part) // part
    middle_block = jnp.concatenate(
        [
            jnp.concatenate(
                [source[k * shard_rows : (k + 1) * shard_rows] for source in back], axis=0
            )
            for k in range(units)
        ],
        axis=1,
    )
    reduce_block = jnp.concatenate([source[units * shard_rows :] for source in back], axis=0)
    vector_lines = front_block.shape[0] - plane_rows
    reduce_rows = reduce_block.shape[0]

    front_held = double(((front_block,), ((0,),)), BLK, 1)
    middle_held = double(((after(middle_block, front_held[0]),), ((0,),)), BLK, 1)
    reduce_held = double(((after(reduce_block, middle_held[0]),), ((0,),)), BLK, 1)
    turn = [
        (a * size_vocab + b, b * size_vocab + a) for a in range(size_blk) for b in range(size_vocab)
    ]
    quarter = lax.ppermute(after(hidden[0], front_held[0]), crossing, turn)
    quarter_far = swap(quarter, VOCAB, 2)
    quarters = in_order(
        member, [quarter, swap(quarter, VOCAB, 1), quarter_far, swap(quarter_far, VOCAB, 1)]
    )
    front_held = double(front_held, BLK, 0)
    front_held = double(held_after(front_held, middle_held[0]), BATCH, 0)
    middle_held = double(middle_held, BATCH, 0)
    reduce_held = double(reduce_held, BLK, 0)
    attend_weight, vectors = place_blocks(
        front_held,
        plane,
        ((0, plane_rows, 0, 3 * part), (plane_rows, vector_lines, 0, LANES)),
    )

    shards_all = size_blk * size_batch * size_vocab
    vectors = vectors.reshape(shards_all, vector_lines // size_vocab, LANES).astype(jnp.float32)
    first_gain, first_shift, output_bias, second_gain, second_shift, reduce_bias = [
        vectors[:, k, :shard_rows].reshape(width) for k in range(6)
    ]
    attend_bias = vectors[:, 6, : 2 * shard_rows].reshape(2 * width)
    expand_bias = vectors[:, 7, : 4 * shard_rows].reshape(2 * ff_part)
    query_bias = rows_of(attend_bias, half * part, part)
    value_bias = rows_of(attend_bias, width + half * part, part)
    joined_bias = jnp.concatenate([query_bias, jnp.zeros((part,), jnp.float32), value_bias])
    expand_bias = rows_of(expand_bias, half * ff_part, ff_part)

    inputs_low = jnp.concatenate(quarters, axis=0)
    inputs = inputs_low.astype(jnp.float32)
    inputs_own = rows_of(inputs_low, half * own_rows, own_rows).astype(jnp.float32)
    normed_one = layer_norm(inputs, first_gain, first_shift).astype(jnp.bfloat16)
    normed_one = after(normed_one, middle_held[0], reduce_held[0])
    joined = (matmul_plain(normed_one, attend_weight) + joined_bias).astype(jnp.bfloat16)
    block = math.gcd(rows, 256)
    mixed_rows = attend_rows(joined, seq_length, block)
    middle_held = held_after(double(middle_held, BLK, 0), mixed_rows)
    reduce_held = double(reduce_held, BATCH, 0)
    mixed_rows = after(mixed_rows, middle_held[0], reduce_held[0])
    expand_weight, output_columns = place_blocks(
        middle_held, plane, ((0, plane_rows, 0, ff_part), (0, plane_rows, ff_part, part))
    )
    output_weight = in_pair(
        is_second,
        rows_of(output_columns, half * part, part),
        swap(rows_of(output_columns, (1 - half) * part, part), VOCAB, 1),
        axis=1,
    )
    attended = matmul_plain(mixed_rows, output_weight)
    middle = (
        inputs_own
        + rows_of(attended, half * own_rows, own_rows)
        + swap_low(rows_of(attended, (1 - half) * own_rows, own_rows))
        + output_bias
    )
    normed_own = layer_norm(middle, second_gain, second_shift).astype(jnp.bfloat16)
    normed_two = jnp.concatenate([normed_own, swap(normed_own, VOCAB, 1)], axis=0)
    inner_rows = matmul_plain(normed_two, expand_weight) + expand_bias
    active = gelu_tanh(inner_rows).astype(jnp.bfloat16)
    active, slope = lax.optimization_barrier((active, gelu_slope(inner_rows)))
    (reduce_columns,) = place_blocks(reduce_held, plane, ((0, reduce_rows, 0, part),))
    reduce_weight = in_pair(
        is_second,
        rows_of(reduce_columns, half * ff_part, ff_part),
        swap(rows_of(reduce_columns, (1 - half) * ff_part, ff_part), VOCAB, 1),
        axis=1,
    )
    reduced = matmul_plain(active, reduce_weight)
    block_out = middle + reduced[:own_rows] + swap_low(reduced[own_rows:]) + reduce_bias
    final_rows = (0.5 * layer_norm(block_out, gain_final, shift_final)).astype(jnp.bfloat16)

    final_far = swap(final_rows, VOCAB, 2)
    final_parts = jnp.stack(
        [final_rows, swap(final_rows, VOCAB, 1), final_far, swap(final_far, VOCAB, 1)]
    )
    vocab_local = embedding.shape[0]
    valid_columns = jnp.clip(VOCAB_REAL - member * vocab_local, 0, vocab_local)
    logit_student, logit_teacher, stats = vocab_stats(
        final_parts, is_teacher, embedding, valid_columns
    )
    stat_parts = [stats] + [swap(stats, VOCAB, distance) for distance in (1, 2, 3)]
    own_sums, core_sums, divergence_rows = vocab_grads(
        logit_student, logit_teacher, embedding, stat_parts
    )
    positions = jnp.arange(rows, dtype=jnp.int32)
    kl_rows = in_pair(is_second, divergence_rows[0, :own_rows], divergence_rows[0, own_rows:])
    kl_rows = 4.0 * kl_rows * (positions < seq_length).astype(jnp.float32)

    both = own_sums + swap(core_sums, VOCAB, 1).astype(jnp.float32)
    grad_final = jnp.where(is_teacher, both[1], both[0]) + swap(
        jnp.where(is_teacher, both[0], both[1]).astype(jnp.bfloat16), VOCAB, 2
    ).astype(jnp.float32)
    own_valid = (half * own_rows + positions[:own_rows] < seq_length).astype(jnp.float32)
    grad_final = grad_final * (2.0 * own_valid)[:, None]

    grad_out, _, _ = norm_back(block_out, gain_final, grad_final)
    branch_own = grad_out.astype(jnp.bfloat16)
    branch_low = jnp.concatenate([branch_own, swap(branch_own, VOCAB, 1)], axis=0)
    grad_reduce = matmul_left_t(active, branch_low).astype(jnp.bfloat16)
    branch_low = after(branch_low, grad_reduce)
    reduce_other = swap(columns_of(grad_reduce, (1 - half) * part, part), VOCAB, 1)
    grad_reduce = in_pair(is_second, columns_of(grad_reduce, half * part, part), reduce_other)
    grid = (2, 2, 2)
    grad_reduce = grad_reduce.reshape(grid + (reduce_rows, part))
    grad_active = matmul_right_t(branch_low, reduce_weight)
    inner_grad = (grad_active * slope).astype(jnp.bfloat16)
    grad_normed = matmul_right_t(after(inner_grad, reduce_other), expand_weight)
    grad_normed_own = grad_normed[:own_rows] + swap_low(grad_normed[own_rows:])
    middle_part, grad_second_gain, grad_second_shift = norm_back(
        middle, second_gain, grad_normed_own
    )
    grad_middle = grad_out + middle_part
    attn_own = grad_middle.astype(jnp.bfloat16)
    attn_low = in_pair(is_second, attn_own, swap(attn_own, VOCAB, 1))
    grad_mixed = matmul_right_t(attn_low, output_weight).astype(jnp.bfloat16)
    grad_expand = matmul_left_t(normed_two, inner_grad).astype(jnp.bfloat16)
    grad_output = matmul_left_t(mixed_rows, attn_low).astype(jnp.bfloat16)
    grad_output = in_pair(
        is_second,
        columns_of(grad_output, half * part, part),
        swap(columns_of(grad_output, (1 - half) * part, part), VOCAB, 1),
    )
    grad_expand = grad_expand.reshape(grid + (plane_rows, ff_part))
    joined_parts = attend_grads(joined, grad_mixed, seq_length, block)
    reduce_sum = halve(grad_reduce, BATCH, 0, joined_parts[0])
    expand_sum = halve(grad_expand, BLK, 0, joined_parts[0])
    joined_grad = after(jnp.concatenate(joined_parts, axis=1), reduce_sum, expand_sum)
    grad_normed = matmul_right_t(joined_grad, attend_weight)
    grad_attend = matmul_left_t(normed_one, joined_grad).astype(jnp.bfloat16)
    reduce_sum, reduce_seen = halve_and_see(reduce_sum, BLK, 0)
    expand_sum, expand_seen = halve_and_see(expand_sum, BATCH, 0)
    normed_other = after(rows_of(grad_normed, (1 - half) * own_rows, own_rows), reduce_seen, expand_seen)
    normed_other = swap_low(normed_other)
    grad_normed_own = rows_of(grad_normed, half * own_rows, own_rows) + normed_other
    input_part, grad_first_gain, grad_first_shift = norm_back(
        inputs_own, first_gain, grad_normed_own
    )
    grad_inputs = (grad_middle + input_part).reshape(2, rows_local, width)
    input_other = swap(
        jnp.where(is_teacher, grad_inputs[0], grad_inputs[1]).astype(jnp.bfloat16), VOCAB, 2
    )
    input_sum = jnp.where(is_teacher, grad_inputs[1], grad_inputs[0])
    input_sum += input_other.astype(jnp.float32)
    home = [
        (a * size_vocab + 2 * m + h, (2 * h + m) * size_vocab + a)
        for a in range(size_blk)
        for m in (0, 1)
        for h in (0, 1)
    ]
    kl_rows = rows_of(kl_rows, (2 * half + model) * rows_local, rows_local)
    kl_high = kl_rows.astype(jnp.bfloat16)
    kl_low = (kl_rows - kl_high.astype(jnp.float32)).astype(jnp.bfloat16)
    kl_line = jnp.concatenate([kl_high, kl_low])
    kl_line = jnp.pad(kl_line[None], ((0, 7), (0, width - kl_line.shape[0])))
    home_rows = lax.ppermute(
        jnp.concatenate([input_sum.astype(jnp.bfloat16), kl_line], axis=0), crossing, home
    ).astype(jnp.float32)
    input_grad = home_rows[:rows_local]
    kl_out = home_rows[rows_local, :rows_local] + home_rows[rows_local, rows_local : 2 * rows_local]

    bias_sums = column_sums(joined_grad)

    def spread_half(values, count):
        return jnp.where(
            jnp.arange(2)[:, None] == half, values.reshape(1, count), 0.0
        ).reshape(2 * count)

    vector_parts = [
        grad_first_gain,
        grad_first_shift,
        column_sums(attn_own),
        grad_second_gain,
        grad_second_shift,
        column_sums(branch_own),
        jnp.concatenate(
            [spread_half(bias_sums[:part], part), spread_half(bias_sums[2 * part :], part)]
        ),
        spread_half(column_sums(inner_grad), ff_part),
    ]
    vector_grads = jnp.concatenate([v.reshape(shards_all, -1) for v in vector_parts], axis=1)
    vector_grads = jnp.pad(
        vector_grads.reshape(size_blk * size_batch, size_vocab, -1),
        ((0, 0), (0, 4), (0, 3 * part - vector_grads.shape[1])),
    ).astype(jnp.bfloat16)
    grad_front = jnp.concatenate(
        [grad_attend.reshape(size_blk * size_batch, plane_rows, 3 * part), vector_grads], axis=1
    )
    front_sum, seen = halve_and_see(grad_front.reshape(grid + grad_front.shape[1:]), BATCH, 0)
    output_sum = halve(grad_output.reshape(grid + (plane_rows, part)), BLK, 0, input_other)
    output_sum = halve(output_sum, BATCH, 0, seen)
    front_sum, seen = halve_and_see(front_sum, BLK, 0)
    reduce_sum = halve(reduce_sum, BLK, 1, seen)[0, 0, 0]
    expand_sum = halve(expand_sum, BLK, 1, seen)[0, 0, 0]
    output_sum = halve(output_sum, BLK, 1, seen)[0, 0, 0]
    front_sum = halve(front_sum, BLK, 1)[0, 0, 0]

    units = (ff_part + part) // part
    share = reduce_rows // size_vocab
    back = exchange_models(
        [
            jnp.concatenate(
                [
                    expand_sum[t * shard_rows : (t + 1) * shard_rows, k * part : (k + 1) * part]
                    for k in range(units - 1)
                ]
                + [output_sum[t * shard_rows : (t + 1) * shard_rows]]
                + [reduce_sum[t * share : (t + 1) * share]],
                axis=0,
            ).astype(jnp.bfloat16)
            for t in range(size_vocab)
        ]
    )
    front = exchange_models(
        [
            jnp.concatenate(
                [
                    front_sum[t * shard_rows : (t + 1) * shard_rows],
                    jnp.pad(front_sum[plane_rows + t][None], ((0, 7), (0, 0))),
                ],
                axis=0,
            ).astype(jnp.bfloat16)
            for t in range(size_vocab)
        ]
    )
    results = []
    for m in (0, 1):
        sides = front[2 * m : 2 * m + 2]
        vector = sum(side[shard_rows].astype(jnp.float32) for side in sides)
        pieces = [vector[k * shard_rows : (k + 1) * shard_rows] for k in range(6)]
        attend = jnp.concatenate(
            [side[:shard_rows, k * part : (k + 1) * part] for k in range(3) for side in sides],
            axis=1,
        ).astype(jnp.float32)
        sides = back[2 * m : 2 * m + 2]
        output = jnp.concatenate(
            [side[(units - 1) * shard_rows : units * shard_rows] for side in sides], axis=1
        ).astype(jnp.float32)
        expand = jnp.concatenate(
            [
                side[k * shard_rows : (k + 1) * shard_rows]
                for side in sides
                for k in range(units - 1)
            ],
            axis=1,
        ).astype(jnp.float32)
        reduce = jnp.concatenate([side[units * shard_rows :] for side in sides], axis=1)
        reduce = reduce.astype(jnp.float32)
        results += [
            pieces[0],
            pieces[1],
            attend,
            vector[6 * shard_rows : 8 * shard_rows],
            output,
            pieces[2],
            pieces[3],
            pieces[4],
            expand,
            vector[8 * shard_rows : 12 * shard_rows],
            reduce,
            pieces[5],
        ]
    return tuple(results) + (input_grad[None], kl_out[None])


def solution(mesh):
    by_model = mesh.shape[VOCAB] == 4 and mesh.shape[BLK] == 4 and mesh.shape[BATCH] == 2
    return jax.shard_map(
        shards_by_model if by_model else shards,
        mesh=mesh,
        in_specs=(
            P((BATCH, VOCAB), BLK, None),
            P((BATCH, VOCAB)),
            P(EVERY),
            P(EVERY),
            P(EVERY, None),
            P(EVERY),
            P(EVERY, None),
            P(EVERY),
            P(EVERY),
            P(EVERY),
            P(EVERY, None),
            P(EVERY),
            P(EVERY, None),
            P(EVERY),
            P(EVERY),
            P(EVERY),
            P(EVERY, None),
            P(EVERY),
            P(EVERY, None),
            P(EVERY),
            P(EVERY),
            P(EVERY),
            P(EVERY, None),
            P(EVERY),
            P(EVERY, None),
            P(EVERY),
            P(),
            P(),
            P(VOCAB, None),
        ),
        out_specs=(
            P(EVERY),
            P(EVERY),
            P(EVERY, None),
            P(EVERY),
            P(EVERY, None),
            P(EVERY),
            P(EVERY),
            P(EVERY),
            P(EVERY, None),
            P(EVERY),
            P(EVERY, None),
            P(EVERY),
            P(EVERY),
            P(EVERY),
            P(EVERY, None),
            P(EVERY),
            P(EVERY, None),
            P(EVERY),
            P(EVERY),
            P(EVERY),
            P(EVERY, None),
            P(EVERY),
            P(EVERY, None),
            P(EVERY),
            P((BATCH, VOCAB), BLK, None),
            P((BATCH, VOCAB), BLK),
        ),
        check_vma=False,
    )
```

```python
import functools
import math

import jax
import jax.numpy as jnp
from jax import lax
from jax.experimental import pallas as pl
from jax.experimental.pallas import tpu as pltpu
from jax.sharding import PartitionSpec as P

HEADS = 12
HEAD = 64
VOCAB_REAL = 50257
BLK, BATCH, VOCAB = "blk", "batch", "vocab"
EVERY = (BLK, BATCH, VOCAB)


def for_sending(shard):
    return jax.tree.map(lambda a: a.astype(jnp.bfloat16) if a.dtype == jnp.float32 else a, shard)


def layer_norm(inputs, gain_row, shift_row):
    centred = inputs - jnp.mean(inputs, axis=-1, keepdims=True)
    spread = jnp.mean(centred * centred, axis=-1, keepdims=True)
    return centred * lax.rsqrt(spread + 1e-05) * gain_row + shift_row


def gelu_tanh(inputs):
    return jax.nn.gelu(inputs, approximate=True)


def matmul_plain(left_side, right_side):
    return jnp.dot(left_side, right_side, preferred_element_type=jnp.float32)


def matmul_right_t(left_side, right_side):
    return lax.dot_general(
        left_side, right_side, (((1,), (1,)), ((), ())), preferred_element_type=jnp.float32
    )


def matmul_left_t(left_side, right_side):
    return lax.dot_general(
        left_side, right_side, (((0,), (0,)), ((), ())), preferred_element_type=jnp.float32
    )


def column_sums(rows_low):
    return jnp.sum(rows_low.astype(jnp.float32), axis=0)


def split_heads(rows_flat):
    return rows_flat.reshape(rows_flat.shape[0], rows_flat.shape[1], HEADS, HEAD)


def front_half(inputs, params):
    model_width = inputs.shape[-1]
    normed_one = layer_norm(
        inputs, params[0].astype(jnp.float32), params[1].astype(jnp.float32)
    ).astype(jnp.bfloat16)
    joined = matmul_plain(normed_one.reshape(-1, model_width), params[2])
    bias_row = params[3].astype(jnp.float32)
    query_rows = (
        (joined[:, :model_width] + bias_row[:model_width])
        .astype(jnp.bfloat16)
        .reshape(inputs.shape)
    )
    key_rows = joined[:, model_width : 2 * model_width].astype(jnp.bfloat16).reshape(inputs.shape)
    value_rows = (
        (joined[:, 2 * model_width :] + bias_row[model_width:])
        .astype(jnp.bfloat16)
        .reshape(inputs.shape)
    )
    return (normed_one.reshape(-1, model_width), query_rows, key_rows, value_rows)


def attend_block(carried, block_in, first_row, queries, query_pos, seq_lengths):
    head_scale = HEAD ** (-0.5)
    key_count = block_in[0].shape[1]
    key_pos = jnp.arange(key_count, dtype=jnp.int32)
    allowed = (
        (key_pos[None, None, :] <= query_pos[None, :, None])
        & (key_pos[None, None, :] < seq_lengths[:, None, None])
    )[:, None]
    skipped = (first_row > query_pos[-1]) | (first_row >= jnp.max(seq_lengths))

    def attend_update():
        results = []
        for model_index in range(2):
            running, row_max, row_total = carried[model_index]
            key_rows = split_heads(block_in[2 * model_index])
            value_rows = split_heads(block_in[2 * model_index + 1])
            scores = (
                jnp.einsum(
                    "sqhd,skhd->shqk",
                    queries[model_index],
                    key_rows,
                    preferred_element_type=jnp.float32,
                )
                * head_scale
            )
            new_max = jnp.maximum(row_max, jnp.max(jnp.where(allowed, scores, -1e30), axis=-1))
            weights = jnp.where(allowed, jnp.exp(scores - new_max[..., None]), 0.0)
            row_total = jnp.sum(weights, axis=-1)
            running = jnp.einsum(
                "shqk,skhd->shqd",
                weights.astype(jnp.bfloat16),
                value_rows,
                preferred_element_type=jnp.float32,
            )
            results.append((running, new_max, row_total))
        return tuple(results)

    return lax.cond(skipped, lambda: carried, attend_update)


def query_grad_block(
    carried, block_in, first_row, queries, grads_heads, log_totals, deltas, query_pos, seq_lengths
):
    head_scale = HEAD ** (-0.5)
    key_count = block_in[0].shape[1]
    key_pos = jnp.arange(key_count, dtype=jnp.int32)
    allowed = (
        (key_pos[None, None, :] <= query_pos[None, :, None])
        & (key_pos[None, None, :] < seq_lengths[:, None, None])
    )[:, None]
    skipped = (first_row > query_pos[-1]) | (first_row >= jnp.max(seq_lengths))

    def query_update():
        results = []
        for model_index in range(2):
            key_rows = split_heads(block_in[2 * model_index])
            value_rows = split_heads(block_in[2 * model_index + 1])
            scores = (
                jnp.einsum(
                    "sqhd,skhd->shqk",
                    queries[model_index],
                    key_rows,
                    preferred_element_type=jnp.float32,
                )
                * head_scale
            )
            prob_rows = jnp.where(
                allowed, jnp.exp(scores - log_totals[model_index][..., None]), 0.0
            )
            grad_prob = jnp.einsum(
                "sqhd,skhd->shqk",
                grads_heads[model_index],
                value_rows,
                preferred_element_type=jnp.float32,
            )
            grad_scores = (prob_rows * (grad_prob - deltas[model_index][..., None])).astype(
                jnp.bfloat16
            )
            results.append(
                carried[model_index]
                + jnp.einsum(
                    "shqk,skhd->shqd", grad_scores, key_rows, preferred_element_type=jnp.float32
                )
                * head_scale
            )
        return tuple(results)

    return lax.cond(skipped, lambda: carried, query_update)


def key_grad_block(carried, block_in, first_row, keys_local, values_local, key_pos, seq_lengths):
    head_scale = HEAD ** (-0.5)
    query_count = block_in[0].shape[1]
    query_pos = jnp.arange(query_count, dtype=jnp.int32)
    allowed = (
        (key_pos[None, None, :] <= query_pos[None, :, None])
        & (key_pos[None, None, :] < seq_lengths[:, None, None])
    )[:, None]
    skipped = (first_row + query_count - 1 < key_pos[0]) | (key_pos[0] >= jnp.max(seq_lengths))

    def key_update():
        results = []
        for model_index in range(2):
            grad_keys, grad_values = carried[model_index]
            query_rows = split_heads(block_in[4 * model_index])
            grad_rows = split_heads(block_in[4 * model_index + 1])
            log_rows = jnp.transpose(block_in[4 * model_index + 2], (0, 2, 1))
            delta_rows = jnp.transpose(block_in[4 * model_index + 3], (0, 2, 1))
            scores = (
                jnp.einsum(
                    "sqhd,skhd->shqk",
                    query_rows,
                    keys_local[model_index],
                    preferred_element_type=jnp.float32,
                )
                * head_scale
            )
            prob_rows = jnp.where(allowed, jnp.exp(scores - log_rows[..., None]), 0.0)
            grad_values = grad_values + jnp.einsum(
                "shqk,sqhd->shkd",
                prob_rows.astype(jnp.bfloat16),
                grad_rows,
                preferred_element_type=jnp.float32,
            )
            grad_prob = jnp.einsum(
                "sqhd,skhd->shqk",
                grad_rows,
                values_local[model_index],
                preferred_element_type=jnp.float32,
            )
            grad_scores = (prob_rows * (grad_prob - delta_rows[..., None])).astype(jnp.bfloat16)
            grad_keys = (
                grad_keys
                + jnp.einsum(
                    "shqk,sqhd->shkd", grad_scores, query_rows, preferred_element_type=jnp.float32
                )
                * head_scale
            )
            results.append((grad_keys, grad_values))
        return tuple(results)

    return lax.cond(skipped, lambda: carried, key_update)


def shards(
    hidden,
    lengths,
    student_first_gain,
    student_first_shift,
    student_attend_weight,
    student_attend_bias,
    student_output_weight,
    student_output_bias,
    student_second_gain,
    student_second_shift,
    student_expand_weight,
    student_expand_bias,
    student_reduce_weight,
    student_reduce_bias,
    teacher_first_gain,
    teacher_first_shift,
    teacher_attend_weight,
    teacher_attend_bias,
    teacher_output_weight,
    teacher_output_bias,
    teacher_second_gain,
    teacher_second_shift,
    teacher_expand_weight,
    teacher_expand_bias,
    teacher_reduce_weight,
    teacher_reduce_bias,
    final_gain,
    final_shift,
    embedding,
):
    gathered = (
        lax.all_gather(student_first_gain, EVERY, axis=0, tiled=True),
        lax.all_gather(student_first_shift, EVERY, axis=0, tiled=True),
        lax.all_gather(student_attend_weight, EVERY, axis=0, tiled=True),
        lax.all_gather(student_attend_bias, EVERY, axis=0, tiled=True),
        lax.all_gather(student_output_weight, EVERY, axis=0, tiled=True),
        lax.all_gather(student_output_bias, EVERY, axis=0, tiled=True),
        lax.all_gather(student_second_gain, EVERY, axis=0, tiled=True),
        lax.all_gather(student_second_shift, EVERY, axis=0, tiled=True),
        lax.all_gather(student_expand_weight, EVERY, axis=0, tiled=True),
        lax.all_gather(student_expand_bias, EVERY, axis=0, tiled=True),
        lax.all_gather(student_reduce_weight, EVERY, axis=0, tiled=True),
        lax.all_gather(student_reduce_bias, EVERY, axis=0, tiled=True),
        lax.all_gather(teacher_first_gain, EVERY, axis=0, tiled=True),
        lax.all_gather(teacher_first_shift, EVERY, axis=0, tiled=True),
        lax.all_gather(teacher_attend_weight, EVERY, axis=0, tiled=True),
        lax.all_gather(teacher_attend_bias, EVERY, axis=0, tiled=True),
        lax.all_gather(teacher_output_weight, EVERY, axis=0, tiled=True),
        lax.all_gather(teacher_output_bias, EVERY, axis=0, tiled=True),
        lax.all_gather(teacher_second_gain, EVERY, axis=0, tiled=True),
        lax.all_gather(teacher_second_shift, EVERY, axis=0, tiled=True),
        lax.all_gather(teacher_expand_weight, EVERY, axis=0, tiled=True),
        lax.all_gather(teacher_expand_bias, EVERY, axis=0, tiled=True),
        lax.all_gather(teacher_reduce_weight, EVERY, axis=0, tiled=True),
        lax.all_gather(teacher_reduce_bias, EVERY, axis=0, tiled=True),
    )
    models = (tuple(gathered[:12]), tuple(gathered[12:]))
    batch_seqs, rows_local, model_width = hidden.shape
    row_count = batch_seqs * rows_local
    inputs = hidden.astype(jnp.float32)
    inputs_flat = inputs.reshape(row_count, model_width)
    query_pos = lax.axis_index(BLK) * rows_local + jnp.arange(rows_local, dtype=jnp.int32)
    fronts = [front_half(inputs, params) for params in models]
    queries = (split_heads(fronts[0][1]), split_heads(fronts[1][1]))
    zero_heads = jnp.zeros((batch_seqs, HEADS, rows_local, HEAD), jnp.float32)
    zero_rows = jnp.zeros((batch_seqs, HEADS, rows_local), jnp.float32)
    start_state = (
        zero_heads,
        jnp.full((batch_seqs, HEADS, rows_local), -1e30, jnp.float32),
        zero_rows,
    )
    folded = attend_block(
        (start_state, start_state),
        (
            lax.all_gather(fronts[0][2], BLK, axis=1, tiled=True),
            lax.all_gather(fronts[0][3], BLK, axis=1, tiled=True),
            lax.all_gather(fronts[1][2], BLK, axis=1, tiled=True),
            lax.all_gather(fronts[1][3], BLK, axis=1, tiled=True),
        ),
        jnp.int32(0),
        queries,
        query_pos,
        lengths,
    )
    gain_final = final_gain.astype(jnp.float32)
    shift_final = final_shift.astype(jnp.float32)
    caches = []
    final_rows = []
    for model_index in range(2):
        params = models[model_index]
        running, row_max, row_total = folded[model_index]
        mixed_rows = (
            jnp.transpose(running / row_total[..., None], (0, 2, 1, 3))
            .reshape(row_count, model_width)
            .astype(jnp.bfloat16)
        )
        log_total = row_max + jnp.log(row_total)
        middle = inputs_flat + matmul_plain(mixed_rows, params[4]) + params[5].astype(jnp.float32)
        normed_two = layer_norm(
            middle, params[6].astype(jnp.float32), params[7].astype(jnp.float32)
        ).astype(jnp.bfloat16)
        inner_rows = matmul_plain(normed_two, params[8]) + params[9].astype(jnp.float32)
        active = gelu_tanh(inner_rows).astype(jnp.bfloat16)
        block_out = middle + matmul_plain(active, params[10]) + params[11].astype(jnp.float32)
        final_rows.append(layer_norm(block_out, gain_final, shift_final).astype(jnp.bfloat16))
        caches.append((mixed_rows, log_total, middle, normed_two, inner_rows, active, block_out))
    all_rows = lax.all_gather(jnp.stack(final_rows), VOCAB, axis=1, tiled=True)
    vocab_local = embedding.shape[0]
    vocab_index = lax.axis_index(VOCAB)
    column_valid = (
        vocab_index * vocab_local + jnp.arange(vocab_local, dtype=jnp.int32) < VOCAB_REAL
    )[None, :]
    total_rows = all_rows.shape[1]

    def scaled_logits(rows_pair):
        scaled_student = jnp.where(
            column_valid, matmul_right_t(rows_pair[0], embedding) * 0.5, -1e30
        )
        scaled_teacher = jnp.where(
            column_valid, matmul_right_t(rows_pair[1], embedding) * 0.5, -1e30
        )
        return (scaled_student, scaled_teacher)

    stat_rows = math.gcd(total_rows, 512)

    def local_stats(block_index):
        rows_pair = lax.dynamic_slice_in_dim(all_rows, block_index * stat_rows, stat_rows, 1)
        scaled_student, scaled_teacher = scaled_logits(rows_pair)
        max_student = jnp.max(scaled_student, axis=-1)
        max_teacher = jnp.max(scaled_teacher, axis=-1)
        exp_student = jnp.where(column_valid, jnp.exp(scaled_student - max_student[:, None]), 0.0)
        exp_teacher = jnp.where(column_valid, jnp.exp(scaled_teacher - max_teacher[:, None]), 0.0)
        cross_sum = jnp.sum(exp_teacher * (scaled_teacher - scaled_student), axis=-1)
        return (
            max_student,
            jnp.sum(exp_student, axis=-1),
            max_teacher,
            jnp.sum(exp_teacher, axis=-1),
            cross_sum,
        )

    stat_blocks = lax.map(local_stats, jnp.arange(total_rows // stat_rows))
    max_student, sum_student, max_teacher, sum_teacher, cross_sum = [
        stat_block.reshape(total_rows) for stat_block in stat_blocks
    ]
    top_student, top_teacher = lax.pmax((max_student, max_teacher), VOCAB)
    factor_student = jnp.exp(max_student - top_student)
    factor_teacher = jnp.exp(max_teacher - top_teacher)
    sum_student, sum_teacher, cross_sum = lax.psum(
        (sum_student * factor_student, sum_teacher * factor_teacher, cross_sum * factor_teacher),
        VOCAB,
    )
    max_student, max_teacher = (top_student, top_teacher)
    lse_student = max_student + jnp.log(sum_student)
    lse_teacher = max_teacher + jnp.log(sum_teacher)
    divergence_rows = cross_sum / sum_teacher - lse_teacher + lse_student
    valid_rows = (query_pos[None, :] < lengths[:, None]).astype(jnp.float32)
    own_start = vocab_index * row_count
    kl_out = (
        4.0
        * lax.dynamic_slice_in_dim(divergence_rows, own_start, row_count).reshape(
            batch_seqs, rows_local
        )
        * valid_rows
    )
    step_rows = math.gcd(row_count * lax.axis_size(VOCAB), 512)

    def one_block(block_index):
        begin = block_index * step_rows
        rows_pair = lax.dynamic_slice_in_dim(all_rows, begin, step_rows, 1)
        scaled_student, scaled_teacher = scaled_logits(rows_pair)
        log_student = (
            scaled_student - lax.dynamic_slice_in_dim(lse_student, begin, step_rows)[:, None]
        )
        log_teacher = (
            scaled_teacher - lax.dynamic_slice_in_dim(lse_teacher, begin, step_rows)[:, None]
        )
        row_kl = lax.dynamic_slice_in_dim(divergence_rows, begin, step_rows)[:, None]
        prob_student = jnp.where(column_valid, jnp.exp(log_student), 0.0)
        prob_teacher = jnp.where(column_valid, jnp.exp(log_teacher), 0.0)
        grad_student = (2.0 * (prob_student - prob_teacher)).astype(jnp.bfloat16)
        grad_teacher = (2.0 * prob_teacher * (log_teacher - log_student - row_kl)).astype(
            jnp.bfloat16
        )
        return jnp.concatenate(
            [matmul_plain(grad_student, embedding), matmul_plain(grad_teacher, embedding)], axis=1
        )

    grad_final = (
        lax.psum_scatter(
            lax.map(one_block, jnp.arange(row_count * lax.axis_size(VOCAB) // step_rows))
            .reshape(row_count * lax.axis_size(VOCAB), 2 * model_width)
            .astype(jnp.bfloat16),
            VOCAB,
            scatter_dimension=0,
            tiled=True,
        ).astype(jnp.float32)
        * valid_rows.reshape(row_count)[:, None]
    )
    regathered = (
        lax.all_gather(student_first_gain, EVERY, axis=0, tiled=True),
        lax.all_gather(student_first_shift, EVERY, axis=0, tiled=True),
        lax.all_gather(student_attend_weight, EVERY, axis=0, tiled=True),
        lax.all_gather(student_attend_bias, EVERY, axis=0, tiled=True),
        lax.all_gather(student_output_weight, EVERY, axis=0, tiled=True),
        lax.all_gather(student_output_bias, EVERY, axis=0, tiled=True),
        lax.all_gather(student_second_gain, EVERY, axis=0, tiled=True),
        lax.all_gather(student_second_shift, EVERY, axis=0, tiled=True),
        lax.all_gather(student_expand_weight, EVERY, axis=0, tiled=True),
        lax.all_gather(student_expand_bias, EVERY, axis=0, tiled=True),
        lax.all_gather(student_reduce_weight, EVERY, axis=0, tiled=True),
        lax.all_gather(student_reduce_bias, EVERY, axis=0, tiled=True),
        lax.all_gather(teacher_first_gain, EVERY, axis=0, tiled=True),
        lax.all_gather(teacher_first_shift, EVERY, axis=0, tiled=True),
        lax.all_gather(teacher_attend_weight, EVERY, axis=0, tiled=True),
        lax.all_gather(teacher_attend_bias, EVERY, axis=0, tiled=True),
        lax.all_gather(teacher_output_weight, EVERY, axis=0, tiled=True),
        lax.all_gather(teacher_output_bias, EVERY, axis=0, tiled=True),
        lax.all_gather(teacher_second_gain, EVERY, axis=0, tiled=True),
        lax.all_gather(teacher_second_shift, EVERY, axis=0, tiled=True),
        lax.all_gather(teacher_expand_weight, EVERY, axis=0, tiled=True),
        lax.all_gather(teacher_expand_bias, EVERY, axis=0, tiled=True),
        lax.all_gather(teacher_reduce_weight, EVERY, axis=0, tiled=True),
        lax.all_gather(teacher_reduce_bias, EVERY, axis=0, tiled=True),
    )
    back_models = (tuple(regathered[:12]), tuple(regathered[12:]))
    uppers = []
    middle_pairs = []
    for model_index in range(2):
        params = back_models[model_index]
        mixed_rows, log_total, middle, normed_two, inner_rows, active, block_out = caches[
            model_index
        ]
        _, final_pull = jax.vjp(
            lambda rows_in: layer_norm(rows_in, gain_final, shift_final), block_out
        )
        grad_out = final_pull(
            grad_final[:, model_index * model_width : (model_index + 1) * model_width]
        )[0]
        branch_low = grad_out.astype(jnp.bfloat16)
        grad_reduce_bias = column_sums(branch_low)
        grad_active = matmul_right_t(branch_low, params[10])
        _, gelu_pull = jax.vjp(gelu_tanh, inner_rows)
        inner_grad = gelu_pull(grad_active)[0].astype(jnp.bfloat16)
        grad_expand_bias = column_sums(inner_grad)
        grad_normed_two = matmul_right_t(inner_grad, params[8])
        _, second_pull = jax.vjp(
            layer_norm, middle, params[6].astype(jnp.float32), params[7].astype(jnp.float32)
        )
        middle_part, grad_second_gain, grad_second_shift = second_pull(grad_normed_two)
        grad_middle = grad_out + middle_part
        attn_low = grad_middle.astype(jnp.bfloat16)
        grad_output_bias = column_sums(attn_low)
        grad_mixed = matmul_right_t(attn_low, params[4]).astype(jnp.bfloat16)
        delta_rows = jnp.sum(
            (grad_mixed.astype(jnp.float32) * mixed_rows.astype(jnp.float32)).reshape(
                batch_seqs, rows_local, HEADS, HEAD
            ),
            axis=-1,
        )
        uppers.append(
            (
                grad_output_bias,
                grad_second_gain,
                grad_second_shift,
                grad_expand_bias,
                grad_reduce_bias,
                grad_middle,
                grad_mixed.reshape(batch_seqs, rows_local, model_width),
                delta_rows,
            )
        )
        middle_pairs.append(
            ((mixed_rows, attn_low), (normed_two, inner_grad), (active, branch_low))
        )
    grads_heads = (split_heads(uppers[0][6]), split_heads(uppers[1][6]))
    log_totals = (caches[0][1], caches[1][1])
    deltas = (jnp.transpose(uppers[0][7], (0, 2, 1)), jnp.transpose(uppers[1][7], (0, 2, 1)))
    query_grads = query_grad_block(
        (zero_heads, zero_heads),
        (
            lax.all_gather(fronts[0][2], BLK, axis=1, tiled=True),
            lax.all_gather(fronts[0][3], BLK, axis=1, tiled=True),
            lax.all_gather(fronts[1][2], BLK, axis=1, tiled=True),
            lax.all_gather(fronts[1][3], BLK, axis=1, tiled=True),
        ),
        jnp.int32(0),
        queries,
        grads_heads,
        log_totals,
        deltas,
        query_pos,
        lengths,
    )
    keys_local = (split_heads(fronts[0][2]), split_heads(fronts[1][2]))
    values_local = (split_heads(fronts[0][3]), split_heads(fronts[1][3]))
    key_grads = key_grad_block(
        ((zero_heads, zero_heads), (zero_heads, zero_heads)),
        (
            lax.all_gather(fronts[0][1], BLK, axis=1, tiled=True),
            lax.all_gather(uppers[0][6], BLK, axis=1, tiled=True),
            lax.all_gather(
                for_sending(jnp.transpose(log_totals[0], (0, 2, 1))), BLK, axis=1, tiled=True
            ),
            lax.all_gather(uppers[0][7].astype(jnp.bfloat16), BLK, axis=1, tiled=True).astype(
                jnp.float32
            ),
            lax.all_gather(fronts[1][1], BLK, axis=1, tiled=True),
            lax.all_gather(uppers[1][6], BLK, axis=1, tiled=True),
            lax.all_gather(
                for_sending(jnp.transpose(log_totals[1], (0, 2, 1))), BLK, axis=1, tiled=True
            ),
            lax.all_gather(uppers[1][7].astype(jnp.bfloat16), BLK, axis=1, tiled=True).astype(
                jnp.float32
            ),
        ),
        jnp.int32(0),
        keys_local,
        values_local,
        query_pos,
        lengths,
    )
    vectors = []
    pairs = []
    input_grad = jnp.zeros((row_count, model_width), jnp.float32)
    for model_index in range(2):
        params = back_models[model_index]
        upper = uppers[model_index]
        grad_keys, grad_values = key_grads[model_index]
        joined_grad = jnp.concatenate(
            [
                jnp.transpose(query_grads[model_index], (0, 2, 1, 3)).reshape(
                    row_count, model_width
                ),
                jnp.transpose(grad_keys, (0, 2, 1, 3)).reshape(row_count, model_width),
                jnp.transpose(grad_values, (0, 2, 1, 3)).reshape(row_count, model_width),
            ],
            axis=1,
        ).astype(jnp.bfloat16)
        bias_sums = column_sums(joined_grad)
        grad_attend_bias = jnp.concatenate([bias_sums[:model_width], bias_sums[2 * model_width :]])
        grad_normed_one = matmul_right_t(joined_grad, params[2])
        _, first_pull = jax.vjp(
            layer_norm, inputs_flat, params[0].astype(jnp.float32), params[1].astype(jnp.float32)
        )
        input_part, grad_first_gain, grad_first_shift = first_pull(grad_normed_one)
        input_grad = input_grad + upper[5] + input_part
        vectors.append(
            [
                grad_first_gain,
                grad_first_shift,
                grad_attend_bias,
                upper[0],
                upper[1],
                upper[2],
                upper[3],
                upper[4],
            ]
        )
        pairs.append(
            [
                (fronts[model_index][0], joined_grad),
                middle_pairs[model_index][0],
                middle_pairs[model_index][1],
                middle_pairs[model_index][2],
            ]
        )
    grads = []
    for model_index in range(2):
        matrix_list = [matmul_left_t(pair[0], pair[1]) for pair in pairs[model_index]]
        vector_list = vectors[model_index]
        grads.extend(
            [
                vector_list[0],
                vector_list[1],
                matrix_list[0],
                vector_list[2],
                matrix_list[1],
                vector_list[3],
                vector_list[4],
                vector_list[5],
                matrix_list[2],
                vector_list[6],
                matrix_list[3],
                vector_list[7],
            ]
        )
    summed = (
        lax.psum_scatter(grads[0], EVERY, scatter_dimension=0, tiled=True),
        lax.psum_scatter(grads[1], EVERY, scatter_dimension=0, tiled=True),
        lax.psum_scatter(grads[2], EVERY, scatter_dimension=0, tiled=True),
        lax.psum_scatter(grads[3], EVERY, scatter_dimension=0, tiled=True),
        lax.psum_scatter(grads[4], EVERY, scatter_dimension=0, tiled=True),
        lax.psum_scatter(grads[5], EVERY, scatter_dimension=0, tiled=True),
        lax.psum_scatter(grads[6], EVERY, scatter_dimension=0, tiled=True),
        lax.psum_scatter(grads[7], EVERY, scatter_dimension=0, tiled=True),
        lax.psum_scatter(grads[8], EVERY, scatter_dimension=0, tiled=True),
        lax.psum_scatter(grads[9], EVERY, scatter_dimension=0, tiled=True),
        lax.psum_scatter(grads[10], EVERY, scatter_dimension=0, tiled=True),
        lax.psum_scatter(grads[11], EVERY, scatter_dimension=0, tiled=True),
        lax.psum_scatter(grads[12], EVERY, scatter_dimension=0, tiled=True),
        lax.psum_scatter(grads[13], EVERY, scatter_dimension=0, tiled=True),
        lax.psum_scatter(grads[14], EVERY, scatter_dimension=0, tiled=True),
        lax.psum_scatter(grads[15], EVERY, scatter_dimension=0, tiled=True),
        lax.psum_scatter(grads[16], EVERY, scatter_dimension=0, tiled=True),
        lax.psum_scatter(grads[17], EVERY, scatter_dimension=0, tiled=True),
        lax.psum_scatter(grads[18], EVERY, scatter_dimension=0, tiled=True),
        lax.psum_scatter(grads[19], EVERY, scatter_dimension=0, tiled=True),
        lax.psum_scatter(grads[20], EVERY, scatter_dimension=0, tiled=True),
        lax.psum_scatter(grads[21], EVERY, scatter_dimension=0, tiled=True),
        lax.psum_scatter(grads[22], EVERY, scatter_dimension=0, tiled=True),
        lax.psum_scatter(grads[23], EVERY, scatter_dimension=0, tiled=True),
    )
    return tuple(summed) + (input_grad.reshape(batch_seqs, rows_local, model_width), kl_out)


LANES = 128
MARGIN = 16.0
SEQUENCE_AT = (0, 2, 3, 1)
VMEM_BYTES = 60 * 1024 * 1024


def lane_fold(tile_in, combine):
    folded = tile_in[:, :LANES]
    for start in range(LANES, tile_in.shape[1], LANES):
        folded = combine(folded, tile_in[:, start : start + LANES])
    return folded


def whole_block(shape):
    return pl.BlockSpec(shape, lambda *_: (0,) * len(shape))


def vocab_stats_kernel(
    scalars_ref,
    mine_low_ref,
    mine_high_ref,
    far_low_ref,
    far_high_ref,
    embed_ref,
    logit_student_ref,
    logit_teacher_ref,
    stats_ref,
    student_ref,
    teacher_ref,
    tile_max_s,
    tile_max_t,
    max_s,
    max_t,
    sum_s,
    sum_t,
    cross,
    part_s,
    part_t,
    part_x,
    low,
    *,
    tile,
    rows_block,
):
    step_index = pl.program_id(0)
    steps = pl.num_programs(0)
    first = step_index == 0
    half_rows = mine_low_ref.shape[0]
    rows = 2 * half_rows

    def keep(student_parts, teacher_parts):
        for kept, parts in ((student_ref, student_parts), (teacher_ref, teacher_parts)):
            for place, part in enumerate(parts):
                kept[place * half_rows : (place + 1) * half_rows, :] = part[...]

    @pl.when((step_index == 0) & (scalars_ref[1] == 0))
    def _():
        keep((mine_low_ref, mine_high_ref), (far_low_ref, far_high_ref))

    @pl.when((step_index == 0) & (scalars_ref[1] == 1))
    def _():
        keep((far_low_ref, far_high_ref), (mine_low_ref, mine_high_ref))

    @pl.when(step_index == 0)
    def _():
        for total in (max_s, max_t, sum_s, sum_t, cross):
            total[...] = jnp.zeros_like(total)

    def sums(scaled_s, scaled_t, top_s, top_t):
        shifted_s = scaled_s - top_s
        shifted_t = scaled_t - top_t
        exp_s = jnp.exp(shifted_s)
        exp_t = jnp.exp(shifted_t)
        return (
            lane_fold(exp_s, jnp.add),
            lane_fold(exp_t, jnp.add),
            lane_fold(exp_t * (shifted_t - shifted_s), jnp.add),
        )

    def one_tile(masked):
        embed_tile = embed_ref[...]
        excess = None
        for start in range(0, rows, rows_block):
            here = pl.ds(start, rows_block)
            scaled_s = matmul_right_t(student_ref[here, :], embed_tile)
            scaled_t = matmul_right_t(teacher_ref[here, :], embed_tile)
            if masked:
                column = lax.broadcasted_iota(jnp.int32, (1, tile), 1) + step_index * tile
                scaled_s = jnp.where(column < scalars_ref[0], scaled_s, -1e30)
                scaled_t = jnp.where(column < scalars_ref[0], scaled_t, -1e30)
            logit_student_ref[here, :] = scaled_s
            logit_teacher_ref[here, :] = scaled_t
            tops_s = lane_fold(scaled_s, jnp.maximum)
            tops_t = lane_fold(scaled_t, jnp.maximum)
            tile_max_s[here, :] = tops_s
            tile_max_t[here, :] = tops_t
            old_s = max_s[here, :]
            old_t = max_t[here, :]
            part_s[here, :], part_t[here, :], part_x[here, :] = sums(
                scaled_s, scaled_t, old_s[:, :1], old_t[:, :1]
            )
            over = jnp.maximum(tops_s - old_s, tops_t - old_t)
            excess = over if excess is None else jnp.maximum(excess, over)

        low[0] = 0.0

        @pl.when(first)
        def _():
            least_s = jnp.min(jnp.max(tile_max_s[...], axis=1, keepdims=True))
            least_t = jnp.min(jnp.max(tile_max_t[...], axis=1, keepdims=True))
            low[0] = -jnp.minimum(least_s, least_t)

        @pl.when(jnp.maximum(jnp.max(excess), low[0]) > MARGIN)
        def _():
            def rescale(chunk, _):
                here = pl.ds(pl.multiple_of(chunk * 64, 64), 64)
                old_s = max_s[here, :]
                old_t = max_t[here, :]
                top_s = jnp.max(tile_max_s[here, :], axis=1, keepdims=True)
                top_t = jnp.max(tile_max_t[here, :], axis=1, keepdims=True)
                new_s = jnp.broadcast_to(
                    jnp.where(first, top_s, jnp.maximum(old_s[:, :1], top_s)), old_s.shape
                )
                new_t = jnp.broadcast_to(
                    jnp.where(first, top_t, jnp.maximum(old_t[:, :1], top_t)), old_t.shape
                )
                factor_t = jnp.where(first, 0.0, jnp.exp(old_t - new_t))
                moved = (old_t - old_s) - (new_t - new_s)
                max_s[here, :] = new_s
                max_t[here, :] = new_t
                sum_s[here, :] = sum_s[here, :] * jnp.where(first, 0.0, jnp.exp(old_s - new_s))
                cross[here, :] = (cross[here, :] + moved * sum_t[here, :]) * factor_t
                sum_t[here, :] = sum_t[here, :] * factor_t
                part_s[here, :], part_t[here, :], part_x[here, :] = sums(
                    logit_student_ref[here, :],
                    logit_teacher_ref[here, :],
                    new_s[:, :1],
                    new_t[:, :1],
                )
                return 0

            lax.fori_loop(0, rows // 64, rescale, 0)

        sum_s[...] += part_s[...]
        sum_t[...] += part_t[...]
        cross[...] += part_x[...]

    @pl.when(step_index < steps - 1)
    def _():
        one_tile(False)

    @pl.when(step_index == steps - 1)
    def _():
        one_tile(True)
        lane = lax.broadcasted_iota(jnp.int32, (rows, LANES), 1)
        result = jnp.sum(cross[...], axis=1, keepdims=True)
        result = jnp.where(lane == 3, jnp.sum(sum_t[...], axis=1, keepdims=True), result)
        result = jnp.where(lane == 2, jnp.sum(sum_s[...], axis=1, keepdims=True), result)
        result = jnp.where(lane == 0, max_s[...], jnp.where(lane == 1, max_t[...], result))
        stats_ref[...] = result.T[:8, :]


def vocab_stats(final_parts, is_teacher, embedding, valid_columns, tile=1280, rows_block=256):
    half_rows, width = final_parts[0].shape
    rows = 2 * half_rows
    steps = pl.cdiv(embedding.shape[0], tile)
    logits = jax.ShapeDtypeStruct((rows, steps * tile), jnp.float32)
    return pl.pallas_call(
        functools.partial(vocab_stats_kernel, tile=tile, rows_block=rows_block),
        grid_spec=pltpu.PrefetchScalarGridSpec(
            num_scalar_prefetch=1,
            grid=(steps,),
            in_specs=[whole_block((half_rows, width))] * 4
            + [pl.BlockSpec((tile, width), lambda j, *_: (j, 0))],
            out_specs=[
                pl.BlockSpec((rows, tile), lambda j, *_: (0, j)),
                pl.BlockSpec((rows, tile), lambda j, *_: (0, j)),
                whole_block((8, rows)),
            ],
            scratch_shapes=[pltpu.VMEM((rows, width), jnp.bfloat16)] * 2
            + [pltpu.VMEM((rows, LANES), jnp.float32)] * 10
            + [pltpu.SMEM((1,), jnp.float32)],
        ),
        out_shape=[logits, logits, jax.ShapeDtypeStruct((8, rows), jnp.float32)],
        compiler_params=pltpu.CompilerParams(vmem_limit_bytes=VMEM_BYTES),
        name="vocab_stats",
    )(
        jnp.stack([valid_columns, is_teacher.astype(jnp.int32)]),
        *final_parts,
        embedding,
    )


def vocab_grads_kernel(
    logit_student_ref,
    logit_teacher_ref,
    embed_ref,
    *refs,
    tile,
    columns,
    rows_block,
    count,
):
    stat_refs = refs[:count]
    own_ref, send_ref, divergence_ref, row_ref, student_ref, teacher_ref = refs[count:]
    step_index = pl.program_id(0)
    rows = student_ref.shape[0]
    half_rows = rows // 2

    @pl.when(step_index == 0)
    def _():
        student_ref[...] = jnp.zeros_like(student_ref)
        teacher_ref[...] = jnp.zeros_like(teacher_ref)
        parts = []
        for index in range(count):
            part = stat_refs[index][...]
            if index % 2:
                part = jnp.concatenate([part[:, half_rows:], part[:, :half_rows]], axis=1)
            parts.append([part[k : k + 1, :] for k in range(5)])
        top_s = functools.reduce(jnp.maximum, [p[0] for p in parts])
        top_t = functools.reduce(jnp.maximum, [p[1] for p in parts])
        sum_s = sum(p[2] * jnp.exp(p[0] - top_s) for p in parts)
        sum_t = sum(p[3] * jnp.exp(p[1] - top_t) for p in parts)
        cross = sum((p[4] + (p[1] - p[0]) * p[3]) * jnp.exp(p[1] - top_t) for p in parts)
        lse_s = top_s + jnp.log(sum_s)
        lse_t = top_t + jnp.log(sum_t)
        mean_gap = cross / sum_t
        divergence_ref[...] = jnp.broadcast_to(mean_gap - lse_t + lse_s, divergence_ref.shape)
        line = lax.broadcasted_iota(jnp.int32, (LANES, rows), 0)
        row_ref[...] = jnp.where(line == 0, lse_s, jnp.where(line == 1, lse_t, mean_gap)).T

    def one_tile(masked):
        embed_tile = embed_ref[...]
        if masked:
            row = lax.broadcasted_iota(jnp.int32, (tile, 1), 0) + step_index * tile
            embed_tile = jnp.where(row < columns, embed_tile, jnp.zeros_like(embed_tile))
        for start in range(0, rows, rows_block):
            here = pl.ds(start, rows_block)
            scaled_s = logit_student_ref[here, :]
            scaled_t = logit_teacher_ref[here, :]
            prob_s = jnp.exp(scaled_s - row_ref[here, 0:1])
            prob_t = jnp.exp(scaled_t - row_ref[here, 1:2])
            grad_s = (prob_s - prob_t).astype(jnp.bfloat16)
            grad_t = (prob_t * ((scaled_t - scaled_s) - row_ref[here, 2:3])).astype(jnp.bfloat16)
            student_ref[here, :] += matmul_plain(grad_s, embed_tile)
            teacher_ref[here, :] += matmul_plain(grad_t, embed_tile)

    last = pl.num_programs(0) - 1

    @pl.when(step_index < last)
    def _():
        one_tile(False)

    @pl.when(step_index == last)
    def _():
        one_tile(True)
        for index, sums in enumerate((student_ref, teacher_ref)):
            own_ref[index] = sums[:half_rows, :]
            send_ref[index] = sums[half_rows:, :].astype(jnp.bfloat16)


def vocab_grads(logit_student, logit_teacher, embedding, stat_parts, tile=1280, rows_block=256):
    rows = logit_student.shape[0]
    columns, width = embedding.shape
    halves = (2, rows // 2, width)
    return pl.pallas_call(
        functools.partial(
            vocab_grads_kernel,
            tile=tile,
            columns=columns,
            rows_block=rows_block,
            count=len(stat_parts),
        ),
        grid=(pl.cdiv(columns, tile),),
        in_specs=[
            pl.BlockSpec((rows, tile), lambda j: (0, j)),
            pl.BlockSpec((rows, tile), lambda j: (0, j)),
            pl.BlockSpec((tile, width), lambda j: (j, 0)),
        ]
        + [whole_block((8, rows))] * len(stat_parts),
        out_specs=[whole_block(halves), whole_block(halves), whole_block((8, rows))],
        out_shape=[
            jax.ShapeDtypeStruct(halves, jnp.float32),
            jax.ShapeDtypeStruct(halves, jnp.bfloat16),
            jax.ShapeDtypeStruct((8, rows), jnp.float32),
        ],
        scratch_shapes=[
            pltpu.VMEM((rows, LANES), jnp.float32),
            pltpu.VMEM((rows, width), jnp.float32),
            pltpu.VMEM((rows, width), jnp.float32),
        ],
        compiler_params=pltpu.CompilerParams(vmem_limit_bytes=VMEM_BYTES),
        name="vocab_grads",
    )(logit_student, logit_teacher, embedding, *stat_parts)


def attend_kernel(length_ref, query_ref, key_ref, value_ref, mixed_ref, *, block):
    rows = query_ref.shape[0]
    lane = lax.broadcasted_iota(jnp.int32, (1, LANES), 1)
    for start in range(0, rows, block):
        keys = start + block
        key_pos = lax.broadcasted_iota(jnp.int32, (block, keys), 1)
        query_pos = lax.broadcasted_iota(jnp.int32, (block, keys), 0) + start
        allowed = (key_pos <= query_pos) & (key_pos < length_ref[0])
        outs = []
        for head in range(LANES // HEAD):
            own = (lane // HEAD) == head
            queries = query_ref[start : start + block, :] * HEAD**-0.5
            queries = jnp.where(own, queries, jnp.zeros_like(queries))
            scores = matmul_right_t(queries, key_ref[:keys, :])
            scores = jnp.where(allowed, scores, -1e30)
            weights = jnp.exp(scores - jnp.max(scores, axis=1, keepdims=True))
            total = jnp.sum(weights, axis=1, keepdims=True)
            outs.append(
                matmul_plain(weights.astype(jnp.bfloat16), value_ref[:keys, :]) / total
            )
        mixed_ref[start : start + block, :] = jnp.where(lane < HEAD, outs[0], outs[1]).astype(
            jnp.bfloat16
        )


def attend_rows(joined, seq_length, block):
    rows, width = joined.shape
    third = width // 3
    pairs = third // LANES
    spec = lambda part: pl.BlockSpec((rows, LANES), lambda p, *_: (0, part * pairs + p))
    return pl.pallas_call(
        functools.partial(attend_kernel, block=block),
        grid_spec=pltpu.PrefetchScalarGridSpec(
            num_scalar_prefetch=1,
            grid=(pairs,),
            in_specs=[spec(0), spec(1), spec(2)],
            out_specs=spec(0),
        ),
        out_shape=jax.ShapeDtypeStruct((rows, third), jnp.bfloat16),
        compiler_params=pltpu.CompilerParams(vmem_limit_bytes=VMEM_BYTES),
        name="attend",
    )(seq_length.reshape(1), joined, joined, joined)


def attend_grads_kernel(
    length_ref,
    query_ref,
    key_ref,
    value_ref,
    grad_ref,
    grad_query_ref,
    grad_key_ref,
    grad_value_ref,
    sum_key,
    sum_value,
    *,
    block,
):
    rows = query_ref.shape[0]
    lane = lax.broadcasted_iota(jnp.int32, (1, LANES), 1)
    sum_key[...] = jnp.zeros_like(sum_key)
    sum_value[...] = jnp.zeros_like(sum_value)
    keys_turned = key_ref[...].T
    for start in range(0, rows, block):
        keys = start + block
        key_pos = lax.broadcasted_iota(jnp.int32, (keys, block), 0)
        query_pos = lax.broadcasted_iota(jnp.int32, (keys, block), 1) + start
        allowed = (key_pos <= query_pos) & (key_pos < length_ref[0])
        outs = []
        for head in range(LANES // HEAD):
            own = (lane // HEAD) == head
            queries = query_ref[start : start + block, :] * HEAD**-0.5
            queries = jnp.where(own, queries, jnp.zeros_like(queries))
            grads = grad_ref[start : start + block, :]
            grads = jnp.where(own, grads, jnp.zeros_like(grads))
            scores = matmul_right_t(key_ref[:keys, :], queries)
            scores = jnp.where(allowed, scores, -1e30)
            weights = jnp.exp(scores - jnp.max(scores, axis=0, keepdims=True))
            soft = weights * (1.0 / jnp.sum(weights, axis=0, keepdims=True))
            grad_soft = matmul_right_t(value_ref[:keys, :], grads)
            soft_grad = soft * grad_soft
            delta = jnp.sum(soft_grad, axis=0, keepdims=True)
            grad_scores = (soft_grad - soft * delta).astype(jnp.bfloat16)
            sum_value[:keys, :] += matmul_plain(soft.astype(jnp.bfloat16), grads)
            sum_key[:keys, :] += matmul_plain(grad_scores, queries)
            outs.append(matmul_plain(keys_turned[:, :keys], grad_scores))
        head_row = lax.broadcasted_iota(jnp.int32, (LANES, 1), 0)
        turned = jnp.where(head_row < HEAD, outs[0], outs[1]) * HEAD**-0.5
        grad_query_ref[start : start + block, :] = turned.T.astype(jnp.bfloat16)
    grad_key_ref[...] = sum_key[...].astype(jnp.bfloat16)
    grad_value_ref[...] = sum_value[...].astype(jnp.bfloat16)


def attend_grads(joined, grad_mixed, seq_length, block):
    rows, width = joined.shape
    third = width // 3
    pairs = third // LANES
    spec = lambda part: pl.BlockSpec((rows, LANES), lambda p, *_: (0, part * pairs + p))
    out = jax.ShapeDtypeStruct((rows, third), jnp.bfloat16)
    return pl.pallas_call(
        functools.partial(attend_grads_kernel, block=block),
        grid_spec=pltpu.PrefetchScalarGridSpec(
            num_scalar_prefetch=1,
            grid=(pairs,),
            in_specs=[spec(0), spec(1), spec(2), spec(0)],
            out_specs=[spec(0)] * 3,
            scratch_shapes=[pltpu.VMEM((rows, LANES), jnp.float32)] * 2,
        ),
        out_shape=[out] * 3,
        compiler_params=pltpu.CompilerParams(vmem_limit_bytes=VMEM_BYTES),
        name="attend_grads",
    )(seq_length.reshape(1), joined, joined, joined, grad_mixed)


def place_kernel(own_ref, *refs, order, cuts):
    count = len(order)
    for block_ref, indices in zip(refs, order):
        height = block_ref.shape[0] // len(indices)
        for place, index in enumerate(indices):
            target = own_ref[0] ^ index
            for (first_row, rows, first_lane, lanes), out in zip(cuts, refs[count:]):
                first = place * height + first_row
                out[pl.ds(pl.multiple_of(target * rows, 16), rows), :] = block_ref[
                    first : first + rows, first_lane : first_lane + lanes
                ]


def place_blocks(gathered, own, cuts):
    gathered, order = gathered
    return pl.pallas_call(
        functools.partial(place_kernel, order=order, cuts=cuts),
        in_specs=[pl.BlockSpec(memory_space=pltpu.SMEM)]
        + [pl.BlockSpec(memory_space=pltpu.VMEM)] * len(order),
        out_specs=[pl.BlockSpec(memory_space=pltpu.VMEM)] * len(cuts),
        out_shape=[
            jax.ShapeDtypeStruct((8 * rows, lanes), jnp.bfloat16) for _, rows, _, lanes in cuts
        ],
        compiler_params=pltpu.CompilerParams(vmem_limit_bytes=VMEM_BYTES),
        name="place_blocks",
    )(own.reshape(1), *gathered)


def swap(rows, axis, distance):
    count = lax.axis_size(axis)
    return lax.ppermute(rows, axis, [(index, index ^ distance) for index in range(count)])


def swap_low(rows):
    return swap(rows.astype(jnp.bfloat16), VOCAB, 1).astype(jnp.float32)


def in_pair(second, mine, other, axis=0):
    return jnp.where(
        second,
        jnp.concatenate([other, mine], axis=axis),
        jnp.concatenate([mine, other], axis=axis),
    )


def in_order(index, parts):
    low = (index & 1) == 1
    high = (index & 2) == 2
    pairs = [
        [jnp.where(low, parts[k + 1], parts[k]), jnp.where(low, parts[k], parts[k + 1])]
        for k in (0, 2)
    ]
    return [
        jnp.where(high, pairs[1][0], pairs[0][0]),
        jnp.where(high, pairs[1][1], pairs[0][1]),
        jnp.where(high, pairs[0][0], pairs[1][0]),
        jnp.where(high, pairs[0][1], pairs[1][1]),
    ]


def norm_back(inputs, gain_row, grad):
    centred = inputs - jnp.mean(inputs, axis=-1, keepdims=True)
    inverse = lax.rsqrt(jnp.mean(centred * centred, axis=-1, keepdims=True) + 1e-05)
    normal = centred * inverse
    scaled = grad * gain_row
    along = jnp.mean(scaled * normal, axis=-1, keepdims=True)
    result = inverse * (scaled - jnp.mean(scaled, axis=-1, keepdims=True) - normal * along)
    return result, jnp.sum(grad * normal, axis=0), jnp.sum(grad, axis=0)


def gelu_slope(inputs):
    root = math.sqrt(2.0 / math.pi)
    square = inputs * inputs
    bent = jnp.tanh(root * inputs * (1.0 + 0.044715 * square))
    return 0.5 * (1.0 + bent) + 0.5 * inputs * (1.0 - bent * bent) * root * (
        1.0 + 3 * 0.044715 * square
    )


def rows_of(array_in, start, count):
    return lax.dynamic_slice_in_dim(array_in, start, count, 0)


def columns_of(array_in, start, count):
    return lax.dynamic_slice_in_dim(array_in, start, count, 1)


def vector_lines_of(params, seq_length, width):
    short, middle, wide = [
        jnp.stack([jnp.stack([p[k] for k in numbers]) for p in params])
        for numbers in ((0, 1, 5, 6, 7, 11), (3,), (9,))
    ]
    lines = jnp.concatenate(
        [
            jnp.pad(group, ((0, 0), (0, 0), (0, LANES - group.shape[2])))
            for group in (short, middle, wide)
        ],
        axis=1,
    )
    length_parts = jnp.stack([seq_length // 32, seq_length % 32]).astype(jnp.bfloat16)
    length_parts = jnp.broadcast_to(length_parts, lines.shape[:2] + (2,))
    lines = jnp.concatenate([lines, length_parts], axis=2)
    return jnp.pad(lines, ((0, 0), (0, 0), (0, width - lines.shape[2])))


def pack_weights(params, half, lines):
    attend, output, expand, reduce = params[2], params[4], params[8], params[10]
    width = output.shape[1]
    part = width // 2
    wide = expand.shape[1] // 2
    begin = half * part
    front = jnp.concatenate(
        [attend[:, k * width + begin : k * width + begin + part] for k in range(3)], axis=1
    )
    return (
        jnp.concatenate([front, lines], axis=0),
        jnp.concatenate(
            [
                expand[:, start : start + part]
                for start in range(half * wide, (half + 1) * wide, part)
            ]
            + [output[:, begin : begin + part], reduce[:, begin : begin + part]],
            axis=0,
        ),
    )


def exchange_models(slabs):
    index = lax.axis_index(VOCAB)
    stacked = jnp.stack(slabs)
    parts = [lax.dynamic_index_in_dim(stacked, index, 0, keepdims=False)]
    for distance in (1, 2, 3):
        parts.append(
            swap(
                lax.dynamic_index_in_dim(stacked, index ^ distance, 0, keepdims=False),
                VOCAB,
                distance,
            )
        )
    return in_order(index, parts)


def after(value, *others):
    return lax.optimization_barrier((value, others))[0]


def held_after(held, *others):
    return after(held[0], *others), held[1]


def halves_of(axis_name, bit):
    distance = 1 << bit
    return distance, distance * (lax.axis_size(BATCH) if axis_name == BLK else 1)


def double(held, axis_name, bit):
    arrays, order = held
    distance, offset = halves_of(axis_name, bit)
    sent = jnp.concatenate(arrays, axis=0) if len(arrays) > 1 else arrays[0]
    sources = sum(order, ())
    return (
        arrays + (swap(sent, axis_name, distance),),
        order + (tuple(source ^ offset for source in sources),),
    )


def halve_and_see(addends, axis_name, bit, *waits):
    axis = 2 if axis_name == BATCH else 1 - bit
    own = (lax.axis_index(axis_name) >> bit) & 1
    mine = lax.dynamic_slice_in_dim(addends, own, 1, axis)
    theirs = lax.dynamic_slice_in_dim(addends, 1 - own, 1, axis)
    received = swap(theirs.astype(jnp.bfloat16), axis_name, 1 << bit)
    seen = after(received, *waits) if waits else received
    return mine.astype(jnp.float32) + seen.astype(jnp.float32), received


def halve(addends, axis_name, bit, *waits):
    return halve_and_see(addends, axis_name, bit, *waits)[0]


def shards_by_model(hidden, lengths, *rest):
    embedding = rest[26]
    gain_final = rest[24].astype(jnp.float32)
    shift_final = rest[25].astype(jnp.float32)
    params = (rest[:12], rest[12:24])
    blk, batch, member = (lax.axis_index(name) for name in EVERY)
    size_blk, size_batch, size_vocab = (lax.axis_size(name) for name in EVERY)
    plane = blk * size_batch + batch
    model, half = member // 2, member % 2
    is_teacher, is_second = model == 1, half == 1
    rows_local, width = hidden.shape[1:]
    rows = rows_local * size_vocab
    own_rows = rows // 2
    part = width // 2
    ff_part = rest[8].shape[1] // 2
    shard_rows = rest[2].shape[0]
    plane_rows = shard_rows * size_vocab
    crossing = (BLK, VOCAB)

    lines = vector_lines_of(params, lengths[0], 3 * part)
    front_slabs, back_slabs = zip(
        *[pack_weights(params[m], h, lines[m]) for m in (0, 1) for h in (0, 1)]
    )
    front = exchange_models(front_slabs)
    back = exchange_models(after(back_slabs, front))
    length_parts = sum(
        jnp.where(blk == place, front[source][shard_rows, LANES : LANES + 2], 0)
        for place, source in enumerate(SEQUENCE_AT)
    ).astype(jnp.int32)
    seq_length = 32 * length_parts[0] + length_parts[1]
    front_block = jnp.concatenate(
        [source[:shard_rows] for source in front] + [source[shard_rows:] for source in front],
        axis=0,
    )
    units = (ff_part + part) // part
    middle_block = jnp.concatenate(
        [
            jnp.concatenate(
                [source[k * shard_rows : (k + 1) * shard_rows] for source in back], axis=0
            )
            for k in range(units)
        ],
        axis=1,
    )
    reduce_block = jnp.concatenate([source[units * shard_rows :] for source in back], axis=0)
    vector_lines = front_block.shape[0] - plane_rows
    reduce_rows = reduce_block.shape[0]

    front_held = double(((front_block,), ((0,),)), BLK, 1)
    middle_held = double(((after(middle_block, front_held[0]),), ((0,),)), BLK, 1)
    reduce_held = double(((after(reduce_block, middle_held[0]),), ((0,),)), BLK, 1)
    turn = [
        (a * size_vocab + SEQUENCE_AT[b], b * size_vocab + a)
        for a in range(size_blk)
        for b in range(size_vocab)
    ]
    front_held = double(front_held, BLK, 0)
    quarter = lax.ppermute(after(hidden[0], front_held[0]), crossing, turn)
    quarter_far = swap(quarter, VOCAB, 2)
    quarters = in_order(
        member, [quarter, swap(quarter, VOCAB, 1), quarter_far, swap(quarter_far, VOCAB, 1)]
    )
    front_held = double(held_after(front_held, middle_held[0]), BATCH, 0)
    middle_held = double(middle_held, BATCH, 0)
    reduce_held = double(reduce_held, BLK, 0)
    attend_weight, vectors = place_blocks(
        front_held,
        plane,
        ((0, plane_rows, 0, 3 * part), (plane_rows, vector_lines, 0, LANES)),
    )

    shards_all = size_blk * size_batch * size_vocab
    vectors = vectors.reshape(shards_all, vector_lines // size_vocab, LANES).astype(jnp.float32)
    first_gain, first_shift, output_bias, second_gain, second_shift, reduce_bias = [
        vectors[:, k, :shard_rows].reshape(width) for k in range(6)
    ]
    attend_bias = vectors[:, 6, : 2 * shard_rows].reshape(2 * width)
    expand_bias = vectors[:, 7, : 4 * shard_rows].reshape(2 * ff_part)
    query_bias = rows_of(attend_bias, half * part, part)
    value_bias = rows_of(attend_bias, width + half * part, part)
    joined_bias = jnp.concatenate([query_bias, jnp.zeros((part,), jnp.float32), value_bias])
    expand_bias = rows_of(expand_bias, half * ff_part, ff_part)

    inputs_low = jnp.concatenate(quarters, axis=0)
    inputs = inputs_low.astype(jnp.float32)
    inputs_own = rows_of(inputs_low, half * own_rows, own_rows).astype(jnp.float32)
    normed_one = layer_norm(inputs, first_gain, first_shift).astype(jnp.bfloat16)
    normed_one = after(normed_one, middle_held[0], reduce_held[0])
    joined = (matmul_plain(normed_one, attend_weight) + joined_bias).astype(jnp.bfloat16)
    block = math.gcd(rows, 256)
    mixed_rows = attend_rows(joined, seq_length, block)
    middle_held = held_after(double(middle_held, BLK, 0), mixed_rows)
    reduce_held = double(reduce_held, BATCH, 0)
    mixed_rows = after(mixed_rows, middle_held[0], reduce_held[0])
    expand_weight, output_columns = place_blocks(
        middle_held, plane, ((0, plane_rows, 0, ff_part), (0, plane_rows, ff_part, part))
    )
    output_weight = in_pair(
        is_second,
        rows_of(output_columns, half * part, part),
        swap(rows_of(output_columns, (1 - half) * part, part), VOCAB, 1),
        axis=1,
    )
    attended = matmul_plain(mixed_rows, output_weight)
    middle = (
        inputs_own
        + rows_of(attended, half * own_rows, own_rows)
        + swap_low(rows_of(attended, (1 - half) * own_rows, own_rows))
        + output_bias
    )
    normed_own = layer_norm(middle, second_gain, second_shift).astype(jnp.bfloat16)
    normed_two = jnp.concatenate([normed_own, swap(normed_own, VOCAB, 1)], axis=0)
    inner_rows = matmul_plain(normed_two, expand_weight) + expand_bias
    active = gelu_tanh(inner_rows).astype(jnp.bfloat16)
    active, slope = lax.optimization_barrier((active, gelu_slope(inner_rows)))
    (reduce_columns,) = place_blocks(reduce_held, plane, ((0, reduce_rows, 0, part),))
    reduce_weight = in_pair(
        is_second,
        rows_of(reduce_columns, half * ff_part, ff_part),
        swap(rows_of(reduce_columns, (1 - half) * ff_part, ff_part), VOCAB, 1),
        axis=1,
    )
    reduced = matmul_plain(active, reduce_weight)
    block_out = middle + reduced[:own_rows] + swap_low(reduced[own_rows:]) + reduce_bias
    final_rows = (0.5 * layer_norm(block_out, gain_final, shift_final)).astype(jnp.bfloat16)

    final_far = swap(final_rows, VOCAB, 2)
    final_parts = (final_rows, swap(final_rows, VOCAB, 1), final_far, swap(final_far, VOCAB, 1))
    vocab_local = embedding.shape[0]
    valid_columns = jnp.clip(VOCAB_REAL - member * vocab_local, 0, vocab_local)
    logit_student, logit_teacher, stats = vocab_stats(
        final_parts, is_teacher, embedding, valid_columns
    )
    stat_parts = [stats] + [swap(stats, VOCAB, distance) for distance in (1, 2, 3)]
    own_sums, core_sums, divergence_rows = vocab_grads(
        logit_student, logit_teacher, embedding, stat_parts
    )
    positions = jnp.arange(rows, dtype=jnp.int32)
    kl_rows = in_pair(is_second, divergence_rows[0, :own_rows], divergence_rows[0, own_rows:])
    kl_rows = 4.0 * kl_rows * (positions < seq_length).astype(jnp.float32)

    both = own_sums + swap(core_sums, VOCAB, 1).astype(jnp.float32)
    grad_final = jnp.where(is_teacher, both[1], both[0]) + swap(
        jnp.where(is_teacher, both[0], both[1]).astype(jnp.bfloat16), VOCAB, 2
    ).astype(jnp.float32)
    own_valid = (half * own_rows + positions[:own_rows] < seq_length).astype(jnp.float32)
    grad_final = grad_final * (2.0 * own_valid)[:, None]

    grad_out, _, _ = norm_back(block_out, gain_final, grad_final)
    branch_own = grad_out.astype(jnp.bfloat16)
    branch_low = jnp.concatenate([branch_own, swap(branch_own, VOCAB, 1)], axis=0)
    grad_reduce = matmul_left_t(active, branch_low).astype(jnp.bfloat16)
    branch_low = after(branch_low, grad_reduce)
    reduce_other = swap(columns_of(grad_reduce, (1 - half) * part, part), VOCAB, 1)
    grad_reduce = in_pair(is_second, columns_of(grad_reduce, half * part, part), reduce_other)
    grid = (2, 2, 2)
    grad_reduce = grad_reduce.reshape(grid + (reduce_rows, part))
    grad_active = matmul_right_t(branch_low, reduce_weight)
    inner_grad = (grad_active * slope).astype(jnp.bfloat16)
    grad_normed = matmul_right_t(after(inner_grad, reduce_other), expand_weight)
    grad_normed_own = grad_normed[:own_rows] + swap_low(grad_normed[own_rows:])
    middle_part, grad_second_gain, grad_second_shift = norm_back(
        middle, second_gain, grad_normed_own
    )
    grad_middle = grad_out + middle_part
    attn_own = grad_middle.astype(jnp.bfloat16)
    attn_low = in_pair(is_second, attn_own, swap(attn_own, VOCAB, 1))
    grad_mixed = matmul_right_t(attn_low, output_weight).astype(jnp.bfloat16)
    grad_expand = matmul_left_t(normed_two, inner_grad).astype(jnp.bfloat16)
    grad_output = matmul_left_t(mixed_rows, attn_low).astype(jnp.bfloat16)
    grad_output = in_pair(
        is_second,
        columns_of(grad_output, half * part, part),
        swap(columns_of(grad_output, (1 - half) * part, part), VOCAB, 1),
    )
    grad_expand = grad_expand.reshape(grid + (plane_rows, ff_part))
    joined_parts = attend_grads(joined, grad_mixed, seq_length, block)
    reduce_sum = halve(grad_reduce, BATCH, 0, joined_parts[0])
    expand_sum = halve(grad_expand, BLK, 0, joined_parts[0])
    joined_grad = after(jnp.concatenate(joined_parts, axis=1), reduce_sum, expand_sum)
    grad_normed = matmul_right_t(joined_grad, attend_weight)
    grad_attend = matmul_left_t(normed_one, joined_grad).astype(jnp.bfloat16)
    reduce_sum, reduce_seen = halve_and_see(reduce_sum, BLK, 0)
    expand_sum, expand_seen = halve_and_see(expand_sum, BATCH, 0)
    normed_other = after(rows_of(grad_normed, (1 - half) * own_rows, own_rows), reduce_seen, expand_seen)
    normed_other = swap_low(normed_other)
    grad_normed_own = rows_of(grad_normed, half * own_rows, own_rows) + normed_other
    input_part, grad_first_gain, grad_first_shift = norm_back(
        inputs_own, first_gain, grad_normed_own
    )
    grad_inputs = (grad_middle + input_part).reshape(2, rows_local, width)
    input_other = swap(
        jnp.where(is_teacher, grad_inputs[0], grad_inputs[1]).astype(jnp.bfloat16), VOCAB, 2
    )
    input_sum = jnp.where(is_teacher, grad_inputs[1], grad_inputs[0])
    input_sum += input_other.astype(jnp.float32)
    home = [
        (a * size_vocab + 2 * m + h, (2 * h + m) * size_vocab + SEQUENCE_AT[a])
        for a in range(size_blk)
        for m in (0, 1)
        for h in (0, 1)
    ]
    kl_rows = rows_of(kl_rows, (2 * half + model) * rows_local, rows_local)
    kl_high = kl_rows.astype(jnp.bfloat16)
    kl_low = (kl_rows - kl_high.astype(jnp.float32)).astype(jnp.bfloat16)
    kl_line = jnp.concatenate([kl_high, kl_low])
    kl_line = jnp.pad(kl_line[None], ((0, 7), (0, width - kl_line.shape[0])))
    home_rows = lax.ppermute(
        jnp.concatenate([input_sum.astype(jnp.bfloat16), kl_line], axis=0), crossing, home
    ).astype(jnp.float32)
    input_grad = home_rows[:rows_local]
    kl_out = home_rows[rows_local, :rows_local] + home_rows[rows_local, rows_local : 2 * rows_local]

    bias_sums = column_sums(joined_grad)

    def spread_half(values, count):
        return jnp.where(
            jnp.arange(2)[:, None] == half, values.reshape(1, count), 0.0
        ).reshape(2 * count)

    vector_parts = [
        grad_first_gain,
        grad_first_shift,
        column_sums(attn_own),
        grad_second_gain,
        grad_second_shift,
        column_sums(branch_own),
        jnp.concatenate(
            [spread_half(bias_sums[:part], part), spread_half(bias_sums[2 * part :], part)]
        ),
        spread_half(column_sums(inner_grad), ff_part),
    ]
    vector_grads = jnp.concatenate([v.reshape(shards_all, -1) for v in vector_parts], axis=1)
    vector_grads = jnp.pad(
        vector_grads.reshape(size_blk * size_batch, size_vocab, -1),
        ((0, 0), (0, 4), (0, 3 * part - vector_grads.shape[1])),
    ).astype(jnp.bfloat16)
    grad_front = jnp.concatenate(
        [grad_attend.reshape(size_blk * size_batch, plane_rows, 3 * part), vector_grads], axis=1
    )
    front_sum, seen = halve_and_see(grad_front.reshape(grid + grad_front.shape[1:]), BATCH, 0)
    output_sum = halve(grad_output.reshape(grid + (plane_rows, part)), BLK, 0, input_other)
    output_sum = halve(output_sum, BATCH, 0, seen)
    front_sum, seen = halve_and_see(front_sum, BLK, 0)
    reduce_sum = halve(reduce_sum, BLK, 1, seen)[0, 0, 0]
    expand_sum = halve(expand_sum, BLK, 1, seen)[0, 0, 0]
    output_sum = halve(output_sum, BLK, 1, seen)[0, 0, 0]
    front_sum = halve(front_sum, BLK, 1)[0, 0, 0]

    units = (ff_part + part) // part
    share = reduce_rows // size_vocab
    back = exchange_models(
        [
            jnp.concatenate(
                [
                    expand_sum[t * shard_rows : (t + 1) * shard_rows, k * part : (k + 1) * part]
                    for k in range(units - 1)
                ]
                + [output_sum[t * shard_rows : (t + 1) * shard_rows]]
                + [reduce_sum[t * share : (t + 1) * share]],
                axis=0,
            ).astype(jnp.bfloat16)
            for t in range(size_vocab)
        ]
    )
    front = exchange_models(
        [
            jnp.concatenate(
                [
                    front_sum[t * shard_rows : (t + 1) * shard_rows],
                    jnp.pad(front_sum[plane_rows + t][None], ((0, 7), (0, 0))),
                ],
                axis=0,
            ).astype(jnp.bfloat16)
            for t in range(size_vocab)
        ]
    )
    results = []
    for m in (0, 1):
        sides = front[2 * m : 2 * m + 2]
        vector = sum(side[shard_rows].astype(jnp.float32) for side in sides)
        pieces = [vector[k * shard_rows : (k + 1) * shard_rows] for k in range(6)]
        attend = jnp.concatenate(
            [side[:shard_rows, k * part : (k + 1) * part] for k in range(3) for side in sides],
            axis=1,
        ).astype(jnp.float32)
        sides = back[2 * m : 2 * m + 2]
        output = jnp.concatenate(
            [side[(units - 1) * shard_rows : units * shard_rows] for side in sides], axis=1
        ).astype(jnp.float32)
        expand = jnp.concatenate(
            [
                side[k * shard_rows : (k + 1) * shard_rows]
                for side in sides
                for k in range(units - 1)
            ],
            axis=1,
        ).astype(jnp.float32)
        reduce = jnp.concatenate([side[units * shard_rows :] for side in sides], axis=1)
        reduce = reduce.astype(jnp.float32)
        results += [
            pieces[0],
            pieces[1],
            attend,
            vector[6 * shard_rows : 8 * shard_rows],
            output,
            pieces[2],
            pieces[3],
            pieces[4],
            expand,
            vector[8 * shard_rows : 12 * shard_rows],
            reduce,
            pieces[5],
        ]
    return tuple(results) + (input_grad[None], kl_out[None])


def solution(mesh):
    by_model = mesh.shape[VOCAB] == 4 and mesh.shape[BLK] == 4 and mesh.shape[BATCH] == 2
    return jax.shard_map(
        shards_by_model if by_model else shards,
        mesh=mesh,
        in_specs=(
            P((BATCH, VOCAB), BLK, None),
            P((BATCH, VOCAB)),
            P(EVERY),
            P(EVERY),
            P(EVERY, None),
            P(EVERY),
            P(EVERY, None),
            P(EVERY),
            P(EVERY),
            P(EVERY),
            P(EVERY, None),
            P(EVERY),
            P(EVERY, None),
            P(EVERY),
            P(EVERY),
            P(EVERY),
            P(EVERY, None),
            P(EVERY),
            P(EVERY, None),
            P(EVERY),
            P(EVERY),
            P(EVERY),
            P(EVERY, None),
            P(EVERY),
            P(EVERY, None),
            P(EVERY),
            P(),
            P(),
            P(VOCAB, None),
        ),
        out_specs=(
            P(EVERY),
            P(EVERY),
            P(EVERY, None),
            P(EVERY),
            P(EVERY, None),
            P(EVERY),
            P(EVERY),
            P(EVERY),
            P(EVERY, None),
            P(EVERY),
            P(EVERY, None),
            P(EVERY),
            P(EVERY),
            P(EVERY),
            P(EVERY, None),
            P(EVERY),
            P(EVERY, None),
            P(EVERY),
            P(EVERY),
            P(EVERY),
            P(EVERY, None),
            P(EVERY),
            P(EVERY, None),
            P(EVERY),
            P((BATCH, VOCAB), BLK, None),
            P((BATCH, VOCAB), BLK),
        ),
        check_vma=False,
    )
```

```python
import functools
import math

import jax
import jax.numpy as jnp
from jax import lax
from jax.experimental import pallas as pl
from jax.experimental.pallas import tpu as pltpu
from jax.sharding import PartitionSpec as P

HEADS = 12
HEAD = 64
VOCAB_REAL = 50257
BLK, BATCH, VOCAB = "blk", "batch", "vocab"
EVERY = (BLK, BATCH, VOCAB)


def for_sending(shard):
    return jax.tree.map(lambda a: a.astype(jnp.bfloat16) if a.dtype == jnp.float32 else a, shard)


def layer_norm(inputs, gain_row, shift_row):
    centred = inputs - jnp.mean(inputs, axis=-1, keepdims=True)
    spread = jnp.mean(centred * centred, axis=-1, keepdims=True)
    return centred * lax.rsqrt(spread + 1e-05) * gain_row + shift_row


def gelu_tanh(inputs):
    return jax.nn.gelu(inputs, approximate=True)


def matmul_plain(left_side, right_side):
    return jnp.dot(left_side, right_side, preferred_element_type=jnp.float32)


def matmul_right_t(left_side, right_side):
    return lax.dot_general(
        left_side, right_side, (((1,), (1,)), ((), ())), preferred_element_type=jnp.float32
    )


def matmul_left_t(left_side, right_side):
    return lax.dot_general(
        left_side, right_side, (((0,), (0,)), ((), ())), preferred_element_type=jnp.float32
    )


def column_sums(rows_low):
    return jnp.sum(rows_low.astype(jnp.float32), axis=0)


def split_heads(rows_flat):
    return rows_flat.reshape(rows_flat.shape[0], rows_flat.shape[1], HEADS, HEAD)


def front_half(inputs, params):
    model_width = inputs.shape[-1]
    normed_one = layer_norm(
        inputs, params[0].astype(jnp.float32), params[1].astype(jnp.float32)
    ).astype(jnp.bfloat16)
    joined = matmul_plain(normed_one.reshape(-1, model_width), params[2])
    bias_row = params[3].astype(jnp.float32)
    query_rows = (
        (joined[:, :model_width] + bias_row[:model_width])
        .astype(jnp.bfloat16)
        .reshape(inputs.shape)
    )
    key_rows = joined[:, model_width : 2 * model_width].astype(jnp.bfloat16).reshape(inputs.shape)
    value_rows = (
        (joined[:, 2 * model_width :] + bias_row[model_width:])
        .astype(jnp.bfloat16)
        .reshape(inputs.shape)
    )
    return (normed_one.reshape(-1, model_width), query_rows, key_rows, value_rows)


def attend_block(carried, block_in, first_row, queries, query_pos, seq_lengths):
    head_scale = HEAD ** (-0.5)
    key_count = block_in[0].shape[1]
    key_pos = jnp.arange(key_count, dtype=jnp.int32)
    allowed = (
        (key_pos[None, None, :] <= query_pos[None, :, None])
        & (key_pos[None, None, :] < seq_lengths[:, None, None])
    )[:, None]
    skipped = (first_row > query_pos[-1]) | (first_row >= jnp.max(seq_lengths))

    def attend_update():
        results = []
        for model_index in range(2):
            running, row_max, row_total = carried[model_index]
            key_rows = split_heads(block_in[2 * model_index])
            value_rows = split_heads(block_in[2 * model_index + 1])
            scores = (
                jnp.einsum(
                    "sqhd,skhd->shqk",
                    queries[model_index],
                    key_rows,
                    preferred_element_type=jnp.float32,
                )
                * head_scale
            )
            new_max = jnp.maximum(row_max, jnp.max(jnp.where(allowed, scores, -1e30), axis=-1))
            weights = jnp.where(allowed, jnp.exp(scores - new_max[..., None]), 0.0)
            row_total = jnp.sum(weights, axis=-1)
            running = jnp.einsum(
                "shqk,skhd->shqd",
                weights.astype(jnp.bfloat16),
                value_rows,
                preferred_element_type=jnp.float32,
            )
            results.append((running, new_max, row_total))
        return tuple(results)

    return lax.cond(skipped, lambda: carried, attend_update)


def query_grad_block(
    carried, block_in, first_row, queries, grads_heads, log_totals, deltas, query_pos, seq_lengths
):
    head_scale = HEAD ** (-0.5)
    key_count = block_in[0].shape[1]
    key_pos = jnp.arange(key_count, dtype=jnp.int32)
    allowed = (
        (key_pos[None, None, :] <= query_pos[None, :, None])
        & (key_pos[None, None, :] < seq_lengths[:, None, None])
    )[:, None]
    skipped = (first_row > query_pos[-1]) | (first_row >= jnp.max(seq_lengths))

    def query_update():
        results = []
        for model_index in range(2):
            key_rows = split_heads(block_in[2 * model_index])
            value_rows = split_heads(block_in[2 * model_index + 1])
            scores = (
                jnp.einsum(
                    "sqhd,skhd->shqk",
                    queries[model_index],
                    key_rows,
                    preferred_element_type=jnp.float32,
                )
                * head_scale
            )
            prob_rows = jnp.where(
                allowed, jnp.exp(scores - log_totals[model_index][..., None]), 0.0
            )
            grad_prob = jnp.einsum(
                "sqhd,skhd->shqk",
                grads_heads[model_index],
                value_rows,
                preferred_element_type=jnp.float32,
            )
            grad_scores = (prob_rows * (grad_prob - deltas[model_index][..., None])).astype(
                jnp.bfloat16
            )
            results.append(
                carried[model_index]
                + jnp.einsum(
                    "shqk,skhd->shqd", grad_scores, key_rows, preferred_element_type=jnp.float32
                )
                * head_scale
            )
        return tuple(results)

    return lax.cond(skipped, lambda: carried, query_update)


def key_grad_block(carried, block_in, first_row, keys_local, values_local, key_pos, seq_lengths):
    head_scale = HEAD ** (-0.5)
    query_count = block_in[0].shape[1]
    query_pos = jnp.arange(query_count, dtype=jnp.int32)
    allowed = (
        (key_pos[None, None, :] <= query_pos[None, :, None])
        & (key_pos[None, None, :] < seq_lengths[:, None, None])
    )[:, None]
    skipped = (first_row + query_count - 1 < key_pos[0]) | (key_pos[0] >= jnp.max(seq_lengths))

    def key_update():
        results = []
        for model_index in range(2):
            grad_keys, grad_values = carried[model_index]
            query_rows = split_heads(block_in[4 * model_index])
            grad_rows = split_heads(block_in[4 * model_index + 1])
            log_rows = jnp.transpose(block_in[4 * model_index + 2], (0, 2, 1))
            delta_rows = jnp.transpose(block_in[4 * model_index + 3], (0, 2, 1))
            scores = (
                jnp.einsum(
                    "sqhd,skhd->shqk",
                    query_rows,
                    keys_local[model_index],
                    preferred_element_type=jnp.float32,
                )
                * head_scale
            )
            prob_rows = jnp.where(allowed, jnp.exp(scores - log_rows[..., None]), 0.0)
            grad_values = grad_values + jnp.einsum(
                "shqk,sqhd->shkd",
                prob_rows.astype(jnp.bfloat16),
                grad_rows,
                preferred_element_type=jnp.float32,
            )
            grad_prob = jnp.einsum(
                "sqhd,skhd->shqk",
                grad_rows,
                values_local[model_index],
                preferred_element_type=jnp.float32,
            )
            grad_scores = (prob_rows * (grad_prob - delta_rows[..., None])).astype(jnp.bfloat16)
            grad_keys = (
                grad_keys
                + jnp.einsum(
                    "shqk,sqhd->shkd", grad_scores, query_rows, preferred_element_type=jnp.float32
                )
                * head_scale
            )
            results.append((grad_keys, grad_values))
        return tuple(results)

    return lax.cond(skipped, lambda: carried, key_update)


def shards(
    hidden,
    lengths,
    student_first_gain,
    student_first_shift,
    student_attend_weight,
    student_attend_bias,
    student_output_weight,
    student_output_bias,
    student_second_gain,
    student_second_shift,
    student_expand_weight,
    student_expand_bias,
    student_reduce_weight,
    student_reduce_bias,
    teacher_first_gain,
    teacher_first_shift,
    teacher_attend_weight,
    teacher_attend_bias,
    teacher_output_weight,
    teacher_output_bias,
    teacher_second_gain,
    teacher_second_shift,
    teacher_expand_weight,
    teacher_expand_bias,
    teacher_reduce_weight,
    teacher_reduce_bias,
    final_gain,
    final_shift,
    embedding,
):
    gathered = (
        lax.all_gather(student_first_gain, EVERY, axis=0, tiled=True),
        lax.all_gather(student_first_shift, EVERY, axis=0, tiled=True),
        lax.all_gather(student_attend_weight, EVERY, axis=0, tiled=True),
        lax.all_gather(student_attend_bias, EVERY, axis=0, tiled=True),
        lax.all_gather(student_output_weight, EVERY, axis=0, tiled=True),
        lax.all_gather(student_output_bias, EVERY, axis=0, tiled=True),
        lax.all_gather(student_second_gain, EVERY, axis=0, tiled=True),
        lax.all_gather(student_second_shift, EVERY, axis=0, tiled=True),
        lax.all_gather(student_expand_weight, EVERY, axis=0, tiled=True),
        lax.all_gather(student_expand_bias, EVERY, axis=0, tiled=True),
        lax.all_gather(student_reduce_weight, EVERY, axis=0, tiled=True),
        lax.all_gather(student_reduce_bias, EVERY, axis=0, tiled=True),
        lax.all_gather(teacher_first_gain, EVERY, axis=0, tiled=True),
        lax.all_gather(teacher_first_shift, EVERY, axis=0, tiled=True),
        lax.all_gather(teacher_attend_weight, EVERY, axis=0, tiled=True),
        lax.all_gather(teacher_attend_bias, EVERY, axis=0, tiled=True),
        lax.all_gather(teacher_output_weight, EVERY, axis=0, tiled=True),
        lax.all_gather(teacher_output_bias, EVERY, axis=0, tiled=True),
        lax.all_gather(teacher_second_gain, EVERY, axis=0, tiled=True),
        lax.all_gather(teacher_second_shift, EVERY, axis=0, tiled=True),
        lax.all_gather(teacher_expand_weight, EVERY, axis=0, tiled=True),
        lax.all_gather(teacher_expand_bias, EVERY, axis=0, tiled=True),
        lax.all_gather(teacher_reduce_weight, EVERY, axis=0, tiled=True),
        lax.all_gather(teacher_reduce_bias, EVERY, axis=0, tiled=True),
    )
    models = (tuple(gathered[:12]), tuple(gathered[12:]))
    batch_seqs, rows_local, model_width = hidden.shape
    row_count = batch_seqs * rows_local
    inputs = hidden.astype(jnp.float32)
    inputs_flat = inputs.reshape(row_count, model_width)
    query_pos = lax.axis_index(BLK) * rows_local + jnp.arange(rows_local, dtype=jnp.int32)
    fronts = [front_half(inputs, params) for params in models]
    queries = (split_heads(fronts[0][1]), split_heads(fronts[1][1]))
    zero_heads = jnp.zeros((batch_seqs, HEADS, rows_local, HEAD), jnp.float32)
    zero_rows = jnp.zeros((batch_seqs, HEADS, rows_local), jnp.float32)
    start_state = (
        zero_heads,
        jnp.full((batch_seqs, HEADS, rows_local), -1e30, jnp.float32),
        zero_rows,
    )
    folded = attend_block(
        (start_state, start_state),
        (
            lax.all_gather(fronts[0][2], BLK, axis=1, tiled=True),
            lax.all_gather(fronts[0][3], BLK, axis=1, tiled=True),
            lax.all_gather(fronts[1][2], BLK, axis=1, tiled=True),
            lax.all_gather(fronts[1][3], BLK, axis=1, tiled=True),
        ),
        jnp.int32(0),
        queries,
        query_pos,
        lengths,
    )
    gain_final = final_gain.astype(jnp.float32)
    shift_final = final_shift.astype(jnp.float32)
    caches = []
    final_rows = []
    for model_index in range(2):
        params = models[model_index]
        running, row_max, row_total = folded[model_index]
        mixed_rows = (
            jnp.transpose(running / row_total[..., None], (0, 2, 1, 3))
            .reshape(row_count, model_width)
            .astype(jnp.bfloat16)
        )
        log_total = row_max + jnp.log(row_total)
        middle = inputs_flat + matmul_plain(mixed_rows, params[4]) + params[5].astype(jnp.float32)
        normed_two = layer_norm(
            middle, params[6].astype(jnp.float32), params[7].astype(jnp.float32)
        ).astype(jnp.bfloat16)
        inner_rows = matmul_plain(normed_two, params[8]) + params[9].astype(jnp.float32)
        active = gelu_tanh(inner_rows).astype(jnp.bfloat16)
        block_out = middle + matmul_plain(active, params[10]) + params[11].astype(jnp.float32)
        final_rows.append(layer_norm(block_out, gain_final, shift_final).astype(jnp.bfloat16))
        caches.append((mixed_rows, log_total, middle, normed_two, inner_rows, active, block_out))
    all_rows = lax.all_gather(jnp.stack(final_rows), VOCAB, axis=1, tiled=True)
    vocab_local = embedding.shape[0]
    vocab_index = lax.axis_index(VOCAB)
    column_valid = (
        vocab_index * vocab_local + jnp.arange(vocab_local, dtype=jnp.int32) < VOCAB_REAL
    )[None, :]
    total_rows = all_rows.shape[1]

    def scaled_logits(rows_pair):
        scaled_student = jnp.where(
            column_valid, matmul_right_t(rows_pair[0], embedding) * 0.5, -1e30
        )
        scaled_teacher = jnp.where(
            column_valid, matmul_right_t(rows_pair[1], embedding) * 0.5, -1e30
        )
        return (scaled_student, scaled_teacher)

    stat_rows = math.gcd(total_rows, 512)

    def local_stats(block_index):
        rows_pair = lax.dynamic_slice_in_dim(all_rows, block_index * stat_rows, stat_rows, 1)
        scaled_student, scaled_teacher = scaled_logits(rows_pair)
        max_student = jnp.max(scaled_student, axis=-1)
        max_teacher = jnp.max(scaled_teacher, axis=-1)
        exp_student = jnp.where(column_valid, jnp.exp(scaled_student - max_student[:, None]), 0.0)
        exp_teacher = jnp.where(column_valid, jnp.exp(scaled_teacher - max_teacher[:, None]), 0.0)
        cross_sum = jnp.sum(exp_teacher * (scaled_teacher - scaled_student), axis=-1)
        return (
            max_student,
            jnp.sum(exp_student, axis=-1),
            max_teacher,
            jnp.sum(exp_teacher, axis=-1),
            cross_sum,
        )

    stat_blocks = lax.map(local_stats, jnp.arange(total_rows // stat_rows))
    max_student, sum_student, max_teacher, sum_teacher, cross_sum = [
        stat_block.reshape(total_rows) for stat_block in stat_blocks
    ]
    top_student, top_teacher = lax.pmax((max_student, max_teacher), VOCAB)
    factor_student = jnp.exp(max_student - top_student)
    factor_teacher = jnp.exp(max_teacher - top_teacher)
    sum_student, sum_teacher, cross_sum = lax.psum(
        (sum_student * factor_student, sum_teacher * factor_teacher, cross_sum * factor_teacher),
        VOCAB,
    )
    max_student, max_teacher = (top_student, top_teacher)
    lse_student = max_student + jnp.log(sum_student)
    lse_teacher = max_teacher + jnp.log(sum_teacher)
    divergence_rows = cross_sum / sum_teacher - lse_teacher + lse_student
    valid_rows = (query_pos[None, :] < lengths[:, None]).astype(jnp.float32)
    own_start = vocab_index * row_count
    kl_out = (
        4.0
        * lax.dynamic_slice_in_dim(divergence_rows, own_start, row_count).reshape(
            batch_seqs, rows_local
        )
        * valid_rows
    )
    step_rows = math.gcd(row_count * lax.axis_size(VOCAB), 512)

    def one_block(block_index):
        begin = block_index * step_rows
        rows_pair = lax.dynamic_slice_in_dim(all_rows, begin, step_rows, 1)
        scaled_student, scaled_teacher = scaled_logits(rows_pair)
        log_student = (
            scaled_student - lax.dynamic_slice_in_dim(lse_student, begin, step_rows)[:, None]
        )
        log_teacher = (
            scaled_teacher - lax.dynamic_slice_in_dim(lse_teacher, begin, step_rows)[:, None]
        )
        row_kl = lax.dynamic_slice_in_dim(divergence_rows, begin, step_rows)[:, None]
        prob_student = jnp.where(column_valid, jnp.exp(log_student), 0.0)
        prob_teacher = jnp.where(column_valid, jnp.exp(log_teacher), 0.0)
        grad_student = (2.0 * (prob_student - prob_teacher)).astype(jnp.bfloat16)
        grad_teacher = (2.0 * prob_teacher * (log_teacher - log_student - row_kl)).astype(
            jnp.bfloat16
        )
        return jnp.concatenate(
            [matmul_plain(grad_student, embedding), matmul_plain(grad_teacher, embedding)], axis=1
        )

    grad_final = (
        lax.psum_scatter(
            lax.map(one_block, jnp.arange(row_count * lax.axis_size(VOCAB) // step_rows))
            .reshape(row_count * lax.axis_size(VOCAB), 2 * model_width)
            .astype(jnp.bfloat16),
            VOCAB,
            scatter_dimension=0,
            tiled=True,
        ).astype(jnp.float32)
        * valid_rows.reshape(row_count)[:, None]
    )
    regathered = (
        lax.all_gather(student_first_gain, EVERY, axis=0, tiled=True),
        lax.all_gather(student_first_shift, EVERY, axis=0, tiled=True),
        lax.all_gather(student_attend_weight, EVERY, axis=0, tiled=True),
        lax.all_gather(student_attend_bias, EVERY, axis=0, tiled=True),
        lax.all_gather(student_output_weight, EVERY, axis=0, tiled=True),
        lax.all_gather(student_output_bias, EVERY, axis=0, tiled=True),
        lax.all_gather(student_second_gain, EVERY, axis=0, tiled=True),
        lax.all_gather(student_second_shift, EVERY, axis=0, tiled=True),
        lax.all_gather(student_expand_weight, EVERY, axis=0, tiled=True),
        lax.all_gather(student_expand_bias, EVERY, axis=0, tiled=True),
        lax.all_gather(student_reduce_weight, EVERY, axis=0, tiled=True),
        lax.all_gather(student_reduce_bias, EVERY, axis=0, tiled=True),
        lax.all_gather(teacher_first_gain, EVERY, axis=0, tiled=True),
        lax.all_gather(teacher_first_shift, EVERY, axis=0, tiled=True),
        lax.all_gather(teacher_attend_weight, EVERY, axis=0, tiled=True),
        lax.all_gather(teacher_attend_bias, EVERY, axis=0, tiled=True),
        lax.all_gather(teacher_output_weight, EVERY, axis=0, tiled=True),
        lax.all_gather(teacher_output_bias, EVERY, axis=0, tiled=True),
        lax.all_gather(teacher_second_gain, EVERY, axis=0, tiled=True),
        lax.all_gather(teacher_second_shift, EVERY, axis=0, tiled=True),
        lax.all_gather(teacher_expand_weight, EVERY, axis=0, tiled=True),
        lax.all_gather(teacher_expand_bias, EVERY, axis=0, tiled=True),
        lax.all_gather(teacher_reduce_weight, EVERY, axis=0, tiled=True),
        lax.all_gather(teacher_reduce_bias, EVERY, axis=0, tiled=True),
    )
    back_models = (tuple(regathered[:12]), tuple(regathered[12:]))
    uppers = []
    middle_pairs = []
    for model_index in range(2):
        params = back_models[model_index]
        mixed_rows, log_total, middle, normed_two, inner_rows, active, block_out = caches[
            model_index
        ]
        _, final_pull = jax.vjp(
            lambda rows_in: layer_norm(rows_in, gain_final, shift_final), block_out
        )
        grad_out = final_pull(
            grad_final[:, model_index * model_width : (model_index + 1) * model_width]
        )[0]
        branch_low = grad_out.astype(jnp.bfloat16)
        grad_reduce_bias = column_sums(branch_low)
        grad_active = matmul_right_t(branch_low, params[10])
        _, gelu_pull = jax.vjp(gelu_tanh, inner_rows)
        inner_grad = gelu_pull(grad_active)[0].astype(jnp.bfloat16)
        grad_expand_bias = column_sums(inner_grad)
        grad_normed_two = matmul_right_t(inner_grad, params[8])
        _, second_pull = jax.vjp(
            layer_norm, middle, params[6].astype(jnp.float32), params[7].astype(jnp.float32)
        )
        middle_part, grad_second_gain, grad_second_shift = second_pull(grad_normed_two)
        grad_middle = grad_out + middle_part
        attn_low = grad_middle.astype(jnp.bfloat16)
        grad_output_bias = column_sums(attn_low)
        grad_mixed = matmul_right_t(attn_low, params[4]).astype(jnp.bfloat16)
        delta_rows = jnp.sum(
            (grad_mixed.astype(jnp.float32) * mixed_rows.astype(jnp.float32)).reshape(
                batch_seqs, rows_local, HEADS, HEAD
            ),
            axis=-1,
        )
        uppers.append(
            (
                grad_output_bias,
                grad_second_gain,
                grad_second_shift,
                grad_expand_bias,
                grad_reduce_bias,
                grad_middle,
                grad_mixed.reshape(batch_seqs, rows_local, model_width),
                delta_rows,
            )
        )
        middle_pairs.append(
            ((mixed_rows, attn_low), (normed_two, inner_grad), (active, branch_low))
        )
    grads_heads = (split_heads(uppers[0][6]), split_heads(uppers[1][6]))
    log_totals = (caches[0][1], caches[1][1])
    deltas = (jnp.transpose(uppers[0][7], (0, 2, 1)), jnp.transpose(uppers[1][7], (0, 2, 1)))
    query_grads = query_grad_block(
        (zero_heads, zero_heads),
        (
            lax.all_gather(fronts[0][2], BLK, axis=1, tiled=True),
            lax.all_gather(fronts[0][3], BLK, axis=1, tiled=True),
            lax.all_gather(fronts[1][2], BLK, axis=1, tiled=True),
            lax.all_gather(fronts[1][3], BLK, axis=1, tiled=True),
        ),
        jnp.int32(0),
        queries,
        grads_heads,
        log_totals,
        deltas,
        query_pos,
        lengths,
    )
    keys_local = (split_heads(fronts[0][2]), split_heads(fronts[1][2]))
    values_local = (split_heads(fronts[0][3]), split_heads(fronts[1][3]))
    key_grads = key_grad_block(
        ((zero_heads, zero_heads), (zero_heads, zero_heads)),
        (
            lax.all_gather(fronts[0][1], BLK, axis=1, tiled=True),
            lax.all_gather(uppers[0][6], BLK, axis=1, tiled=True),
            lax.all_gather(
                for_sending(jnp.transpose(log_totals[0], (0, 2, 1))), BLK, axis=1, tiled=True
            ),
            lax.all_gather(uppers[0][7].astype(jnp.bfloat16), BLK, axis=1, tiled=True).astype(
                jnp.float32
            ),
            lax.all_gather(fronts[1][1], BLK, axis=1, tiled=True),
            lax.all_gather(uppers[1][6], BLK, axis=1, tiled=True),
            lax.all_gather(
                for_sending(jnp.transpose(log_totals[1], (0, 2, 1))), BLK, axis=1, tiled=True
            ),
            lax.all_gather(uppers[1][7].astype(jnp.bfloat16), BLK, axis=1, tiled=True).astype(
                jnp.float32
            ),
        ),
        jnp.int32(0),
        keys_local,
        values_local,
        query_pos,
        lengths,
    )
    vectors = []
    pairs = []
    input_grad = jnp.zeros((row_count, model_width), jnp.float32)
    for model_index in range(2):
        params = back_models[model_index]
        upper = uppers[model_index]
        grad_keys, grad_values = key_grads[model_index]
        joined_grad = jnp.concatenate(
            [
                jnp.transpose(query_grads[model_index], (0, 2, 1, 3)).reshape(
                    row_count, model_width
                ),
                jnp.transpose(grad_keys, (0, 2, 1, 3)).reshape(row_count, model_width),
                jnp.transpose(grad_values, (0, 2, 1, 3)).reshape(row_count, model_width),
            ],
            axis=1,
        ).astype(jnp.bfloat16)
        bias_sums = column_sums(joined_grad)
        grad_attend_bias = jnp.concatenate([bias_sums[:model_width], bias_sums[2 * model_width :]])
        grad_normed_one = matmul_right_t(joined_grad, params[2])
        _, first_pull = jax.vjp(
            layer_norm, inputs_flat, params[0].astype(jnp.float32), params[1].astype(jnp.float32)
        )
        input_part, grad_first_gain, grad_first_shift = first_pull(grad_normed_one)
        input_grad = input_grad + upper[5] + input_part
        vectors.append(
            [
                grad_first_gain,
                grad_first_shift,
                grad_attend_bias,
                upper[0],
                upper[1],
                upper[2],
                upper[3],
                upper[4],
            ]
        )
        pairs.append(
            [
                (fronts[model_index][0], joined_grad),
                middle_pairs[model_index][0],
                middle_pairs[model_index][1],
                middle_pairs[model_index][2],
            ]
        )
    grads = []
    for model_index in range(2):
        matrix_list = [matmul_left_t(pair[0], pair[1]) for pair in pairs[model_index]]
        vector_list = vectors[model_index]
        grads.extend(
            [
                vector_list[0],
                vector_list[1],
                matrix_list[0],
                vector_list[2],
                matrix_list[1],
                vector_list[3],
                vector_list[4],
                vector_list[5],
                matrix_list[2],
                vector_list[6],
                matrix_list[3],
                vector_list[7],
            ]
        )
    summed = (
        lax.psum_scatter(grads[0], EVERY, scatter_dimension=0, tiled=True),
        lax.psum_scatter(grads[1], EVERY, scatter_dimension=0, tiled=True),
        lax.psum_scatter(grads[2], EVERY, scatter_dimension=0, tiled=True),
        lax.psum_scatter(grads[3], EVERY, scatter_dimension=0, tiled=True),
        lax.psum_scatter(grads[4], EVERY, scatter_dimension=0, tiled=True),
        lax.psum_scatter(grads[5], EVERY, scatter_dimension=0, tiled=True),
        lax.psum_scatter(grads[6], EVERY, scatter_dimension=0, tiled=True),
        lax.psum_scatter(grads[7], EVERY, scatter_dimension=0, tiled=True),
        lax.psum_scatter(grads[8], EVERY, scatter_dimension=0, tiled=True),
        lax.psum_scatter(grads[9], EVERY, scatter_dimension=0, tiled=True),
        lax.psum_scatter(grads[10], EVERY, scatter_dimension=0, tiled=True),
        lax.psum_scatter(grads[11], EVERY, scatter_dimension=0, tiled=True),
        lax.psum_scatter(grads[12], EVERY, scatter_dimension=0, tiled=True),
        lax.psum_scatter(grads[13], EVERY, scatter_dimension=0, tiled=True),
        lax.psum_scatter(grads[14], EVERY, scatter_dimension=0, tiled=True),
        lax.psum_scatter(grads[15], EVERY, scatter_dimension=0, tiled=True),
        lax.psum_scatter(grads[16], EVERY, scatter_dimension=0, tiled=True),
        lax.psum_scatter(grads[17], EVERY, scatter_dimension=0, tiled=True),
        lax.psum_scatter(grads[18], EVERY, scatter_dimension=0, tiled=True),
        lax.psum_scatter(grads[19], EVERY, scatter_dimension=0, tiled=True),
        lax.psum_scatter(grads[20], EVERY, scatter_dimension=0, tiled=True),
        lax.psum_scatter(grads[21], EVERY, scatter_dimension=0, tiled=True),
        lax.psum_scatter(grads[22], EVERY, scatter_dimension=0, tiled=True),
        lax.psum_scatter(grads[23], EVERY, scatter_dimension=0, tiled=True),
    )
    return tuple(summed) + (input_grad.reshape(batch_seqs, rows_local, model_width), kl_out)


LANES = 128
MARGIN = 16.0
SEQUENCE_AT = (0, 2, 3, 1)
VMEM_BYTES = 60 * 1024 * 1024


def lane_fold(tile_in, combine):
    folded = tile_in[:, :LANES]
    for start in range(LANES, tile_in.shape[1], LANES):
        folded = combine(folded, tile_in[:, start : start + LANES])
    return folded


def whole_block(shape):
    return pl.BlockSpec(shape, lambda *_: (0,) * len(shape))


def vocab_stats_kernel(
    scalars_ref,
    mine_low_ref,
    mine_high_ref,
    far_low_ref,
    far_high_ref,
    embed_ref,
    logit_student_ref,
    logit_teacher_ref,
    stats_ref,
    student_ref,
    teacher_ref,
    tile_max_s,
    tile_max_t,
    max_s,
    max_t,
    sum_s,
    sum_t,
    cross,
    part_s,
    part_t,
    part_x,
    low,
    *,
    tile,
    rows_block,
):
    step_index = pl.program_id(0)
    steps = pl.num_programs(0)
    first = step_index == 0
    half_rows = mine_low_ref.shape[0]
    rows = 2 * half_rows

    def keep(student_parts, teacher_parts):
        for kept, parts in ((student_ref, student_parts), (teacher_ref, teacher_parts)):
            for place, part in enumerate(parts):
                kept[place * half_rows : (place + 1) * half_rows, :] = part[...]

    @pl.when((step_index == 0) & (scalars_ref[1] == 0))
    def _():
        keep((mine_low_ref, mine_high_ref), (far_low_ref, far_high_ref))

    @pl.when((step_index == 0) & (scalars_ref[1] == 1))
    def _():
        keep((far_low_ref, far_high_ref), (mine_low_ref, mine_high_ref))

    @pl.when(step_index == 0)
    def _():
        for total in (max_s, max_t, sum_s, sum_t, cross):
            total[...] = jnp.zeros_like(total)

    def sums(scaled_s, scaled_t, top_s, top_t):
        shifted_s = scaled_s - top_s
        shifted_t = scaled_t - top_t
        exp_s = jnp.exp(shifted_s)
        exp_t = jnp.exp(shifted_t)
        return (
            lane_fold(exp_s, jnp.add),
            lane_fold(exp_t, jnp.add),
            lane_fold(exp_t * (shifted_t - shifted_s), jnp.add),
        )

    def one_tile(masked):
        embed_tile = embed_ref[...]
        excess = None
        for start in range(0, rows, rows_block):
            here = pl.ds(start, rows_block)
            scaled_s = matmul_right_t(student_ref[here, :], embed_tile)
            scaled_t = matmul_right_t(teacher_ref[here, :], embed_tile)
            if masked:
                column = lax.broadcasted_iota(jnp.int32, (1, tile), 1) + step_index * tile
                scaled_s = jnp.where(column < scalars_ref[0], scaled_s, -1e30)
                scaled_t = jnp.where(column < scalars_ref[0], scaled_t, -1e30)
            logit_student_ref[here, :] = scaled_s
            logit_teacher_ref[here, :] = scaled_t
            tops_s = lane_fold(scaled_s, jnp.maximum)
            tops_t = lane_fold(scaled_t, jnp.maximum)
            tile_max_s[here, :] = tops_s
            tile_max_t[here, :] = tops_t
            old_s = max_s[here, :]
            old_t = max_t[here, :]
            part_s[here, :], part_t[here, :], part_x[here, :] = sums(
                scaled_s, scaled_t, old_s[:, :1], old_t[:, :1]
            )
            over = jnp.maximum(tops_s - old_s, tops_t - old_t)
            excess = over if excess is None else jnp.maximum(excess, over)

        low[0] = 0.0

        @pl.when(first)
        def _():
            least_s = jnp.min(jnp.max(tile_max_s[...], axis=1, keepdims=True))
            least_t = jnp.min(jnp.max(tile_max_t[...], axis=1, keepdims=True))
            low[0] = -jnp.minimum(least_s, least_t)

        @pl.when(jnp.maximum(jnp.max(excess), low[0]) > MARGIN)
        def _():
            def rescale(chunk, _):
                here = pl.ds(pl.multiple_of(chunk * 64, 64), 64)
                old_s = max_s[here, :]
                old_t = max_t[here, :]
                top_s = jnp.max(tile_max_s[here, :], axis=1, keepdims=True)
                top_t = jnp.max(tile_max_t[here, :], axis=1, keepdims=True)
                new_s = jnp.broadcast_to(
                    jnp.where(first, top_s, jnp.maximum(old_s[:, :1], top_s)), old_s.shape
                )
                new_t = jnp.broadcast_to(
                    jnp.where(first, top_t, jnp.maximum(old_t[:, :1], top_t)), old_t.shape
                )
                factor_t = jnp.where(first, 0.0, jnp.exp(old_t - new_t))
                moved = (old_t - old_s) - (new_t - new_s)
                max_s[here, :] = new_s
                max_t[here, :] = new_t
                sum_s[here, :] = sum_s[here, :] * jnp.where(first, 0.0, jnp.exp(old_s - new_s))
                cross[here, :] = (cross[here, :] + moved * sum_t[here, :]) * factor_t
                sum_t[here, :] = sum_t[here, :] * factor_t
                part_s[here, :], part_t[here, :], part_x[here, :] = sums(
                    logit_student_ref[here, :],
                    logit_teacher_ref[here, :],
                    new_s[:, :1],
                    new_t[:, :1],
                )
                return 0

            lax.fori_loop(0, rows // 64, rescale, 0)

        sum_s[...] += part_s[...]
        sum_t[...] += part_t[...]
        cross[...] += part_x[...]

    @pl.when(step_index < steps - 1)
    def _():
        one_tile(False)

    @pl.when(step_index == steps - 1)
    def _():
        one_tile(True)
        lane = lax.broadcasted_iota(jnp.int32, (rows, LANES), 1)
        result = jnp.sum(cross[...], axis=1, keepdims=True)
        result = jnp.where(lane == 3, jnp.sum(sum_t[...], axis=1, keepdims=True), result)
        result = jnp.where(lane == 2, jnp.sum(sum_s[...], axis=1, keepdims=True), result)
        result = jnp.where(lane == 0, max_s[...], jnp.where(lane == 1, max_t[...], result))
        stats_ref[...] = result.T[:8, :]


def vocab_stats(final_parts, is_teacher, embedding, valid_columns, tile=1280, rows_block=256):
    half_rows, width = final_parts[0].shape
    rows = 2 * half_rows
    steps = pl.cdiv(embedding.shape[0], tile)
    logits = jax.ShapeDtypeStruct((rows, steps * tile), jnp.float32)
    return pl.pallas_call(
        functools.partial(vocab_stats_kernel, tile=tile, rows_block=rows_block),
        grid_spec=pltpu.PrefetchScalarGridSpec(
            num_scalar_prefetch=1,
            grid=(steps,),
            in_specs=[whole_block((half_rows, width))] * 4
            + [pl.BlockSpec((tile, width), lambda j, *_: (j, 0))],
            out_specs=[
                pl.BlockSpec((rows, tile), lambda j, *_: (0, j)),
                pl.BlockSpec((rows, tile), lambda j, *_: (0, j)),
                whole_block((8, rows)),
            ],
            scratch_shapes=[pltpu.VMEM((rows, width), jnp.bfloat16)] * 2
            + [pltpu.VMEM((rows, LANES), jnp.float32)] * 10
            + [pltpu.SMEM((1,), jnp.float32)],
        ),
        out_shape=[logits, logits, jax.ShapeDtypeStruct((8, rows), jnp.float32)],
        compiler_params=pltpu.CompilerParams(vmem_limit_bytes=VMEM_BYTES),
        name="vocab_stats",
    )(
        jnp.stack([valid_columns, is_teacher.astype(jnp.int32)]),
        *final_parts,
        embedding,
    )


def vocab_grads_kernel(
    logit_student_ref,
    logit_teacher_ref,
    embed_ref,
    *refs,
    tile,
    columns,
    rows_block,
    count,
):
    stat_refs = refs[:count]
    own_ref, send_ref, divergence_ref, row_ref, student_ref, teacher_ref = refs[count:]
    step_index = pl.program_id(0)
    rows = student_ref.shape[0]
    half_rows = rows // 2

    @pl.when(step_index == 0)
    def _():
        student_ref[...] = jnp.zeros_like(student_ref)
        teacher_ref[...] = jnp.zeros_like(teacher_ref)
        parts = []
        for index in range(count):
            part = stat_refs[index][...]
            if index % 2:
                part = jnp.concatenate([part[:, half_rows:], part[:, :half_rows]], axis=1)
            parts.append([part[k : k + 1, :] for k in range(5)])
        top_s = functools.reduce(jnp.maximum, [p[0] for p in parts])
        top_t = functools.reduce(jnp.maximum, [p[1] for p in parts])
        sum_s = sum(p[2] * jnp.exp(p[0] - top_s) for p in parts)
        sum_t = sum(p[3] * jnp.exp(p[1] - top_t) for p in parts)
        cross = sum((p[4] + (p[1] - p[0]) * p[3]) * jnp.exp(p[1] - top_t) for p in parts)
        lse_s = top_s + jnp.log(sum_s)
        lse_t = top_t + jnp.log(sum_t)
        mean_gap = cross / sum_t
        divergence_ref[...] = jnp.broadcast_to(mean_gap - lse_t + lse_s, divergence_ref.shape)
        line = lax.broadcasted_iota(jnp.int32, (LANES, rows), 0)
        row_ref[...] = jnp.where(line == 0, lse_s, jnp.where(line == 1, lse_t, mean_gap)).T

    def one_tile(masked):
        embed_tile = embed_ref[...]
        if masked:
            row = lax.broadcasted_iota(jnp.int32, (tile, 1), 0) + step_index * tile
            embed_tile = jnp.where(row < columns, embed_tile, jnp.zeros_like(embed_tile))
        for start in range(0, rows, rows_block):
            here = pl.ds(start, rows_block)
            scaled_s = logit_student_ref[here, :]
            scaled_t = logit_teacher_ref[here, :]
            prob_s = jnp.exp(scaled_s - row_ref[here, 0:1])
            prob_t = jnp.exp(scaled_t - row_ref[here, 1:2])
            grad_s = (prob_s - prob_t).astype(jnp.bfloat16)
            grad_t = (prob_t * ((scaled_t - scaled_s) - row_ref[here, 2:3])).astype(jnp.bfloat16)
            student_ref[here, :] += matmul_plain(grad_s, embed_tile)
            teacher_ref[here, :] += matmul_plain(grad_t, embed_tile)

    last = pl.num_programs(0) - 1

    @pl.when(step_index < last)
    def _():
        one_tile(False)

    @pl.when(step_index == last)
    def _():
        one_tile(True)
        for index, sums in enumerate((student_ref, teacher_ref)):
            own_ref[index] = sums[:half_rows, :]
            send_ref[index] = sums[half_rows:, :].astype(jnp.bfloat16)


def vocab_grads(logit_student, logit_teacher, embedding, stat_parts, tile=1280, rows_block=256):
    rows = logit_student.shape[0]
    columns, width = embedding.shape
    halves = (2, rows // 2, width)
    return pl.pallas_call(
        functools.partial(
            vocab_grads_kernel,
            tile=tile,
            columns=columns,
            rows_block=rows_block,
            count=len(stat_parts),
        ),
        grid=(pl.cdiv(columns, tile),),
        in_specs=[
            pl.BlockSpec((rows, tile), lambda j: (0, j)),
            pl.BlockSpec((rows, tile), lambda j: (0, j)),
            pl.BlockSpec((tile, width), lambda j: (j, 0)),
        ]
        + [whole_block((8, rows))] * len(stat_parts),
        out_specs=[whole_block(halves), whole_block(halves), whole_block((8, rows))],
        out_shape=[
            jax.ShapeDtypeStruct(halves, jnp.float32),
            jax.ShapeDtypeStruct(halves, jnp.bfloat16),
            jax.ShapeDtypeStruct((8, rows), jnp.float32),
        ],
        scratch_shapes=[
            pltpu.VMEM((rows, LANES), jnp.float32),
            pltpu.VMEM((rows, width), jnp.float32),
            pltpu.VMEM((rows, width), jnp.float32),
        ],
        compiler_params=pltpu.CompilerParams(vmem_limit_bytes=VMEM_BYTES),
        name="vocab_grads",
    )(logit_student, logit_teacher, embedding, *stat_parts)


def attend_kernel(length_ref, query_ref, key_ref, value_ref, mixed_ref, *, block):
    rows = query_ref.shape[0]
    lane = lax.broadcasted_iota(jnp.int32, (1, LANES), 1)
    for start in range(0, rows, block):
        keys = start + block
        key_pos = lax.broadcasted_iota(jnp.int32, (block, keys), 1)
        query_pos = lax.broadcasted_iota(jnp.int32, (block, keys), 0) + start
        allowed = (key_pos <= query_pos) & (key_pos < length_ref[0])
        outs = []
        for head in range(LANES // HEAD):
            own = (lane // HEAD) == head
            queries = query_ref[start : start + block, :] * HEAD**-0.5
            queries = jnp.where(own, queries, jnp.zeros_like(queries))
            scores = matmul_right_t(queries, key_ref[:keys, :])
            scores = jnp.where(allowed, scores, -1e30)
            weights = jnp.exp(scores - jnp.max(scores, axis=1, keepdims=True))
            total = jnp.sum(weights, axis=1, keepdims=True)
            outs.append(
                matmul_plain(weights.astype(jnp.bfloat16), value_ref[:keys, :]) / total
            )
        mixed_ref[start : start + block, :] = jnp.where(lane < HEAD, outs[0], outs[1]).astype(
            jnp.bfloat16
        )


def attend_rows(joined, seq_length, block):
    rows, width = joined.shape
    third = width // 3
    pairs = third // LANES
    spec = lambda part: pl.BlockSpec((rows, LANES), lambda p, *_: (0, part * pairs + p))
    return pl.pallas_call(
        functools.partial(attend_kernel, block=block),
        grid_spec=pltpu.PrefetchScalarGridSpec(
            num_scalar_prefetch=1,
            grid=(pairs,),
            in_specs=[spec(0), spec(1), spec(2)],
            out_specs=spec(0),
        ),
        out_shape=jax.ShapeDtypeStruct((rows, third), jnp.bfloat16),
        compiler_params=pltpu.CompilerParams(vmem_limit_bytes=VMEM_BYTES),
        name="attend",
    )(seq_length.reshape(1), joined, joined, joined)


def attend_grads_kernel(
    length_ref,
    query_ref,
    key_ref,
    value_ref,
    grad_ref,
    grad_query_ref,
    grad_key_ref,
    grad_value_ref,
    sum_key,
    sum_value,
    *,
    block,
):
    rows = query_ref.shape[0]
    lane = lax.broadcasted_iota(jnp.int32, (1, LANES), 1)
    sum_key[...] = jnp.zeros_like(sum_key)
    sum_value[...] = jnp.zeros_like(sum_value)
    keys_turned = key_ref[...].T
    for start in range(0, rows, block):
        keys = start + block
        key_pos = lax.broadcasted_iota(jnp.int32, (keys, block), 0)
        query_pos = lax.broadcasted_iota(jnp.int32, (keys, block), 1) + start
        allowed = (key_pos <= query_pos) & (key_pos < length_ref[0])
        outs = []
        for head in range(LANES // HEAD):
            own = (lane // HEAD) == head
            queries = query_ref[start : start + block, :] * HEAD**-0.5
            queries = jnp.where(own, queries, jnp.zeros_like(queries))
            grads = grad_ref[start : start + block, :]
            grads = jnp.where(own, grads, jnp.zeros_like(grads))
            scores = matmul_right_t(key_ref[:keys, :], queries)
            scores = jnp.where(allowed, scores, -1e30)
            weights = jnp.exp(scores - jnp.max(scores, axis=0, keepdims=True))
            soft = weights * (1.0 / jnp.sum(weights, axis=0, keepdims=True))
            grad_soft = matmul_right_t(value_ref[:keys, :], grads)
            soft_grad = soft * grad_soft
            delta = jnp.sum(soft_grad, axis=0, keepdims=True)
            grad_scores = (soft_grad - soft * delta).astype(jnp.bfloat16)
            sum_value[:keys, :] += matmul_plain(soft.astype(jnp.bfloat16), grads)
            sum_key[:keys, :] += matmul_plain(grad_scores, queries)
            outs.append(matmul_plain(keys_turned[:, :keys], grad_scores))
        head_row = lax.broadcasted_iota(jnp.int32, (LANES, 1), 0)
        turned = jnp.where(head_row < HEAD, outs[0], outs[1]) * HEAD**-0.5
        grad_query_ref[start : start + block, :] = turned.T.astype(jnp.bfloat16)
    grad_key_ref[...] = sum_key[...].astype(jnp.bfloat16)
    grad_value_ref[...] = sum_value[...].astype(jnp.bfloat16)


def attend_grads(joined, grad_mixed, seq_length, block):
    rows, width = joined.shape
    third = width // 3
    pairs = third // LANES
    spec = lambda part: pl.BlockSpec((rows, LANES), lambda p, *_: (0, part * pairs + p))
    out = jax.ShapeDtypeStruct((rows, third), jnp.bfloat16)
    return pl.pallas_call(
        functools.partial(attend_grads_kernel, block=block),
        grid_spec=pltpu.PrefetchScalarGridSpec(
            num_scalar_prefetch=1,
            grid=(pairs,),
            in_specs=[spec(0), spec(1), spec(2), spec(0)],
            out_specs=[spec(0)] * 3,
            scratch_shapes=[pltpu.VMEM((rows, LANES), jnp.float32)] * 2,
        ),
        out_shape=[out] * 3,
        compiler_params=pltpu.CompilerParams(vmem_limit_bytes=VMEM_BYTES),
        name="attend_grads",
    )(seq_length.reshape(1), joined, joined, joined, grad_mixed)


def place_kernel(own_ref, *refs, order, cuts):
    count = len(order)
    for block_ref, indices in zip(refs, order):
        height = block_ref.shape[0] // len(indices)
        for place, index in enumerate(indices):
            target = own_ref[0] ^ index
            for (first_row, rows, first_lane, lanes), out in zip(cuts, refs[count:]):
                first = place * height + first_row
                out[pl.ds(pl.multiple_of(target * rows, 16), rows), :] = block_ref[
                    first : first + rows, first_lane : first_lane + lanes
                ]


def place_blocks(gathered, own, cuts):
    gathered, order = gathered
    return pl.pallas_call(
        functools.partial(place_kernel, order=order, cuts=cuts),
        in_specs=[pl.BlockSpec(memory_space=pltpu.SMEM)]
        + [pl.BlockSpec(memory_space=pltpu.VMEM)] * len(order),
        out_specs=[pl.BlockSpec(memory_space=pltpu.VMEM)] * len(cuts),
        out_shape=[
            jax.ShapeDtypeStruct((8 * rows, lanes), jnp.bfloat16) for _, rows, _, lanes in cuts
        ],
        compiler_params=pltpu.CompilerParams(vmem_limit_bytes=VMEM_BYTES),
        name="place_blocks",
    )(own.reshape(1), *gathered)


def swap(rows, axis, distance):
    count = lax.axis_size(axis)
    return lax.ppermute(rows, axis, [(index, index ^ distance) for index in range(count)])


def swap_low(rows):
    return swap(rows.astype(jnp.bfloat16), VOCAB, 1).astype(jnp.float32)


def in_pair(second, mine, other, axis=0):
    return jnp.where(
        second,
        jnp.concatenate([other, mine], axis=axis),
        jnp.concatenate([mine, other], axis=axis),
    )


def in_order(index, parts):
    low = (index & 1) == 1
    high = (index & 2) == 2
    pairs = [
        [jnp.where(low, parts[k + 1], parts[k]), jnp.where(low, parts[k], parts[k + 1])]
        for k in (0, 2)
    ]
    return [
        jnp.where(high, pairs[1][0], pairs[0][0]),
        jnp.where(high, pairs[1][1], pairs[0][1]),
        jnp.where(high, pairs[0][0], pairs[1][0]),
        jnp.where(high, pairs[0][1], pairs[1][1]),
    ]


def norm_back(inputs, gain_row, grad):
    centred = inputs - jnp.mean(inputs, axis=-1, keepdims=True)
    inverse = lax.rsqrt(jnp.mean(centred * centred, axis=-1, keepdims=True) + 1e-05)
    normal = centred * inverse
    scaled = grad * gain_row
    along = jnp.mean(scaled * normal, axis=-1, keepdims=True)
    result = inverse * (scaled - jnp.mean(scaled, axis=-1, keepdims=True) - normal * along)
    return result, jnp.sum(grad * normal, axis=0), jnp.sum(grad, axis=0)


def gelu_slope(inputs):
    root = math.sqrt(2.0 / math.pi)
    square = inputs * inputs
    bent = jnp.tanh(root * inputs * (1.0 + 0.044715 * square))
    return 0.5 * (1.0 + bent) + 0.5 * inputs * (1.0 - bent * bent) * root * (
        1.0 + 3 * 0.044715 * square
    )


def rows_of(array_in, start, count):
    return lax.dynamic_slice_in_dim(array_in, start, count, 0)


def columns_of(array_in, start, count):
    return lax.dynamic_slice_in_dim(array_in, start, count, 1)


def vector_lines_of(params, seq_length, width):
    short, middle, wide = [
        jnp.stack([jnp.stack([p[k] for k in numbers]) for p in params])
        for numbers in ((0, 1, 5, 6, 7, 11), (3,), (9,))
    ]
    lines = jnp.concatenate(
        [
            jnp.pad(group, ((0, 0), (0, 0), (0, LANES - group.shape[2])))
            for group in (short, middle, wide)
        ],
        axis=1,
    )
    length_parts = jnp.stack([seq_length // 32, seq_length % 32]).astype(jnp.bfloat16)
    length_parts = jnp.broadcast_to(length_parts, lines.shape[:2] + (2,))
    lines = jnp.concatenate([lines, length_parts], axis=2)
    return jnp.pad(lines, ((0, 0), (0, 0), (0, width - lines.shape[2])))


def pack_weights(params, half, lines):
    attend, output, expand, reduce = params[2], params[4], params[8], params[10]
    width = output.shape[1]
    part = width // 2
    wide = expand.shape[1] // 2
    begin = half * part
    front = jnp.concatenate(
        [attend[:, k * width + begin : k * width + begin + part] for k in range(3)], axis=1
    )
    return (
        jnp.concatenate([front, lines], axis=0),
        jnp.concatenate(
            [
                expand[:, start : start + part]
                for start in range(half * wide, (half + 1) * wide, part)
            ]
            + [output[:, begin : begin + part], reduce[:, begin : begin + part]],
            axis=0,
        ),
    )


def exchange_models(slabs):
    index = lax.axis_index(VOCAB)
    stacked = jnp.stack(slabs)
    parts = [lax.dynamic_index_in_dim(stacked, index, 0, keepdims=False)]
    for distance in (1, 2, 3):
        parts.append(
            swap(
                lax.dynamic_index_in_dim(stacked, index ^ distance, 0, keepdims=False),
                VOCAB,
                distance,
            )
        )
    return in_order(index, parts)


def after(value, *others):
    return lax.optimization_barrier((value, others))[0]


def held_after(held, *others):
    return after(held[0], *others), held[1]


def halves_of(axis_name, bit):
    distance = 1 << bit
    return distance, distance * (lax.axis_size(BATCH) if axis_name == BLK else 1)


def double(held, axis_name, bit):
    arrays, order = held
    distance, offset = halves_of(axis_name, bit)
    sent = jnp.concatenate(arrays, axis=0) if len(arrays) > 1 else arrays[0]
    sources = sum(order, ())
    return (
        arrays + (swap(sent, axis_name, distance),),
        order + (tuple(source ^ offset for source in sources),),
    )


def halve_and_see(addends, axis_name, bit, *waits):
    axis = 2 if axis_name == BATCH else 1 - bit
    own = (lax.axis_index(axis_name) >> bit) & 1
    mine = lax.dynamic_slice_in_dim(addends, own, 1, axis)
    theirs = lax.dynamic_slice_in_dim(addends, 1 - own, 1, axis)
    received = swap(theirs.astype(jnp.bfloat16), axis_name, 1 << bit)
    seen = after(received, *waits) if waits else received
    return mine.astype(jnp.float32) + seen.astype(jnp.float32), received


def halve(addends, axis_name, bit, *waits):
    return halve_and_see(addends, axis_name, bit, *waits)[0]


def shards_by_model(hidden, lengths, *rest):
    embedding = rest[26]
    gain_final = rest[24].astype(jnp.float32)
    shift_final = rest[25].astype(jnp.float32)
    params = (rest[:12], rest[12:24])
    blk, batch, member = (lax.axis_index(name) for name in EVERY)
    size_blk, size_batch, size_vocab = (lax.axis_size(name) for name in EVERY)
    plane = blk * size_batch + batch
    model, half = member // 2, member % 2
    is_teacher, is_second = model == 1, half == 1
    rows_local, width = hidden.shape[1:]
    rows = rows_local * size_vocab
    own_rows = rows // 2
    part = width // 2
    ff_part = rest[8].shape[1] // 2
    shard_rows = rest[2].shape[0]
    plane_rows = shard_rows * size_vocab
    crossing = (BLK, VOCAB)

    lines = vector_lines_of(params, lengths[0], 3 * part)
    front_slabs, back_slabs = zip(
        *[pack_weights(params[m], h, lines[m]) for m in (0, 1) for h in (0, 1)]
    )
    front = exchange_models(front_slabs)
    back = exchange_models(after(back_slabs, front))
    length_parts = sum(
        jnp.where(blk == place, front[source][shard_rows, LANES : LANES + 2], 0)
        for place, source in enumerate(SEQUENCE_AT)
    ).astype(jnp.int32)
    seq_length = 32 * length_parts[0] + length_parts[1]
    front_block = jnp.concatenate(
        [source[:shard_rows] for source in front] + [source[shard_rows:] for source in front],
        axis=0,
    )
    units = (ff_part + part) // part
    middle_block = jnp.concatenate(
        [
            jnp.concatenate(
                [source[k * shard_rows : (k + 1) * shard_rows] for source in back], axis=0
            )
            for k in range(units)
        ],
        axis=1,
    )
    reduce_block = jnp.concatenate([source[units * shard_rows :] for source in back], axis=0)
    vector_lines = front_block.shape[0] - plane_rows
    reduce_rows = reduce_block.shape[0]

    front_held = double(((front_block,), ((0,),)), BLK, 1)
    middle_held = double(((after(middle_block, front_held[0]),), ((0,),)), BLK, 1)
    reduce_held = double(((after(reduce_block, middle_held[0]),), ((0,),)), BLK, 1)
    turn = [
        (a * size_vocab + SEQUENCE_AT[b], b * size_vocab + a)
        for a in range(size_blk)
        for b in range(size_vocab)
    ]
    front_held = double(front_held, BLK, 0)
    quarter = lax.ppermute(after(hidden[0], front_held[0]), crossing, turn)
    quarter_far = swap(quarter, VOCAB, 2)
    quarters = in_order(
        member, [quarter, swap(quarter, VOCAB, 1), quarter_far, swap(quarter_far, VOCAB, 1)]
    )
    front_held = double(held_after(front_held, middle_held[0]), BATCH, 0)
    middle_held = double(middle_held, BATCH, 0)
    reduce_held = double(reduce_held, BLK, 0)
    attend_weight, vectors = place_blocks(
        front_held,
        plane,
        ((0, plane_rows, 0, 3 * part), (plane_rows, vector_lines, 0, LANES)),
    )

    shards_all = size_blk * size_batch * size_vocab
    vectors = vectors.reshape(shards_all, vector_lines // size_vocab, LANES).astype(jnp.float32)
    first_gain, first_shift, output_bias, second_gain, second_shift, reduce_bias = [
        vectors[:, k, :shard_rows].reshape(width) for k in range(6)
    ]
    attend_bias = vectors[:, 6, : 2 * shard_rows].reshape(2 * width)
    expand_bias = vectors[:, 7, : 4 * shard_rows].reshape(2 * ff_part)
    query_bias = rows_of(attend_bias, half * part, part)
    value_bias = rows_of(attend_bias, width + half * part, part)
    joined_bias = jnp.concatenate([query_bias, jnp.zeros((part,), jnp.float32), value_bias])
    expand_bias = rows_of(expand_bias, half * ff_part, ff_part)

    inputs_low = jnp.concatenate(quarters, axis=0)
    inputs = inputs_low.astype(jnp.float32)
    inputs_own = rows_of(inputs_low, half * own_rows, own_rows).astype(jnp.float32)
    normed_one = layer_norm(inputs, first_gain, first_shift).astype(jnp.bfloat16)
    normed_one = after(normed_one, middle_held[0], reduce_held[0])
    joined = (matmul_plain(normed_one, attend_weight) + joined_bias).astype(jnp.bfloat16)
    block = math.gcd(rows, 256)
    mixed_rows = attend_rows(joined, seq_length, block)
    middle_held = held_after(double(middle_held, BLK, 0), mixed_rows)
    reduce_held = double(reduce_held, BATCH, 0)
    mixed_rows = after(mixed_rows, middle_held[0], reduce_held[0])
    expand_weight, output_columns = place_blocks(
        middle_held, plane, ((0, plane_rows, 0, ff_part), (0, plane_rows, ff_part, part))
    )
    output_weight = in_pair(
        is_second,
        rows_of(output_columns, half * part, part),
        swap(rows_of(output_columns, (1 - half) * part, part), VOCAB, 1),
        axis=1,
    )
    attended = matmul_plain(mixed_rows, output_weight)
    middle = (
        inputs_own
        + rows_of(attended, half * own_rows, own_rows)
        + swap_low(rows_of(attended, (1 - half) * own_rows, own_rows))
        + output_bias
    )
    normed_own = layer_norm(middle, second_gain, second_shift).astype(jnp.bfloat16)
    normed_two = jnp.concatenate([normed_own, swap(normed_own, VOCAB, 1)], axis=0)
    inner_rows = matmul_plain(normed_two, expand_weight) + expand_bias
    active = gelu_tanh(inner_rows).astype(jnp.bfloat16)
    active, slope = lax.optimization_barrier(
        (active, gelu_slope(inner_rows).astype(jnp.bfloat16))
    )
    (reduce_columns,) = place_blocks(reduce_held, plane, ((0, reduce_rows, 0, part),))
    reduce_weight = in_pair(
        is_second,
        rows_of(reduce_columns, half * ff_part, ff_part),
        swap(rows_of(reduce_columns, (1 - half) * ff_part, ff_part), VOCAB, 1),
        axis=1,
    )
    reduced = matmul_plain(active, reduce_weight)
    block_out = middle + reduced[:own_rows] + swap_low(reduced[own_rows:]) + reduce_bias
    final_rows = (0.5 * layer_norm(block_out, gain_final, shift_final)).astype(jnp.bfloat16)

    final_far = swap(final_rows, VOCAB, 2)
    final_parts = (final_rows, swap(final_rows, VOCAB, 1), final_far, swap(final_far, VOCAB, 1))
    vocab_local = embedding.shape[0]
    valid_columns = jnp.clip(VOCAB_REAL - member * vocab_local, 0, vocab_local)
    logit_student, logit_teacher, stats = vocab_stats(
        final_parts, is_teacher, embedding, valid_columns
    )
    stat_parts = [stats] + [swap(stats, VOCAB, distance) for distance in (1, 2, 3)]
    own_sums, core_sums, divergence_rows = vocab_grads(
        logit_student, logit_teacher, embedding, stat_parts
    )
    positions = jnp.arange(rows, dtype=jnp.int32)
    kl_rows = in_pair(is_second, divergence_rows[0, :own_rows], divergence_rows[0, own_rows:])
    kl_rows = 4.0 * kl_rows * (positions < seq_length).astype(jnp.float32)

    both = own_sums + swap(core_sums, VOCAB, 1).astype(jnp.float32)
    grad_final = jnp.where(is_teacher, both[1], both[0]) + swap(
        jnp.where(is_teacher, both[0], both[1]).astype(jnp.bfloat16), VOCAB, 2
    ).astype(jnp.float32)
    own_valid = (half * own_rows + positions[:own_rows] < seq_length).astype(jnp.float32)
    grad_final = grad_final * (2.0 * own_valid)[:, None]

    grad_out, _, _ = norm_back(block_out, gain_final, grad_final)
    branch_own = grad_out.astype(jnp.bfloat16)
    branch_low = jnp.concatenate([branch_own, swap(branch_own, VOCAB, 1)], axis=0)
    grad_reduce = matmul_left_t(active, branch_low).astype(jnp.bfloat16)
    branch_low = after(branch_low, grad_reduce)
    reduce_other = swap(columns_of(grad_reduce, (1 - half) * part, part), VOCAB, 1)
    grad_reduce = in_pair(is_second, columns_of(grad_reduce, half * part, part), reduce_other)
    grid = (2, 2, 2)
    grad_reduce = grad_reduce.reshape(grid + (reduce_rows, part))
    grad_active = matmul_right_t(branch_low, reduce_weight)
    inner_grad = (grad_active * slope.astype(jnp.float32)).astype(jnp.bfloat16)
    grad_normed = matmul_right_t(after(inner_grad, reduce_other), expand_weight)
    grad_normed_own = grad_normed[:own_rows] + swap_low(grad_normed[own_rows:])
    middle_part, grad_second_gain, grad_second_shift = norm_back(
        middle, second_gain, grad_normed_own
    )
    grad_middle = grad_out + middle_part
    attn_own = grad_middle.astype(jnp.bfloat16)
    attn_low = in_pair(is_second, attn_own, swap(attn_own, VOCAB, 1))
    grad_mixed = matmul_right_t(attn_low, output_weight).astype(jnp.bfloat16)
    grad_expand = matmul_left_t(normed_two, inner_grad).astype(jnp.bfloat16)
    grad_output = matmul_left_t(mixed_rows, attn_low).astype(jnp.bfloat16)
    grad_output = in_pair(
        is_second,
        columns_of(grad_output, half * part, part),
        swap(columns_of(grad_output, (1 - half) * part, part), VOCAB, 1),
    )
    grad_expand = grad_expand.reshape(grid + (plane_rows, ff_part))
    joined_parts = attend_grads(joined, grad_mixed, seq_length, block)
    reduce_sum = halve(grad_reduce, BATCH, 0, joined_parts[0])
    expand_sum = halve(grad_expand, BLK, 0, joined_parts[0])
    joined_grad = after(jnp.concatenate(joined_parts, axis=1), reduce_sum, expand_sum)
    grad_normed = matmul_right_t(joined_grad, attend_weight)
    grad_attend = matmul_left_t(normed_one, joined_grad).astype(jnp.bfloat16)
    reduce_sum, reduce_seen = halve_and_see(reduce_sum, BLK, 0)
    expand_sum, expand_seen = halve_and_see(expand_sum, BATCH, 0)
    normed_other = after(rows_of(grad_normed, (1 - half) * own_rows, own_rows), reduce_seen, expand_seen)
    normed_other = swap_low(normed_other)
    grad_normed_own = rows_of(grad_normed, half * own_rows, own_rows) + normed_other
    input_part, grad_first_gain, grad_first_shift = norm_back(
        inputs_own, first_gain, grad_normed_own
    )
    grad_inputs = (grad_middle + input_part).reshape(2, rows_local, width)
    input_other = swap(
        jnp.where(is_teacher, grad_inputs[0], grad_inputs[1]).astype(jnp.bfloat16), VOCAB, 2
    )
    input_sum = jnp.where(is_teacher, grad_inputs[1], grad_inputs[0])
    input_sum += input_other.astype(jnp.float32)
    home = [
        (a * size_vocab + 2 * m + h, (2 * h + m) * size_vocab + SEQUENCE_AT[a])
        for a in range(size_blk)
        for m in (0, 1)
        for h in (0, 1)
    ]
    kl_rows = rows_of(kl_rows, (2 * half + model) * rows_local, rows_local)
    kl_high = kl_rows.astype(jnp.bfloat16)
    kl_low = (kl_rows - kl_high.astype(jnp.float32)).astype(jnp.bfloat16)
    kl_line = jnp.concatenate([kl_high, kl_low])
    kl_line = jnp.pad(kl_line[None], ((0, 7), (0, width - kl_line.shape[0])))
    home_rows = lax.ppermute(
        jnp.concatenate([input_sum.astype(jnp.bfloat16), kl_line], axis=0), crossing, home
    ).astype(jnp.float32)
    input_grad = home_rows[:rows_local]
    kl_out = home_rows[rows_local, :rows_local] + home_rows[rows_local, rows_local : 2 * rows_local]

    bias_sums = column_sums(joined_grad)

    def spread_half(values, count):
        return jnp.where(
            jnp.arange(2)[:, None] == half, values.reshape(1, count), 0.0
        ).reshape(2 * count)

    vector_parts = [
        grad_first_gain,
        grad_first_shift,
        column_sums(attn_own),
        grad_second_gain,
        grad_second_shift,
        column_sums(branch_own),
        jnp.concatenate(
            [spread_half(bias_sums[:part], part), spread_half(bias_sums[2 * part :], part)]
        ),
        spread_half(column_sums(inner_grad), ff_part),
    ]
    vector_grads = jnp.concatenate([v.reshape(shards_all, -1) for v in vector_parts], axis=1)
    vector_grads = jnp.pad(
        vector_grads.reshape(size_blk * size_batch, size_vocab, -1),
        ((0, 0), (0, 4), (0, 3 * part - vector_grads.shape[1])),
    ).astype(jnp.bfloat16)
    grad_front = jnp.concatenate(
        [grad_attend.reshape(size_blk * size_batch, plane_rows, 3 * part), vector_grads], axis=1
    )
    front_sum, seen = halve_and_see(grad_front.reshape(grid + grad_front.shape[1:]), BATCH, 0)
    output_sum = halve(grad_output.reshape(grid + (plane_rows, part)), BLK, 0, input_other)
    output_sum = halve(output_sum, BATCH, 0, seen)
    front_sum, seen = halve_and_see(front_sum, BLK, 0)
    reduce_sum = halve(reduce_sum, BLK, 1, seen)[0, 0, 0]
    expand_sum = halve(expand_sum, BLK, 1, seen)[0, 0, 0]
    output_sum = halve(output_sum, BLK, 1, seen)[0, 0, 0]
    front_sum = halve(front_sum, BLK, 1)[0, 0, 0]

    units = (ff_part + part) // part
    share = reduce_rows // size_vocab
    back = exchange_models(
        [
            jnp.concatenate(
                [
                    expand_sum[t * shard_rows : (t + 1) * shard_rows, k * part : (k + 1) * part]
                    for k in range(units - 1)
                ]
                + [output_sum[t * shard_rows : (t + 1) * shard_rows]]
                + [reduce_sum[t * share : (t + 1) * share]],
                axis=0,
            ).astype(jnp.bfloat16)
            for t in range(size_vocab)
        ]
    )
    front = exchange_models(
        [
            jnp.concatenate(
                [
                    front_sum[t * shard_rows : (t + 1) * shard_rows],
                    jnp.pad(front_sum[plane_rows + t][None], ((0, 7), (0, 0))),
                ],
                axis=0,
            ).astype(jnp.bfloat16)
            for t in range(size_vocab)
        ]
    )
    results = []
    for m in (0, 1):
        sides = front[2 * m : 2 * m + 2]
        vector = sum(side[shard_rows].astype(jnp.float32) for side in sides)
        pieces = [vector[k * shard_rows : (k + 1) * shard_rows] for k in range(6)]
        attend = jnp.concatenate(
            [side[:shard_rows, k * part : (k + 1) * part] for k in range(3) for side in sides],
            axis=1,
        ).astype(jnp.float32)
        sides = back[2 * m : 2 * m + 2]
        output = jnp.concatenate(
            [side[(units - 1) * shard_rows : units * shard_rows] for side in sides], axis=1
        ).astype(jnp.float32)
        expand = jnp.concatenate(
            [
                side[k * shard_rows : (k + 1) * shard_rows]
                for side in sides
                for k in range(units - 1)
            ],
            axis=1,
        ).astype(jnp.float32)
        reduce = jnp.concatenate([side[units * shard_rows :] for side in sides], axis=1)
        reduce = reduce.astype(jnp.float32)
        results += [
            pieces[0],
            pieces[1],
            attend,
            vector[6 * shard_rows : 8 * shard_rows],
            output,
            pieces[2],
            pieces[3],
            pieces[4],
            expand,
            vector[8 * shard_rows : 12 * shard_rows],
            reduce,
            pieces[5],
        ]
    return tuple(results) + (input_grad[None], kl_out[None])


def solution(mesh):
    by_model = mesh.shape[VOCAB] == 4 and mesh.shape[BLK] == 4 and mesh.shape[BATCH] == 2
    return jax.shard_map(
        shards_by_model if by_model else shards,
        mesh=mesh,
        in_specs=(
            P((BATCH, VOCAB), BLK, None),
            P((BATCH, VOCAB)),
            P(EVERY),
            P(EVERY),
            P(EVERY, None),
            P(EVERY),
            P(EVERY, None),
            P(EVERY),
            P(EVERY),
            P(EVERY),
            P(EVERY, None),
            P(EVERY),
            P(EVERY, None),
            P(EVERY),
            P(EVERY),
            P(EVERY),
            P(EVERY, None),
            P(EVERY),
            P(EVERY, None),
            P(EVERY),
            P(EVERY),
            P(EVERY),
            P(EVERY, None),
            P(EVERY),
            P(EVERY, None),
            P(EVERY),
            P(),
            P(),
            P(VOCAB, None),
        ),
        out_specs=(
            P(EVERY),
            P(EVERY),
            P(EVERY, None),
            P(EVERY),
            P(EVERY, None),
            P(EVERY),
            P(EVERY),
            P(EVERY),
            P(EVERY, None),
            P(EVERY),
            P(EVERY, None),
            P(EVERY),
            P(EVERY),
            P(EVERY),
            P(EVERY, None),
            P(EVERY),
            P(EVERY, None),
            P(EVERY),
            P(EVERY),
            P(EVERY),
            P(EVERY, None),
            P(EVERY),
            P(EVERY, None),
            P(EVERY),
            P((BATCH, VOCAB), BLK, None),
            P((BATCH, VOCAB), BLK),
        ),
        check_vma=False,
    )
```
